256 devices in a mesh: dp: 32 (over z, x_lo, core), space: 8 (over y, x_hi).
Axes of the slice: x: 4 (x_hi: 2, x_lo: 2; x = x_hi * 2 + x_lo), y: 4, z: 8, core: 2. Of those that a mesh axis runs over, the one named last changes fastest.
Arguments:
- latents: bfloat16 [32, 8, 24, 8, 256], P('dp', None, 'space'), may hold values from -48 to 48
- cotangent: bfloat16 [32, 8, 24, 8, 256], P('dp', None, 'space'), may hold values from -17 to 17
- conv_weights: bfloat16 [2, 6912, 256], replicated, may hold values from -0.078125 to 0.078125
- gains: float32 [2, 256], replicated, may hold values from 0.25 to 1.75
- shifts: float32 [2, 256], replicated, may hold values from -3 to 3
- moment: float32 [2, 6912, 256], P(None, 'dp'), may hold values from -30 to 30
- second: float32 [2, 6912, 256], P(None, 'dp'), may hold values from 10 to 100
Outputs:
- decoded: bfloat16 [32, 8, 24, 8, 256], P('dp', None, 'space')
- grad_input: bfloat16 [32, 8, 24, 8, 256], P('dp', None, 'space')
- new_moment: float32 [2, 6912, 256], P(None, 'dp')
- new_second: float32 [2, 6912, 256], P(None, 'dp')
- direction: float32 [2, 6912, 256], P(None, 'dp')
- vector_grads: float32 [4, 256], replicated
The draws below stay inside these ranges and needn't reach their ends.
All inputs are finite; a program needn't handle non-finite values.
Results may differ from the reference program's by a relative error of at most 0.0045.
Values may be sent and summed in bfloat16 or wider, within the bound.
No kernel may reach another device: no remote copies, remote signals or barrier semaphores. Data moves between devices by JAX's collectives and lax.ppermute only.
A program may use at most 128 MiB of HBM per device.

```python
import math
import jax
import jax.numpy as jnp
from jax import lax

C = 256
GROUPS = 32
FRAMES = 8
W = 8
CLIPS = 32
H = 24


def draw_latents(key, part):
    key = jax.random.fold_in(key, 11)
    key_values, key_chans = jax.random.split(key, 2)
    shape = (CLIPS, FRAMES, H, W, C)
    rows = jnp.arange(H).astype(jnp.float32)
    row_scale = 1.0 + 2.0 * rows / max(H - 1, 1)
    chan_scale = jnp.exp(jax.random.uniform(key_chans, (C,), jnp.float32, 0.0, jnp.log(4.0)))
    values = jnp.clip(jax.random.normal(key_values, shape, jnp.float32), -4.0, 4.0)
    return (values * row_scale[None, None, :, None, None] * chan_scale).astype(jnp.bfloat16)


def draw_cotangent(key, part):
    key = jax.random.fold_in(key, 23)
    key_values, key_level, key_sign = jax.random.split(key, 3)
    shape = (CLIPS, FRAMES, H, W, C)
    rows = jnp.arange(H).astype(jnp.float32)
    row_scale = 1.0 + 2.0 * rows / max(H - 1, 1)
    signs = 2.0 * jax.random.randint(key_sign, (C,), 0, 2).astype(jnp.float32) - 1.0
    level = jax.random.uniform(key_level, (C,), jnp.float32, 0.5, 1.2)
    values = jnp.clip(jax.random.normal(key_values, shape, jnp.float32), -4.0, 4.0)
    values = values + signs * level
    return (values * row_scale[None, None, :, None, None]).astype(jnp.bfloat16)


def shard_levels(own_key, extent, shards, low, high):
    level = 1.0
    for axis_at, blocks in shards:
        heights = jax.random.uniform(jax.random.fold_in(jax.random.fold_in(own_key, 6), axis_at), (blocks,), jnp.float32, low / len(shards), high / len(shards))
        level = level * jnp.repeat(jnp.exp(heights), extent[axis_at] // blocks).reshape((-1,) + (1,) * (len(extent) - 1 - axis_at))
    return level


def scatter_about(rng, shape, deviation, reach, cuts=(), kind=jnp.bfloat16):
    drawn = deviation * jax.random.normal(rng, shape, jnp.float32)
    if cuts:
        drawn = drawn * shard_levels(rng, shape, cuts, -0.22, 0.18)
    return jnp.clip(drawn, -reach, reach).astype(kind)


def setup_inputs(seed: int = 0) -> dict:
    seeds = jax.random.split(jax.random.key(seed), 8)
    latents = draw_latents(jax.random.fold_in(seeds[7], 71), 0)
    cotangent = draw_cotangent(jax.random.fold_in(seeds[7], 71), 0)
    conv_weights = scatter_about(seeds[2], (2, 27 * C, C), (27 * C) ** -0.5, 0.078125)
    gains = jnp.clip(1.0 + 0.15 * jax.random.normal(seeds[3], (2, C), jnp.float32), 0.25, 1.75)
    shifts = scatter_about(seeds[4], (2, C), 0.5, 3.0, (), jnp.float32)
    moment = scatter_about(seeds[5], (2, 27 * C, C), 5.0, 30.0, ((1, 32),), jnp.float32)
    second = jnp.clip(jnp.exp(math.log(100.0) - 2.3025851 * jax.random.uniform(seeds[6], (2, 27 * C, C), jnp.float32) ** shard_levels(seeds[6], (2, 27 * C, C), ((1, 32),), -0.2, 0.2)), 10.0, 100.0)
    return dict(latents=latents, cotangent=cotangent, conv_weights=conv_weights, gains=gains, shifts=shifts, moment=moment, second=second)


bias_first = 1.0 - math.exp(100.0 * math.log(0.9))
bias_second = 1.0 - math.exp(100.0 * math.log(0.999))

def local_sums(values, groups):
    frames, rows, cols, chans = values.shape
    grouped = values.reshape(frames, rows, cols, groups, chans // groups)
    return (lax.optimization_barrier(jnp.sum(grouped, axis=(1, 2, 4))), lax.optimization_barrier(jnp.sum(grouped * grouped, axis=(1, 2, 4))))

def normalize(values, first, squares, gain, shift, count):
    frames, rows, cols, chans = values.shape
    groups = first.shape[1]
    mean = first / count
    spread = squares / count - mean * mean
    factor = lax.rsqrt(spread + 1e-05)
    grouped = values.reshape(frames, rows, cols, groups, chans // groups)
    normed = (grouped - mean[:, None, None, :, None]) * factor[:, None, None, :, None]
    return normed.reshape(values.shape) * gain + shift

def normalize_full(values, gain, shift):
    first, squares = local_sums(values, GROUPS)
    return normalize(values, first, squares, gain, shift, H * W * (C // GROUPS))

def silu_slope(values):
    sig = jax.nn.sigmoid(values)
    return sig * (1.0 + values * (1.0 - sig))

def frame_pad(rows_in):
    front = jnp.concatenate([rows_in[:1], rows_in[:1], rows_in], 0)
    return jnp.pad(front, ((0, 0), (0, 0), (1, 1), (0, 0)))

def patch_matrix(rows_in):
    frames = rows_in.shape[0]
    out_rows = rows_in.shape[1] - 2
    cols = rows_in.shape[2]
    padded = frame_pad(rows_in)
    views = []
    for step_t in range(3):
        for step_h in range(3):
            for step_w in range(3):
                views.append(padded[step_t:step_t + frames, step_h:step_h + out_rows, step_w:step_w + cols])
    return jnp.concatenate(views, -1).reshape(frames * out_rows * cols, -1)

def conv_out(rows_in, weight):
    frames, padded_rows, cols, chans = rows_in.shape
    result = jnp.dot(patch_matrix(rows_in), weight, preferred_element_type=jnp.float32)
    return result.reshape(frames, padded_rows - 2, cols, weight.shape[1])

def weight_grad(rows_in, grad):
    flat = grad.reshape(-1, grad.shape[-1])
    return lax.dot_general(patch_matrix(rows_in), flat, (((0,), (0,)), ((), ())), preferred_element_type=jnp.float32)

def fold_rows(grad, weight):
    frames, out_rows, cols, chans = grad.shape
    flat = grad.reshape(-1, chans)
    patches = lax.dot_general(flat, weight, (((1,), (1,)), ((), ())), preferred_element_type=jnp.float32)
    taps = patches.reshape(frames, out_rows, cols, 27, chans)
    padded = jnp.zeros((frames + 2, out_rows + 2, cols + 2, chans), jnp.float32)
    number = 0
    for step_t in range(3):
        for step_h in range(3):
            for step_w in range(3):
                padded = padded.at[step_t:step_t + frames, step_h:step_h + out_rows, step_w:step_w + cols].add(taps[:, :, :, number])
                number += 1
    first = padded[0] + padded[1] + padded[2]
    joined = jnp.concatenate([first[None], padded[3:]], 0)
    return joined[:, :, 1:-1]

def adam(grad, moment, second):
    new_m = 0.9 * moment + 0.1 * grad
    new_v = 0.999 * second + 0.001 * grad * grad
    return (new_m, new_v, new_m / bias_first / (jnp.sqrt(new_v / bias_second) + 1e-08))

def one_clip(carry, inputs):
    latent, upstream = inputs
    conv_weights, gains, shifts = (carry[2], carry[3], carry[4])
    xfull = latent.astype(jnp.float32)
    pad_spec = ((0, 0), (1, 1), (0, 0), (0, 0))
    u_one = normalize_full(xfull, gains[0], shifts[0])
    a_one = jnp.pad(jax.nn.silu(u_one).astype(jnp.bfloat16), pad_spec)
    h_one = conv_out(a_one, conv_weights[0]).astype(jnp.bfloat16)
    h_full = h_one.astype(jnp.float32)
    u_two = normalize_full(h_full, gains[1], shifts[1])
    a_two = jnp.pad(jax.nn.silu(u_two).astype(jnp.bfloat16), pad_spec)
    decoded = (xfull + conv_out(a_two, conv_weights[1])).astype(jnp.bfloat16)
    grad_two = weight_grad(a_two, upstream)
    d_u2 = fold_rows(upstream, conv_weights[1])[:, 1:-1] * silu_slope(u_two)
    _, pull_two = jax.vjp(normalize_full, h_full, gains[1], shifts[1])
    d_h1, gain_two, shift_two = pull_two(d_u2)
    d_h1 = d_h1.astype(jnp.bfloat16)
    grad_one = weight_grad(a_one, d_h1)
    d_u1 = fold_rows(d_h1, conv_weights[0])[:, 1:-1] * silu_slope(u_one)
    _, pull_one = jax.vjp(normalize_full, xfull, gains[0], shifts[0])
    d_x, gain_one, shift_one = pull_one(d_u1)
    grad_input = (upstream.astype(jnp.float32) + d_x).astype(jnp.bfloat16)
    kernels = carry[0] + jnp.stack([grad_one, grad_two])
    vectors = carry[1] + jnp.stack([gain_one, shift_one, gain_two, shift_two])
    return ((kernels, vectors, conv_weights, gains, shifts), (decoded, grad_input))

def reference(latents, cotangent, conv_weights, gains, shifts, moment, second):
    start = (jnp.zeros((2, 27 * C, C), jnp.float32), jnp.zeros((4, C), jnp.float32), conv_weights, gains, shifts)
    final, outputs = lax.scan(one_clip, start, (latents, cotangent))
    kernels = final[0] / CLIPS
    vector_grads = final[1] / CLIPS
    first_layer = adam(kernels[0], moment[0], second[0])
    second_layer = adam(kernels[1], moment[1], second[1])
    new_moment = jnp.stack([first_layer[0], second_layer[0]])
    new_second = jnp.stack([first_layer[1], second_layer[1]])
    direction = jnp.stack([first_layer[2], second_layer[2]])
    return (outputs[0], outputs[1], new_moment, new_second, direction, vector_grads)
```

```python
import math

import jax
import jax.numpy as jnp
from jax import lax
from jax.sharding import PartitionSpec as P

GROUPS = 32


bias_first = 1.0 - math.exp(100.0 * math.log(0.9))
bias_second = 1.0 - math.exp(100.0 * math.log(0.999))


def spread(value, axis):
    return lax.all_to_all(jnp.broadcast_to(value[None], (lax.axis_size(axis),) + value.shape), axis, 0, 0)


def gather_rows(value):
    every = spread(value, "space")
    count, frames, rows, cols, chans = every.shape
    return every.transpose(1, 0, 2, 3, 4).reshape(frames, count * rows, cols, chans)


def group_all(sums):
    frames, chans = sums.shape
    size = chans // GROUPS
    total = jnp.sum(sums.reshape(frames, GROUPS, size), -1)
    return jnp.repeat(total, size, axis=-1)


def norm_parts(values):
    count = values.shape[1] * values.shape[2] * (values.shape[3] // GROUPS)
    mean = group_all(jnp.sum(values, (1, 2))) / count
    var = group_all(jnp.sum(values * values, (1, 2))) / count - mean * mean
    factor = lax.rsqrt(var + 1e-05)
    return mean[:, None, None], factor[:, None, None]


def norm_back(normed, factor, gain, d_out):
    count = normed.shape[1] * normed.shape[2] * (normed.shape[3] // GROUPS)
    d_shift = jnp.sum(d_out, (1, 2))
    d_gain = jnp.sum(d_out * normed, (1, 2))
    one = group_all(d_shift * gain)[:, None, None] / count
    two = group_all(d_gain * gain)[:, None, None] / count
    d_in = factor * (d_out * gain - one - normed * two)
    return d_in, jnp.sum(d_gain, 0), jnp.sum(d_shift, 0)


def silu_slope(values):
    sig = jax.nn.sigmoid(values)
    return sig * (1.0 + values * (1.0 - sig))


def front(values):
    return jnp.concatenate([values[:1], values[:1], values], 0)


def conv(values, weight, row_pad):
    chans = values.shape[-1]
    return lax.conv_general_dilated(
        values[None],
        weight.reshape(3, 3, 3, chans, -1),
        (1, 1, 1),
        ((0, 0), (row_pad, row_pad), (1, 1)),
        dimension_numbers=("NDHWC", "DHWIO", "NDHWC"),
        preferred_element_type=jnp.float32,
    )[0]


def conv_back(grads, weight):
    chans = grads.shape[-1]
    return lax.conv_general_dilated(
        grads[None],
        weight.reshape(3, 3, 3, -1, chans)[::-1, ::-1, ::-1],
        (1, 1, 1),
        ((0, 0), (1, 1), (1, 1)),
        dimension_numbers=("NDHWC", "DHWOI", "NDHWC"),
        preferred_element_type=jnp.float32,
    )[0]


def kernel_grad(values, grads):
    frames, rows, cols, chans = values.shape
    outs = grads.shape[-1]
    padded = jnp.pad(grads, ((0, 0), (1, 1), (1, 1), (0, 0)))
    views = [
        padded[:, 2 - h : 2 - h + rows, 2 - w : 2 - w + cols] for h in range(3) for w in range(3)
    ]
    nine = jnp.concatenate(views, -1).reshape(frames * rows * cols, 9 * outs)
    long = front(values).reshape((frames + 2) * rows * cols, chans)
    size = rows * cols
    parts = [
        lax.dot_general(
            nine,
            long[t * size : (t + frames) * size],
            (((0,), (0,)), ((), ())),
            preferred_element_type=jnp.float32,
        )
        for t in range(3)
    ]
    return jnp.stack(parts).reshape(27, outs, chans)


def pieces(grad, clips):
    taps, outs, chans = grad.shape
    flat = grad.astype(jnp.bfloat16).transpose(1, 0, 2).reshape(outs, clips, taps * chans // clips)
    flat = flat.transpose(1, 0, 2)
    return jnp.pad(flat, ((0, 0), (0, 0), (0, chans - flat.shape[2])))


def adam(grad, moment, second):
    new_m = 0.9 * moment + 0.1 * grad
    new_v = 0.999 * second + 0.001 * grad * grad
    return (new_m, new_v, new_m / bias_first / (jnp.sqrt(new_v / bias_second) + 1e-08))


def per_device(latents, cotangent, conv_weights, gains, shifts, moment, second):
    frames, rows, cols, chans = latents.shape[1:]
    clips, parts = lax.axis_size("dp"), lax.axis_size("space")
    me = lax.axis_index("space")
    width = chans // parts
    f32, bf16 = jnp.float32, jnp.bfloat16
    lat = gather_rows(latents[0])
    cot = gather_rows(cotangent[0])
    xfull = lat.astype(f32)
    mean_one, factor_one = norm_parts(xfull)
    normed_one = (xfull - mean_one) * factor_one
    u_one = normed_one * gains[0] + shifts[0]
    a_one = jax.nn.silu(u_one).astype(bf16)
    h_one = conv(front(a_one), conv_weights[0], 1).astype(bf16).astype(f32)
    mean_two, factor_two = norm_parts(h_one)
    normed_two = (h_one - mean_two) * factor_two
    u_two = normed_two * gains[1] + shifts[1]
    a_two = jax.nn.silu(u_two).astype(bf16)

    later = kernel_grad(a_two, lax.dynamic_slice_in_dim(cot, me * width, width, 3))
    later = lax.all_to_all(pieces(later, clips), "dp", 0, 0)

    full = conv_back(jnp.pad(cot, ((2, 2), (0, 0), (0, 0), (0, 0))), conv_weights[1])
    d_a2 = jnp.concatenate([(full[0] + full[1] + full[2])[None], full[3:]], 0)
    d_h1, gain_two, shift_two = norm_back(
        normed_two, factor_two, gains[1], d_a2 * silu_slope(u_two)
    )
    d_h1 = d_h1.astype(bf16)

    def frame(value):
        return lax.dynamic_slice_in_dim(value, me, 1, 0)

    near = lax.dynamic_slice_in_dim(jnp.pad(d_h1, ((0, 2), (0, 0), (0, 0), (0, 0))), me, 3, 0)
    near = near.astype(f32)
    first = (me == 0).astype(f32)
    near = jnp.stack(
        [near[0], near[1] + first * near[0], near[2] + first * (near[0] + near[1])]
    ).astype(bf16)
    d_a1 = conv_back(near, conv_weights[0])
    d_x, gain_one, shift_one = norm_back(
        frame(normed_one), frame(factor_one), gains[0], d_a1 * silu_slope(frame(u_one))
    )
    grad_input = (frame(cot).astype(f32) + d_x).astype(bf16)
    grad_input = grad_input[0].reshape(parts, rows, cols, chans)
    grad_input = lax.all_to_all(grad_input, "space", 0, 0)

    earlier = kernel_grad(a_one, lax.dynamic_slice_in_dim(d_h1, me * width, width, 3))
    share = 1.0 / parts
    vectors = jnp.stack([gain_one, shift_one, gain_two * share, shift_two * share])
    high = vectors.astype(bf16)
    low = (vectors - high.astype(f32)).astype(bf16)
    extra = jnp.concatenate([high, low, jnp.zeros((8, chans), bf16)], 0)
    extra = jnp.broadcast_to(extra[None], (clips,) + extra.shape)
    earlier = lax.all_to_all(jnp.concatenate([pieces(earlier, clips), extra], 1), "dp", 0, 0)

    tall = lax.dynamic_slice_in_dim(
        jnp.pad(front(a_two), ((0, 0), (1, 1), (0, 0), (0, 0))), me * rows, rows + 2, 1
    )
    decoded = (latents[0].astype(f32) + conv(tall, conv_weights[1], 0)).astype(bf16)

    total = jnp.sum(jnp.concatenate([later, earlier], 1).astype(f32), 0) / clips
    every = spread(total, "space")
    owned = moment.shape[1]

    def layer(start):
        return every[:, start : start + width, :owned].reshape(chans, owned).T

    vector = jnp.sum(every[:, 2 * width :], 0)
    vector = vector[:4] + vector[4:8]
    grad = jnp.stack([layer(width), layer(0)])
    new_moment, new_second, direction = adam(grad, moment, second)
    return (decoded[None], grad_input[None], new_moment, new_second, direction, vector)


def solution(mesh):
    placed = (
        P("dp", None, "space", None, None),
        P("dp", None, "space", None, None),
        P(),
        P(),
        P(),
        P(None, "dp", None),
        P(None, "dp", None),
    )
    return jax.shard_map(
        per_device,
        mesh=mesh,
        in_specs=placed,
        out_specs=(
            P("dp", None, "space", None, None),
            P("dp", None, "space", None, None),
            P(None, "dp", None),
            P(None, "dp", None),
            P(None, "dp", None),
            P(),
        ),
        check_vma=False,
    )
```

```python
import math

import jax
import jax.numpy as jnp
from jax import lax
from jax.experimental import pallas as pl
from jax.experimental.pallas import tpu as pltpu
from jax.sharding import PartitionSpec as P

GROUPS = 32
STEP = 4


bias_first = 1.0 - math.exp(100.0 * math.log(0.9))
bias_second = 1.0 - math.exp(100.0 * math.log(0.999))


def rolled(value, amount, axis):
    return pltpu.roll(value, amount % value.shape[axis], axis)


def all_cols(value):
    total = jnp.sum(value, 0)
    for step in (4, 2, 1):
        total = total + rolled(total, step, 0)
    return total


def group_all(sums):
    size = sums.shape[1] // GROUPS
    lane = lax.broadcasted_iota(jnp.int32, sums.shape, 1)
    step = 1
    while step < size:
        partner = jnp.where((lane & step) == 0, rolled(sums, -step, 1), rolled(sums, step, 1))
        sums = sums + partner
        step *= 2
    return sums


def norm_parts(values):
    count = values.shape[0] * values.shape[1] * (values.shape[2] // GROUPS)
    mean = group_all(all_cols(values)) / count
    var = group_all(all_cols(values * values)) / count - mean * mean
    return mean, lax.rsqrt(var + 1e-05)


def col_shifted(value, step):
    if step == 0:
        return value
    col = lax.broadcasted_iota(jnp.int32, value.shape, 1)
    edge = value.shape[1] - 1 if step > 0 else 0
    return jnp.where(col == edge, 0.0, rolled(value, -step, 1))


def row_shifted(value, step):
    if step == 0:
        return value
    zero = jnp.zeros_like(value[:1])
    if step > 0:
        return jnp.concatenate([value[1:], zero], 0)
    return jnp.concatenate([zero, value[:-1]], 0)


def store_nine(target, frame, value, sign):
    rows, cols, chans = value.shape
    size = rows * cols
    for w in range(3):
        moved = col_shifted(value, sign * (w - 1))
        for h in range(3):
            view = row_shifted(moved, sign * (h - 1)).reshape(size, chans)
            number = 3 * h + w
            target[pl.ds(pl.multiple_of(frame * size, 16), size), number * chans : (number + 1) * chans] = view.astype(jnp.bfloat16)


def load_frame(raw, frame):
    blocks, _, flat, chans = raw.shape
    parts = [raw[b, frame].astype(jnp.float32).reshape(flat // 8, 8, chans) for b in range(blocks)]
    return jnp.concatenate(parts, 0)


def frame_of(flat, frame, size):
    part = flat[pl.ds(pl.multiple_of(frame * size, 16), size), :]
    return part.astype(jnp.float32).reshape(size // 8, 8, part.shape[-1])


def put_frame(flat, frame, value):
    size = value.shape[0] * value.shape[1]
    flat[pl.ds(pl.multiple_of(frame * size, 16), size), :] = value.reshape(size, -1).astype(flat.dtype)


def ahead_kernel(raw, weight, gains, shifts, a_one, h_one, a_two, nine):
    frames, chans = raw.shape[1], raw.shape[3]
    size = raw.shape[0] * raw.shape[2]
    depth = 9 * chans

    @pl.loop(0, frames)
    def _(t):
        value = load_frame(raw, t)
        mean, factor = norm_parts(value)
        u = (value - mean) * factor * gains[0:1, :] + shifts[0:1, :]
        act = (u * jax.nn.sigmoid(u)).astype(jnp.bfloat16).astype(jnp.float32)
        put_frame(a_one, t, act)
        store_nine(nine, t + 2, act, 1)

    nine[0:size, :] = nine[2 * size : 3 * size, :]
    nine[size : 2 * size, :] = nine[2 * size : 3 * size, :]

    @pl.loop(0, frames // STEP)
    def _(b):
        total = None
        for t in range(3):
            left = nine[pl.ds(pl.multiple_of((b * STEP + t) * size, 16), STEP * size), :]
            part = jnp.dot(left, weight[t * depth : (t + 1) * depth, :], preferred_element_type=jnp.float32)
            total = part if total is None else total + part
        h_one[pl.ds(pl.multiple_of(b * STEP * size, 16), STEP * size), :] = total.astype(jnp.bfloat16)

    @pl.loop(0, frames)
    def _(t):
        value = frame_of(h_one, t, size)
        mean, factor = norm_parts(value)
        u = (value - mean) * factor * gains[1:2, :] + shifts[1:2, :]
        put_frame(a_two, t, u * jax.nn.sigmoid(u))


def back_kernel(raw, weight, h_one, gains, shifts, d_h1, vectors, nine, d_act):
    frames, chans = raw.shape[1], raw.shape[3]
    size = raw.shape[0] * raw.shape[2]
    depth = 9 * chans

    @pl.loop(0, frames)
    def _(t):
        store_nine(nine, t, load_frame(raw, t), -1)

    nine[frames * size :, :] = jnp.zeros((2 * size, depth), jnp.bfloat16)

    @pl.loop(0, frames // STEP)
    def _(b):
        total = None
        for t in range(3):
            left = nine[pl.ds(pl.multiple_of((b * STEP + 2 - t) * size, 16), STEP * size), :]
            part = jnp.dot(left, weight[t * depth : (t + 1) * depth, :], preferred_element_type=jnp.float32)
            total = part if total is None else total + part
        d_act[pl.ds(pl.multiple_of(b * STEP * size, 16), STEP * size), :] = total

    pair = jnp.dot(nine[0:size, :], weight[depth : 2 * depth, :], preferred_element_type=jnp.float32)
    both = jnp.dot(nine[0 : 2 * size, :], weight[0:depth, :], preferred_element_type=jnp.float32)
    d_act[0:size, :] = d_act[0:size, :] + (pair + (both[:size] + both[size:]))

    vectors[...] = jnp.zeros_like(vectors)
    count = size * (chans // GROUPS)

    @pl.loop(0, frames)
    def _(t):
        value = frame_of(h_one, t, size)
        mean, factor = norm_parts(value)
        normed = (value - mean) * factor
        u = normed * gains[1:2, :] + shifts[1:2, :]
        sig = jax.nn.sigmoid(u)
        d_out = frame_of(d_act, t, size) * (sig * (1.0 + u * (1.0 - sig)))
        d_shift = all_cols(d_out)
        d_gain = all_cols(d_out * normed)
        vectors[0] += d_gain
        vectors[1] += d_shift
        one = group_all(d_shift * gains[1:2, :]) / count
        two = group_all(d_gain * gains[1:2, :]) / count
        put_frame(d_h1, t, factor * (d_out * gains[1:2, :] - one - normed * two))


def grad_kernel(place, values, grads, extra, out, long, block, total):
    frames_size, chans = values.shape
    owners, tall, _ = out.shape
    size = long.shape[0] - frames_size
    size, outs = size // 2, total.shape[0] // 27
    frames = frames_size // size
    long[0:size, :] = values[0:size, :]
    long[size : 2 * size, :] = values[0:size, :]
    long[2 * size :, :] = values[...]
    lanes = block.shape[1]
    chan = lax.broadcasted_iota(jnp.int32, (chans, lanes), 0)
    lane = lax.broadcasted_iota(jnp.int32, (chans, lanes), 1)
    pick = (chan == place[0] * outs + lane % outs).astype(jnp.bfloat16)

    @pl.loop(0, frames)
    def _(t):
        rows = grads[pl.ds(pl.multiple_of(t * size, 16), size), :]
        spread_out = jnp.dot(rows, pick, preferred_element_type=jnp.float32).reshape(size // 8, 8, lanes)
        for piece in range(lanes // 128):
            value = spread_out[:, :, piece * 128 : (piece + 1) * 128]
            lane = lax.broadcasted_iota(jnp.int32, value.shape, 2)
            kept = jnp.zeros_like(value)
            for place_in in range(128 // outs):
                number = piece * (128 // outs) + place_in
                if number < 9:
                    h, w = divmod(number, 3)
                    moved = row_shifted(col_shifted(value, 1 - w), 1 - h)
                    kept = jnp.where(lane // outs == place_in, moved, kept)
            block[pl.ds(pl.multiple_of(t * size, 16), size), piece * 128 : (piece + 1) * 128] = kept.reshape(size, 128).astype(jnp.bfloat16)

    side = block[...].T
    for t in range(3):
        part = jnp.dot(side, long[t * size : (t + frames) * size, :], preferred_element_type=jnp.float32)
        total[t * 9 * outs : (t + 1) * 9 * outs, :] = part[: 9 * outs]

    owned = 27 * chans // owners
    for d in range(owners):
        tap, start = divmod(d * owned, chans)
        one = total[tap * outs : (tap + 1) * outs, :]
        if start + owned > chans:
            one = jnp.concatenate([one, total[(tap + 1) * outs : (tap + 2) * outs, :]], 1)
        out[d, 0:outs, :] = rolled(one, -start, 1)[:, :chans].astype(jnp.bfloat16)
        if tall > outs:
            out[d, outs:, :] = extra[...]


def adam_kernel(every, moment, second, new_moment, new_second, direction, vector):
    parts, tall, chans = every.shape
    owned = moment.shape[1]
    width = chans // parts
    for layer in range(2):
        start = width * (1 - layer)
        grad = every[:, start : start + width, :].reshape(chans, chans).T[:owned, :]
        new_m = 0.9 * moment[layer] + 0.1 * grad
        new_v = 0.999 * second[layer] + 0.001 * grad * grad
        new_moment[layer] = new_m
        new_second[layer] = new_v
        direction[layer] = new_m / bias_first / (jnp.sqrt(new_v / bias_second) + 1e-08)
    sums = every[0, 2 * width :, :]
    for p in range(1, parts):
        sums = sums + every[p, 2 * width :, :]
    vector[...] = sums[0:4] + sums[4:8]


def called(kernel, outs, scratch, args, scalars=0, flops=0, limit=56):
    whole = pl.BlockSpec(memory_space=pltpu.VMEM)
    small = pl.BlockSpec(memory_space=pltpu.SMEM)
    moved = sum(math.prod(a.shape) * a.dtype.itemsize for a in (*args, *outs))
    return pl.pallas_call(
        kernel,
        out_shape=outs,
        in_specs=[small] * scalars + [whole] * (len(args) - scalars),
        out_specs=[whole] * len(outs),
        scratch_shapes=scratch,
        compiler_params=pltpu.CompilerParams(vmem_limit_bytes=limit * 2**20),
        cost_estimate=pl.CostEstimate(flops=flops, bytes_accessed=moved, transcendentals=0),
    )(*args)


def ahead(raw, weight, gains, shifts):
    blocks, frames, flat, chans = raw.shape
    places = blocks * frames * flat
    shape = jax.ShapeDtypeStruct((places, chans), jnp.bfloat16)
    scratch = [pltpu.VMEM((places + 2 * blocks * flat, 9 * chans), jnp.bfloat16)]
    return called(ahead_kernel, [shape] * 3, scratch, (raw, weight, gains, shifts), 0, 2 * places * weight.size)


def back(raw, weight, h_one, gains, shifts):
    blocks, frames, flat, chans = raw.shape
    places = blocks * frames * flat
    outs = [jax.ShapeDtypeStruct((places, chans), jnp.bfloat16), jax.ShapeDtypeStruct((2, 8, chans), jnp.float32)]
    scratch = [
        pltpu.VMEM((places + 2 * blocks * flat, 9 * chans), jnp.bfloat16),
        pltpu.VMEM((places, chans), jnp.float32),
    ]
    return called(back_kernel, outs, scratch, (raw, weight, h_one, gains, shifts), 0, 2 * places * weight.size)


def kernel_grad(place, values, grads, extra, width, size, clips):
    places, chans = values.shape
    outs = [jax.ShapeDtypeStruct((clips, width + extra.shape[0], chans), jnp.bfloat16)]
    if extra.shape[0] == 0:
        body = lambda p, v, g, *rest: grad_kernel(p, v, g, None, *rest)
        args = (place, values, grads)
    else:
        body, args = grad_kernel, (place, values, grads, extra)
    scratch = [
        pltpu.VMEM((places + 2 * size, chans), jnp.bfloat16),
        pltpu.VMEM((places, -(-9 * width // 128) * 128), jnp.bfloat16),
        pltpu.VMEM((27 * width, chans), jnp.float32),
    ]
    return called(body, outs, scratch, args, 1, 2 * places * 27 * width * chans)[0]


def spread(value, axis):
    return lax.all_to_all(jnp.broadcast_to(value[None], (lax.axis_size(axis),) + value.shape), axis, 0, 0)


def silu_slope(values):
    sig = jax.nn.sigmoid(values)
    return sig * (1.0 + values * (1.0 - sig))


def group_sum(sums):
    frames, chans = sums.shape
    size = chans // GROUPS
    return jnp.repeat(jnp.sum(sums.reshape(frames, GROUPS, size), -1), size, axis=-1)


def frame_stats(values):
    count = values.shape[1] * values.shape[2] * (values.shape[3] // GROUPS)
    mean = group_sum(jnp.sum(values, (1, 2))) / count
    var = group_sum(jnp.sum(values * values, (1, 2))) / count - mean * mean
    return mean[:, None, None], lax.rsqrt(var + 1e-05)[:, None, None]


def norm_back(normed, factor, gain, d_out):
    count = normed.shape[1] * normed.shape[2] * (normed.shape[3] // GROUPS)
    d_shift = jnp.sum(d_out, (1, 2))
    d_gain = jnp.sum(d_out * normed, (1, 2))
    one = group_sum(d_shift * gain)[:, None, None] / count
    two = group_sum(d_gain * gain)[:, None, None] / count
    d_in = factor * (d_out * gain - one - normed * two)
    return d_in, jnp.sum(d_gain, 0), jnp.sum(d_shift, 0)


def conv(values, weight, row_pad):
    chans = values.shape[-1]
    return lax.conv_general_dilated(
        values[None],
        weight.reshape(3, 3, 3, chans, -1),
        (1, 1, 1),
        ((0, 0), (row_pad, row_pad), (1, 1)),
        dimension_numbers=("NDHWC", "DHWIO", "NDHWC"),
        preferred_element_type=jnp.float32,
    )[0]


def conv_back(grads, weight):
    chans = grads.shape[-1]
    return lax.conv_general_dilated(
        grads[None],
        weight.reshape(3, 3, 3, -1, chans)[::-1, ::-1, ::-1],
        (1, 1, 1),
        ((0, 0), (1, 1), (1, 1)),
        dimension_numbers=("NDHWC", "DHWOI", "NDHWC"),
        preferred_element_type=jnp.float32,
    )[0]


def per_device(latents, cotangent, conv_weights, gains, shifts, moment, second):
    frames, rows, cols, chans = latents.shape[1:]
    clips, parts = lax.axis_size("dp"), lax.axis_size("space")
    me = lax.axis_index("space")
    place = me.astype(jnp.int32).reshape(1)
    width, size = chans // parts, parts * rows * cols
    f32, bf16 = jnp.float32, jnp.bfloat16
    raw_lat = spread(latents[0].reshape(frames, rows * cols, chans), "space")
    raw_cot = spread(cotangent[0].reshape(frames, rows * cols, chans), "space")
    turned = conv_weights[1].reshape(27, chans, chans).transpose(0, 2, 1).reshape(27 * chans, chans)

    a_one, h_one, a_two = ahead(raw_lat, conv_weights[0], gains, shifts)
    cot = raw_cot.transpose(1, 0, 2, 3).reshape(frames * size, chans)
    none = jnp.zeros((0, chans), bf16)
    later = kernel_grad(place, a_two, cot, none, width, size, clips)
    later = lax.all_to_all(later, "dp", 0, 0)

    d_h1, sums_two = back(raw_cot, turned, h_one, gains, shifts)

    def frame(raw):
        value = lax.dynamic_slice_in_dim(raw, me, 1, 1)
        return value.reshape(1, parts * rows, cols, chans).astype(f32)

    xown = frame(raw_lat)
    mean_one, factor_one = frame_stats(xown)
    normed_one = (xown - mean_one) * factor_one
    u_one = normed_one * gains[0] + shifts[0]
    near = jnp.pad(d_h1.reshape(frames, size // cols, cols, chans), ((0, 2), (0, 0), (0, 0), (0, 0)))
    near = lax.dynamic_slice_in_dim(near, me, 3, 0).astype(f32)
    first = (me == 0).astype(f32)
    near = jnp.stack(
        [near[0], near[1] + first * near[0], near[2] + first * (near[0] + near[1])]
    ).astype(bf16)
    d_a1 = conv_back(near, conv_weights[0])
    d_x, gain_one, shift_one = norm_back(normed_one, factor_one, gains[0], d_a1 * silu_slope(u_one))
    grad_input = (frame(raw_cot) + d_x).astype(bf16)
    grad_input = grad_input[0].reshape(parts, rows, cols, chans)
    grad_input = lax.all_to_all(grad_input, "space", 0, 0)

    share = 1.0 / parts
    vectors = jnp.concatenate([gain_one[None], shift_one[None], sums_two[:, 0] * share])
    high = vectors.astype(bf16)
    low = (vectors - high.astype(f32)).astype(bf16)
    extra = jnp.concatenate([high, low, jnp.zeros((8, chans), bf16)], 0)
    earlier = kernel_grad(place, a_one, d_h1, extra, width, size, clips)
    earlier = lax.all_to_all(earlier, "dp", 0, 0)

    tall = a_two.reshape(frames, size // cols, cols, chans)
    tall = jnp.pad(jnp.concatenate([tall[:1], tall[:1], tall], 0), ((0, 0), (1, 1), (0, 0), (0, 0)))
    tall = lax.dynamic_slice_in_dim(tall, me * rows, rows + 2, 1)
    decoded = (latents[0].astype(f32) + conv(tall, conv_weights[1], 0)).astype(bf16)

    total = jnp.sum(jnp.concatenate([later, earlier], 1).astype(f32), 0) / clips
    every = spread(total, "space")
    shape = jax.ShapeDtypeStruct(moment.shape, f32)
    outs = [shape, shape, shape, jax.ShapeDtypeStruct((4, chans), f32)]
    new_moment, new_second, direction, vector = called(adam_kernel, outs, [], (every, moment, second))
    return (decoded[None], grad_input[None], new_moment, new_second, direction, vector)


def solution(mesh):
    placed = (
        P("dp", None, "space", None, None),
        P("dp", None, "space", None, None),
        P(),
        P(),
        P(),
        P(None, "dp", None),
        P(None, "dp", None),
    )
    return jax.shard_map(
        per_device,
        mesh=mesh,
        in_specs=placed,
        out_specs=(
            P("dp", None, "space", None, None),
            P("dp", None, "space", None, None),
            P(None, "dp", None),
            P(None, "dp", None),
            P(None, "dp", None),
            P(),
        ),
        check_vma=False,
    )
```

```python
import functools
import math

import jax
import jax.numpy as jnp
from jax import lax
from jax.experimental import pallas as pl
from jax.experimental.pallas import tpu as pltpu
from jax.sharding import PartitionSpec as P

GROUPS = 32
STEP = 4


bias_first = 1.0 - math.exp(100.0 * math.log(0.9))
bias_second = 1.0 - math.exp(100.0 * math.log(0.999))


def rolled(value, amount, axis):
    return pltpu.roll(value, amount % value.shape[axis], axis)


def all_cols(value):
    total = jnp.sum(value, 0)
    for step in (4, 2, 1):
        total = total + rolled(total, step, 0)
    return total


def group_all(sums):
    size = sums.shape[1] // GROUPS
    lane = lax.broadcasted_iota(jnp.int32, sums.shape, 1)
    step = 1
    while step < size:
        partner = jnp.where((lane & step) == 0, rolled(sums, -step, 1), rolled(sums, step, 1))
        sums = sums + partner
        step *= 2
    return sums


def norm_parts(values):
    count = values.shape[0] * values.shape[1] * (values.shape[2] // GROUPS)
    mean = group_all(all_cols(values)) / count
    var = group_all(all_cols(values * values)) / count - mean * mean
    return mean, lax.rsqrt(var + 1e-05)


def col_shifted(value, step):
    if step == 0:
        return value
    col = lax.broadcasted_iota(jnp.int32, value.shape, 1)
    edge = value.shape[1] - 1 if step > 0 else 0
    return jnp.where(col == edge, 0.0, rolled(value, -step, 1))


def row_shifted(value, step):
    if step == 0:
        return value
    zero = jnp.zeros_like(value[:1])
    if step > 0:
        return jnp.concatenate([value[1:], zero], 0)
    return jnp.concatenate([zero, value[:-1]], 0)


def store_nine(target, frame, value, sign):
    rows, cols, chans = value.shape
    size = rows * cols
    for w in range(3):
        moved = col_shifted(value, sign * (w - 1))
        for h in range(3):
            view = row_shifted(moved, sign * (h - 1)).reshape(size, chans)
            number = 3 * h + w
            target[pl.ds(pl.multiple_of(frame * size, 16), size), number * chans : (number + 1) * chans] = view.astype(jnp.bfloat16)


def load_frame(raw, frame):
    blocks, _, flat, chans = raw.shape
    parts = [raw[b, frame].astype(jnp.float32).reshape(flat // 8, 8, chans) for b in range(blocks)]
    return jnp.concatenate(parts, 0)


def frame_of(flat, frame, size):
    part = flat[pl.ds(pl.multiple_of(frame * size, 16), size), :]
    return part.astype(jnp.float32).reshape(size // 8, 8, part.shape[-1])


def put_frame(flat, frame, value):
    size = value.shape[0] * value.shape[1]
    flat[pl.ds(pl.multiple_of(frame * size, 16), size), :] = value.reshape(size, -1).astype(flat.dtype)


def ahead_kernel(raw, weight, gains, shifts, a_one, h_one, a_two, nine):
    frames, chans = raw.shape[1], raw.shape[3]
    size = raw.shape[0] * raw.shape[2]
    depth = 9 * chans

    @pl.loop(0, frames)
    def _(t):
        value = load_frame(raw, t)
        mean, factor = norm_parts(value)
        u = (value - mean) * factor * gains[0:1, :] + shifts[0:1, :]
        act = (u * jax.nn.sigmoid(u)).astype(jnp.bfloat16).astype(jnp.float32)
        put_frame(a_one, t, act)
        store_nine(nine, t + 2, act, 1)

    nine[0:size, :] = nine[2 * size : 3 * size, :]
    nine[size : 2 * size, :] = nine[2 * size : 3 * size, :]

    @pl.loop(0, frames // STEP)
    def _(b):
        total = None
        for t in range(3):
            left = nine[pl.ds(pl.multiple_of((b * STEP + t) * size, 16), STEP * size), :]
            part = jnp.dot(left, weight[t * depth : (t + 1) * depth, :], preferred_element_type=jnp.float32)
            total = part if total is None else total + part
        h_one[pl.ds(pl.multiple_of(b * STEP * size, 16), STEP * size), :] = total.astype(jnp.bfloat16)

    @pl.loop(0, frames)
    def _(t):
        value = frame_of(h_one, t, size)
        mean, factor = norm_parts(value)
        u = (value - mean) * factor * gains[1:2, :] + shifts[1:2, :]
        put_frame(a_two, t, u * jax.nn.sigmoid(u))


def back_kernel(raw, weight, h_one, gains, shifts, d_h1, vectors, nine, d_act):
    frames, chans = raw.shape[1], raw.shape[3]
    size = raw.shape[0] * raw.shape[2]
    depth = 9 * chans

    @pl.loop(0, frames)
    def _(t):
        store_nine(nine, t, load_frame(raw, t), -1)

    nine[frames * size :, :] = jnp.zeros((2 * size, depth), jnp.bfloat16)

    @pl.loop(0, frames // STEP)
    def _(b):
        total = None
        for t in range(3):
            left = nine[pl.ds(pl.multiple_of((b * STEP + 2 - t) * size, 16), STEP * size), :]
            part = jnp.dot(left, weight[t * depth : (t + 1) * depth, :], preferred_element_type=jnp.float32)
            total = part if total is None else total + part
        d_act[pl.ds(pl.multiple_of(b * STEP * size, 16), STEP * size), :] = total

    pair = jnp.dot(nine[0:size, :], weight[depth : 2 * depth, :], preferred_element_type=jnp.float32)
    both = jnp.dot(nine[0 : 2 * size, :], weight[0:depth, :], preferred_element_type=jnp.float32)
    d_act[0:size, :] = d_act[0:size, :] + (pair + (both[:size] + both[size:]))

    vectors[...] = jnp.zeros_like(vectors)
    count = size * (chans // GROUPS)

    @pl.loop(0, frames)
    def _(t):
        value = frame_of(h_one, t, size)
        mean, factor = norm_parts(value)
        normed = (value - mean) * factor
        u = normed * gains[1:2, :] + shifts[1:2, :]
        sig = jax.nn.sigmoid(u)
        d_out = frame_of(d_act, t, size) * (sig * (1.0 + u * (1.0 - sig)))
        d_shift = all_cols(d_out)
        d_gain = all_cols(d_out * normed)
        vectors[0] += d_gain
        vectors[1] += d_shift
        one = group_all(d_shift * gains[1:2, :]) / count
        two = group_all(d_gain * gains[1:2, :]) / count
        put_frame(d_h1, t, factor * (d_out * gains[1:2, :] - one - normed * two))


def grad_kernel(place, values, grads, extra, out, long, block, total):
    frames_size, chans = values.shape
    owners, tall, _ = out.shape
    size, outs = (long.shape[0] - frames_size) // 2, total.shape[0] // 27
    frames = frames_size // size
    long[0:size, :] = values[0:size, :]
    long[size : 2 * size, :] = values[0:size, :]
    long[2 * size :, :] = values[...]
    lanes = block.shape[1]
    chan = lax.broadcasted_iota(jnp.int32, (chans, lanes), 0)
    lane = lax.broadcasted_iota(jnp.int32, (chans, lanes), 1)
    pick = (chan == place[0] * outs + lane % outs).astype(jnp.bfloat16)

    @pl.loop(0, frames)
    def _(t):
        rows = grads[pl.ds(pl.multiple_of(t * size, 16), size), :]
        spread_out = jnp.dot(rows, pick, preferred_element_type=jnp.float32).reshape(size // 8, 8, lanes)
        for piece in range(lanes // 128):
            value = spread_out[:, :, piece * 128 : (piece + 1) * 128]
            lane = lax.broadcasted_iota(jnp.int32, value.shape, 2)
            kept = jnp.zeros_like(value)
            for place_in in range(128 // outs):
                number = piece * (128 // outs) + place_in
                if number < 9:
                    h, w = divmod(number, 3)
                    moved = row_shifted(col_shifted(value, 1 - w), 1 - h)
                    kept = jnp.where(lane // outs == place_in, moved, kept)
            block[pl.ds(pl.multiple_of(t * size, 16), size), piece * 128 : (piece + 1) * 128] = kept.reshape(size, 128).astype(jnp.bfloat16)

    side = block[...].T
    for t in range(3):
        part = jnp.dot(side, long[t * size : (t + frames) * size, :], preferred_element_type=jnp.float32)
        total[t * 9 * outs : (t + 1) * 9 * outs, :] = part[: 9 * outs]

    owned = 27 * chans // owners
    lane = lax.broadcasted_iota(jnp.int32, (outs, chans), 1)
    for d in range(owners):
        tap, start = divmod(d * owned, chans)
        one = total[tap * outs : (tap + 1) * outs, :]
        if start + owned > chans:
            one = jnp.concatenate([one, total[(tap + 1) * outs : (tap + 2) * outs, :]], 1)
        one = rolled(one, -start, 1)[:, :chans]
        if extra is not None:
            one = jnp.where(lane < owned, one, extra[...])
        out[d] = one.astype(jnp.bfloat16)


def halves(value):
    high = value.astype(jnp.bfloat16).astype(jnp.float32)
    return high, value - high


def to_spare(value, start, width):
    chans = value.shape[1]
    row = lax.broadcasted_iota(jnp.int32, value.shape, 0)
    lane = lax.broadcasted_iota(jnp.int32, value.shape, 1)
    held = (lane >= start) & (lane < start + width)
    tiles = []
    for tile in range(chans // width // 8):
        kept = jnp.zeros_like(value)
        for r in range(8):
            moved = rolled(value, start - width * (8 * tile + r), 1)
            kept = jnp.where((row == r) & held, moved, kept)
        tiles.append(kept)
    return jnp.concatenate(tiles, 0)


def from_spare(value, start, width):
    rows, chans = value.shape
    row = lax.broadcasted_iota(jnp.int32, (8, chans), 0)
    lane = lax.broadcasted_iota(jnp.int32, (8, chans), 1)
    kept = jnp.zeros((8, chans), jnp.float32)
    for r in range(rows):
        tile = value[8 * (r // 8) : 8 * (r // 8) + 8, :]
        moved = rolled(tile, width * r - start, 1)
        kept = kept + jnp.where((row == r % 8) & (lane // width == r), moved, 0.0)
    for step in (4, 2, 1):
        kept = kept + rolled(kept, step, 0)
    return kept


def own_kernel(place, d_h1, weight, raw_lat, raw_cot, gains, shifts, sums_two, grad, extra, nine, d_act):
    blocks, frames, flat, chans = raw_lat.shape
    size = blocks * flat
    depth = 9 * chans
    me = place[0]
    for ahead_by in range(3):
        value = frame_of(d_h1, jnp.minimum(me + ahead_by, frames - 1), size)
        if ahead_by:
            value = jnp.where(me + ahead_by < frames, value, 0.0)
        store_nine(nine, ahead_by, value, -1)

    def term(frame, tap):
        left = nine[frame * size : (frame + 1) * size, :]
        return jnp.dot(left, weight[tap * depth : (tap + 1) * depth, :], preferred_element_type=jnp.float32)

    d_act[...] = term(2, 0) + term(1, 1) + term(0, 2)

    @pl.when(me == 0)
    def _():
        d_act[...] = d_act[...] + (term(0, 1) + (term(0, 0) + term(1, 0)))

    count = size * (chans // GROUPS)
    value = load_frame(raw_lat, me)
    mean, factor = norm_parts(value)
    normed = (value - mean) * factor
    u = normed * gains[0:1, :] + shifts[0:1, :]
    sig = jax.nn.sigmoid(u)
    d_out = d_act[...].reshape(size // 8, 8, chans) * (sig * (1.0 + u * (1.0 - sig)))
    d_shift = all_cols(d_out)
    d_gain = all_cols(d_out * normed)
    one = group_all(d_shift * gains[0:1, :]) / count
    two = group_all(d_gain * gains[0:1, :]) / count
    d_in = factor * (d_out * gains[0:1, :] - one - normed * two)
    result = (load_frame(raw_cot, me) + d_in).astype(jnp.bfloat16).astype(jnp.float32)
    grad[...] = result.reshape(blocks, flat, chans)

    owned = chans - 40
    pieces = [to_spare(part, owned, 32) for part in (*halves(d_gain), *halves(d_shift))]
    gain_high, gain_low = halves(sums_two[0])
    shift_high, shift_low = halves(sums_two[1])
    turn = me % 4
    mine = jnp.where(turn < 2, jnp.where(turn == 0, gain_high, gain_low), jnp.where(turn == 2, shift_high, shift_low))
    extra[...] = jnp.concatenate(pieces, 0) + to_spare(0.5 * mine, owned + 32, 8)


def sum_kernel(later, earlier, grad, out, *, clips):
    total = earlier[0].astype(jnp.float32)
    for d in range(1, clips):
        total = total + earlier[d].astype(jnp.float32)
    total = total / clips
    rows = total.shape[0]
    for p in range(out.shape[0]):
        out[p, 0:rows, :] = later[...]
        out[p, rows : 2 * rows, :] = total
        out[p, 2 * rows :, :] = grad[p]


def adam_kernel(every, moment, second, new_moment, new_second, direction, vector, grad_input):
    parts, tall, chans = every.shape
    owned = moment.shape[1]
    width = chans // parts
    for layer in range(2):
        start = width * (1 - layer)
        grad = every[:, start : start + width, :].reshape(chans, chans).T[:owned, :]
        new_m = 0.9 * moment[layer] + 0.1 * grad
        new_v = 0.999 * second[layer] + 0.001 * grad * grad
        new_moment[layer] = new_m
        new_second[layer] = new_v
        direction[layer] = new_m / bias_first / (jnp.sqrt(new_v / bias_second) + 1e-08)
    for p in range(parts):
        grad_input[p] = every[p, 2 * width :, :].astype(jnp.bfloat16)
    held = [every[p, width : 2 * width, :] for p in range(parts)]
    summed = held[0]
    for p in range(1, parts):
        summed = summed + held[p]
    for row in range(2):
        high = from_spare(summed[16 * row : 16 * row + 8], owned, 32)
        low = from_spare(summed[16 * row + 8 : 16 * row + 16], owned, 32)
        vector[row : row + 1, :] = (high + low)[0:1]
        mine = sum(held[p] for p in range(parts) if p % 4 in (2 * row, 2 * row + 1))
        vector[2 + row : 3 + row, :] = from_spare(mine, owned + 32, 8)[0:1]


def called(kernel, outs, scratch, args, scalars=0, flops=0, limit=56):
    whole = pl.BlockSpec(memory_space=pltpu.VMEM)
    small = pl.BlockSpec(memory_space=pltpu.SMEM)
    moved = sum(math.prod(a.shape) * a.dtype.itemsize for a in (*args, *outs))
    return pl.pallas_call(
        kernel,
        out_shape=outs,
        in_specs=[small] * scalars + [whole] * (len(args) - scalars),
        out_specs=[whole] * len(outs),
        scratch_shapes=scratch,
        compiler_params=pltpu.CompilerParams(vmem_limit_bytes=limit * 2**20),
        cost_estimate=pl.CostEstimate(flops=flops, bytes_accessed=moved, transcendentals=0),
    )(*args)


def ahead(raw, weight, gains, shifts):
    blocks, frames, flat, chans = raw.shape
    places = blocks * frames * flat
    shape = jax.ShapeDtypeStruct((places, chans), jnp.bfloat16)
    scratch = [pltpu.VMEM((places + 2 * blocks * flat, 9 * chans), jnp.bfloat16)]
    return called(ahead_kernel, [shape] * 3, scratch, (raw, weight, gains, shifts), 0, 2 * places * weight.size)


def back(raw, weight, h_one, gains, shifts):
    blocks, frames, flat, chans = raw.shape
    places = blocks * frames * flat
    outs = [jax.ShapeDtypeStruct((places, chans), jnp.bfloat16), jax.ShapeDtypeStruct((2, 8, chans), jnp.float32)]
    scratch = [
        pltpu.VMEM((places + 2 * blocks * flat, 9 * chans), jnp.bfloat16),
        pltpu.VMEM((places, chans), jnp.float32),
    ]
    return called(back_kernel, outs, scratch, (raw, weight, h_one, gains, shifts), 0, 2 * places * weight.size)


def kernel_grad(place, values, grads, extra, width, size, clips):
    places, chans = values.shape
    outs = [jax.ShapeDtypeStruct((clips, width, chans), jnp.bfloat16)]
    if extra is None:
        body = lambda p, v, g, *rest: grad_kernel(p, v, g, None, *rest)
        args = (place, values, grads)
    else:
        body, args = grad_kernel, (place, values, grads, extra)
    scratch = [
        pltpu.VMEM((places + 2 * size, chans), jnp.bfloat16),
        pltpu.VMEM((places, -(-9 * width // 128) * 128), jnp.bfloat16),
        pltpu.VMEM((27 * width, chans), jnp.float32),
    ]
    return called(body, outs, scratch, args, 1, 2 * places * 27 * width * chans)[0]


def own(place, d_h1, weight, raw_lat, raw_cot, gains, shifts, sums_two):
    blocks, frames, flat, chans = raw_lat.shape
    size = blocks * flat
    outs = [
        jax.ShapeDtypeStruct((blocks, flat, chans), jnp.float32),
        jax.ShapeDtypeStruct((32, chans), jnp.float32),
    ]
    scratch = [pltpu.VMEM((3 * size, 9 * chans), jnp.bfloat16), pltpu.VMEM((size, chans), jnp.float32)]
    args = (place, d_h1, weight, raw_lat, raw_cot, gains, shifts, sums_two)
    return called(own_kernel, outs, scratch, args, 1, 2 * size * weight.size)


def gathered(later, earlier, grads, clips):
    parts, flat, chans = grads.shape
    outs = [jax.ShapeDtypeStruct((parts, 2 * later.shape[0] + flat, chans), jnp.float32)]
    return called(functools.partial(sum_kernel, clips=clips), outs, [], (later, earlier, grads))[0]


def spread(value, axis):
    return lax.all_to_all(jnp.broadcast_to(value[None], (lax.axis_size(axis),) + value.shape), axis, 0, 0)


def conv(values, weight, row_pad):
    chans = values.shape[-1]
    return lax.conv_general_dilated(
        values[None],
        weight.reshape(3, 3, 3, chans, -1),
        (1, 1, 1),
        ((0, 0), (row_pad, row_pad), (1, 1)),
        dimension_numbers=("NDHWC", "DHWIO", "NDHWC"),
        preferred_element_type=jnp.float32,
    )[0]


def per_device(latents, cotangent, conv_weights, gains, shifts, moment, second):
    frames, rows, cols, chans = latents.shape[1:]
    clips, parts = lax.axis_size("dp"), lax.axis_size("space")
    me = lax.axis_index("space")
    place = me.astype(jnp.int32).reshape(1)
    width, size = chans // parts, parts * rows * cols
    f32, bf16 = jnp.float32, jnp.bfloat16
    raw_lat = spread(latents[0].reshape(frames, rows * cols, chans), "space")
    raw_cot = spread(cotangent[0].reshape(frames, rows * cols, chans), "space")
    turned = conv_weights.reshape(2, 27, chans, chans).transpose(0, 1, 3, 2).reshape(2, 27 * chans, chans)

    a_one, h_one, a_two = ahead(raw_lat, conv_weights[0], gains, shifts)
    cot = raw_cot.transpose(1, 0, 2, 3).reshape(frames * size, chans)
    later = kernel_grad(place, a_two, cot, None, width, size, clips)
    later, raw_cot = lax.optimization_barrier((later, raw_cot))
    later = lax.all_to_all(later, "dp", 0, 0)

    d_h1, sums_two = back(raw_cot, turned[1], h_one, gains, shifts)
    grads, extra = own(place, d_h1, turned[0], raw_lat, raw_cot, gains, shifts, sums_two)
    earlier = kernel_grad(place, a_one, d_h1, extra, width, size, clips)
    earlier = lax.all_to_all(earlier, "dp", 0, 0)

    tall = a_two.reshape(frames, size // cols, cols, chans)
    tall = jnp.pad(jnp.concatenate([tall[:1], tall[:1], tall], 0), ((0, 0), (1, 1), (0, 0), (0, 0)))
    tall = lax.dynamic_slice_in_dim(tall, me * rows, rows + 2, 1)
    decoded = (latents[0].astype(f32) + conv(tall, conv_weights[1], 0)).astype(bf16)

    later = jnp.sum(later.astype(f32), 0) / clips
    every = gathered(later, earlier, grads, clips)
    every = lax.all_to_all(every, "space", 0, 0)
    shape = jax.ShapeDtypeStruct(moment.shape, f32)
    outs = [shape, shape, shape, jax.ShapeDtypeStruct((4, chans), f32)]
    outs.append(jax.ShapeDtypeStruct((frames, rows * cols, chans), bf16))
    outs = called(adam_kernel, outs, [], (every, moment, second))
    new_moment, new_second, direction, vector, grad_input = outs
    grad_input = grad_input.reshape(latents.shape)
    return (decoded[None], grad_input, new_moment, new_second, direction, vector)


def solution(mesh):
    placed = (
        P("dp", None, "space", None, None),
        P("dp", None, "space", None, None),
        P(),
        P(),
        P(),
        P(None, "dp", None),
        P(None, "dp", None),
    )
    return jax.shard_map(
        per_device,
        mesh=mesh,
        in_specs=placed,
        out_specs=(
            P("dp", None, "space", None, None),
            P("dp", None, "space", None, None),
            P(None, "dp", None),
            P(None, "dp", None),
            P(None, "dp", None),
            P(),
        ),
        check_vma=False,
    )
```

```python
import functools
import math

import jax
import jax.numpy as jnp
from jax import lax
from jax.experimental import pallas as pl
from jax.experimental.pallas import tpu as pltpu
from jax.sharding import PartitionSpec as P

GROUPS = 32
STEP = 4


bias_first = 1.0 - math.exp(100.0 * math.log(0.9))
bias_second = 1.0 - math.exp(100.0 * math.log(0.999))


def rolled(value, amount, axis):
    return pltpu.roll(value, amount % value.shape[axis], axis)


def all_cols(value):
    total = jnp.sum(value, 0)
    for step in (4, 2, 1):
        total = total + rolled(total, step, 0)
    return total


def group_all(sums):
    size = sums.shape[1] // GROUPS
    lane = lax.broadcasted_iota(jnp.int32, sums.shape, 1)
    step = 1
    while step < size:
        partner = jnp.where((lane & step) == 0, rolled(sums, -step, 1), rolled(sums, step, 1))
        sums = sums + partner
        step *= 2
    return sums


def norm_parts(values):
    count = values.shape[0] * values.shape[1] * (values.shape[2] // GROUPS)
    mean = group_all(all_cols(values)) / count
    var = group_all(all_cols(values * values)) / count - mean * mean
    return mean, lax.rsqrt(var + 1e-05)


def col_shifted(value, step):
    if step == 0:
        return value
    col = lax.broadcasted_iota(jnp.int32, value.shape, 1)
    edge = value.shape[1] - 1 if step > 0 else 0
    return jnp.where(col == edge, 0.0, rolled(value, -step, 1))


def row_shifted(value, step):
    if step == 0:
        return value
    zero = jnp.zeros_like(value[:1])
    if step > 0:
        return jnp.concatenate([value[1:], zero], 0)
    return jnp.concatenate([zero, value[:-1]], 0)


def store_nine(target, frame, value, sign):
    rows, cols, chans = value.shape
    size = rows * cols
    for w in range(3):
        moved = col_shifted(value, sign * (w - 1))
        for h in range(3):
            view = row_shifted(moved, sign * (h - 1)).reshape(size, chans)
            number = 3 * h + w
            target[pl.ds(pl.multiple_of(frame * size, 16), size), number * chans : (number + 1) * chans] = view.astype(jnp.bfloat16)


def load_frame(raw, frame):
    blocks, _, flat, chans = raw.shape
    parts = [raw[b, frame].astype(jnp.float32).reshape(flat // 8, 8, chans) for b in range(blocks)]
    return jnp.concatenate(parts, 0)


def frame_of(flat, frame, size):
    part = flat[pl.ds(pl.multiple_of(frame * size, 16), size), :]
    return part.astype(jnp.float32).reshape(size // 8, 8, part.shape[-1])


def put_frame(flat, frame, value):
    size = value.shape[0] * value.shape[1]
    flat[pl.ds(pl.multiple_of(frame * size, 16), size), :] = value.reshape(size, -1).astype(flat.dtype)


def ahead_kernel(raw, weights, gains, shifts, a_one, h_one, a_two, nine, weight, sem):
    copy = pltpu.make_async_copy(weights.at[0], weight, sem)
    copy.start()
    frames, chans = raw.shape[1], raw.shape[3]
    size = raw.shape[0] * raw.shape[2]
    depth = 9 * chans

    @pl.loop(0, frames, unroll=frames)
    def _(t):
        value = load_frame(raw, t)
        mean, factor = norm_parts(value)
        u = (value - mean) * factor * gains[0:1, :] + shifts[0:1, :]
        act = (u * jax.nn.sigmoid(u)).astype(jnp.bfloat16).astype(jnp.float32)
        put_frame(a_one, t, act)
        store_nine(nine, t + 2, act, 1)

    nine[0:size, :] = nine[2 * size : 3 * size, :]
    nine[size : 2 * size, :] = nine[2 * size : 3 * size, :]
    copy.wait()

    @pl.loop(0, frames // STEP)
    def _(b):
        total = None
        for t in range(3):
            left = nine[pl.ds(pl.multiple_of((b * STEP + t) * size, 16), STEP * size), :]
            part = jnp.dot(left, weight[t * depth : (t + 1) * depth, :], preferred_element_type=jnp.float32)
            total = part if total is None else total + part
        h_one[pl.ds(pl.multiple_of(b * STEP * size, 16), STEP * size), :] = total.astype(jnp.bfloat16)

    @pl.loop(0, frames, unroll=frames)
    def _(t):
        value = frame_of(h_one, t, size)
        mean, factor = norm_parts(value)
        u = (value - mean) * factor * gains[1:2, :] + shifts[1:2, :]
        put_frame(a_two, t, u * jax.nn.sigmoid(u))


def back_kernel(raw, weights, h_one, gains, shifts, d_h1, vectors, nine, d_act, weight, sem):
    copy = pltpu.make_async_copy(weights.at[1], weight, sem)
    copy.start()
    frames, chans = raw.shape[1], raw.shape[3]
    size = raw.shape[0] * raw.shape[2]
    depth = 9 * chans

    @pl.loop(0, frames, unroll=frames)
    def _(t):
        store_nine(nine, t, load_frame(raw, t), -1)

    nine[frames * size :, :] = jnp.zeros((2 * size, depth), jnp.bfloat16)
    copy.wait()

    @pl.loop(0, frames // STEP)
    def _(b):
        total = None
        for t in range(3):
            left = nine[pl.ds(pl.multiple_of((b * STEP + 2 - t) * size, 16), STEP * size), :]
            part = jnp.dot(left, weight[t * depth : (t + 1) * depth, :], preferred_element_type=jnp.float32)
            total = part if total is None else total + part
        d_act[pl.ds(pl.multiple_of(b * STEP * size, 16), STEP * size), :] = total

    pair = jnp.dot(nine[0:size, :], weight[depth : 2 * depth, :], preferred_element_type=jnp.float32)
    both = jnp.dot(nine[0 : 2 * size, :], weight[0:depth, :], preferred_element_type=jnp.float32)
    d_act[0:size, :] = d_act[0:size, :] + (pair + (both[:size] + both[size:]))

    vectors[...] = jnp.zeros_like(vectors)
    count = size * (chans // GROUPS)

    @pl.loop(0, frames, unroll=frames)
    def _(t):
        value = frame_of(h_one, t, size)
        mean, factor = norm_parts(value)
        normed = (value - mean) * factor
        u = normed * gains[1:2, :] + shifts[1:2, :]
        sig = jax.nn.sigmoid(u)
        d_out = frame_of(d_act, t, size) * (sig * (1.0 + u * (1.0 - sig)))
        d_shift = all_cols(d_out)
        d_gain = all_cols(d_out * normed)
        vectors[0] += d_gain
        vectors[1] += d_shift
        one = group_all(d_shift * gains[1:2, :]) / count
        two = group_all(d_gain * gains[1:2, :]) / count
        put_frame(d_h1, t, factor * (d_out * gains[1:2, :] - one - normed * two))


def grad_kernel(place, values, grads, extra, out, long, block, total):
    frames_size, chans = values.shape
    owners, tall, _ = out.shape
    size, outs = (long.shape[0] - frames_size) // 2, total.shape[0] // 27
    frames = frames_size // size
    long[0:size, :] = values[0:size, :]
    long[size : 2 * size, :] = values[0:size, :]
    long[2 * size :, :] = values[...]
    lanes = block.shape[1]
    chan = lax.broadcasted_iota(jnp.int32, (chans, lanes), 0)
    lane = lax.broadcasted_iota(jnp.int32, (chans, lanes), 1)
    pick = (chan == place[0] * outs + lane % outs).astype(jnp.bfloat16)

    @pl.loop(0, frames, unroll=frames)
    def _(t):
        if len(grads.shape) == 4:
            rows = load_frame(grads, t).reshape(size, chans).astype(jnp.bfloat16)
        else:
            rows = grads[pl.ds(pl.multiple_of(t * size, 16), size), :]
        spread_out = jnp.dot(rows, pick, preferred_element_type=jnp.float32).reshape(size // 8, 8, lanes)
        for piece in range(lanes // 128):
            value = spread_out[:, :, piece * 128 : (piece + 1) * 128]
            lane = lax.broadcasted_iota(jnp.int32, value.shape, 2)
            kept = jnp.zeros_like(value)
            for place_in in range(128 // outs):
                number = piece * (128 // outs) + place_in
                if number < 9:
                    h, w = divmod(number, 3)
                    moved = row_shifted(col_shifted(value, 1 - w), 1 - h)
                    kept = jnp.where(lane // outs == place_in, moved, kept)
            block[pl.ds(pl.multiple_of(t * size, 16), size), piece * 128 : (piece + 1) * 128] = kept.reshape(size, 128).astype(jnp.bfloat16)

    side = block[...].T
    for t in range(3):
        part = jnp.dot(side, long[t * size : (t + frames) * size, :], preferred_element_type=jnp.float32)
        total[t * 9 * outs : (t + 1) * 9 * outs, :] = part[: 9 * outs]

    owned = 27 * chans // owners
    lane = lax.broadcasted_iota(jnp.int32, (outs, chans), 1)
    for d in range(owners):
        tap, start = divmod(d * owned, chans)
        one = total[tap * outs : (tap + 1) * outs, :]
        if start + owned > chans:
            one = jnp.concatenate([one, total[(tap + 1) * outs : (tap + 2) * outs, :]], 1)
        one = rolled(one, -start, 1)[:, :chans]
        if extra is not None:
            one = jnp.where(lane < owned, one, extra[...])
        out[d] = one.astype(jnp.bfloat16)


def halves(value):
    high = value.astype(jnp.bfloat16).astype(jnp.float32)
    return high, value - high


def to_spare(value, start, width):
    chans = value.shape[1]
    row = lax.broadcasted_iota(jnp.int32, value.shape, 0)
    lane = lax.broadcasted_iota(jnp.int32, value.shape, 1)
    held = (lane >= start) & (lane < start + width)
    tiles = []
    for tile in range(chans // width // 8):
        kept = jnp.zeros_like(value)
        for r in range(8):
            moved = rolled(value, start - width * (8 * tile + r), 1)
            kept = jnp.where((row == r) & held, moved, kept)
        tiles.append(kept)
    return jnp.concatenate(tiles, 0)


def from_spare(value, start, width):
    rows, chans = value.shape
    row = lax.broadcasted_iota(jnp.int32, (8, chans), 0)
    lane = lax.broadcasted_iota(jnp.int32, (8, chans), 1)
    kept = jnp.zeros((8, chans), jnp.float32)
    for r in range(rows):
        tile = value[8 * (r // 8) : 8 * (r // 8) + 8, :]
        moved = rolled(tile, width * r - start, 1)
        kept = kept + jnp.where((row == r % 8) & (lane // width == r), moved, 0.0)
    for step in (4, 2, 1):
        kept = kept + rolled(kept, step, 0)
    return kept


def own_kernel(place, d_h1, weights, raw_lat, raw_cot, gains, shifts, sums_two, grad, extra, nine, d_act, weight, sem):
    copy = pltpu.make_async_copy(weights.at[0], weight, sem)
    copy.start()
    blocks, frames, flat, chans = raw_lat.shape
    size = blocks * flat
    depth = 9 * chans
    me = place[0]
    for ahead_by in range(3):
        value = frame_of(d_h1, jnp.minimum(me + ahead_by, frames - 1), size)
        if ahead_by:
            value = jnp.where(me + ahead_by < frames, value, 0.0)
        store_nine(nine, ahead_by, value, -1)
    copy.wait()

    def term(frame, tap):
        left = nine[frame * size : (frame + 1) * size, :]
        return jnp.dot(left, weight[tap * depth : (tap + 1) * depth, :], preferred_element_type=jnp.float32)

    d_act[...] = term(2, 0) + term(1, 1) + term(0, 2)

    @pl.when(me == 0)
    def _():
        d_act[...] = d_act[...] + (term(0, 1) + (term(0, 0) + term(1, 0)))

    count = size * (chans // GROUPS)
    value = load_frame(raw_lat, me)
    mean, factor = norm_parts(value)
    normed = (value - mean) * factor
    u = normed * gains[0:1, :] + shifts[0:1, :]
    sig = jax.nn.sigmoid(u)
    d_out = d_act[...].reshape(size // 8, 8, chans) * (sig * (1.0 + u * (1.0 - sig)))
    d_shift = all_cols(d_out)
    d_gain = all_cols(d_out * normed)
    one = group_all(d_shift * gains[0:1, :]) / count
    two = group_all(d_gain * gains[0:1, :]) / count
    d_in = factor * (d_out * gains[0:1, :] - one - normed * two)
    result = (load_frame(raw_cot, me) + d_in).astype(jnp.bfloat16).astype(jnp.float32)
    grad[...] = result.reshape(blocks, flat, chans)

    owned = chans - 40
    pieces = [to_spare(part, owned, 32) for part in (*halves(d_gain), *halves(d_shift))]
    gain_high, gain_low = halves(sums_two[0])
    shift_high, shift_low = halves(sums_two[1])
    turn = me % 4
    mine = jnp.where(turn < 2, jnp.where(turn == 0, gain_high, gain_low), jnp.where(turn == 2, shift_high, shift_low))
    extra[...] = jnp.concatenate(pieces, 0) + to_spare(0.5 * mine, owned + 32, 8)


def sum_kernel(later, earlier, grad, out, *, clips):
    total = earlier[0].astype(jnp.float32)
    for d in range(1, clips):
        total = total + earlier[d].astype(jnp.float32)
    total = total / clips
    rows = total.shape[0]
    for p in range(out.shape[0]):
        out[p, 0:rows, :] = later[...]
        out[p, rows : 2 * rows, :] = total
        out[p, 2 * rows :, :] = grad[p]


def adam_kernel(every, moment, second, new_moment, new_second, direction, vector, grad_input):
    parts, tall, chans = every.shape
    owned = moment.shape[1]
    width = chans // parts
    for layer in range(2):
        start = width * (1 - layer)
        grad = every[:, start : start + width, :].reshape(chans, chans).T[:owned, :]
        new_m = 0.9 * moment[layer] + 0.1 * grad
        new_v = 0.999 * second[layer] + 0.001 * grad * grad
        new_moment[layer] = new_m
        new_second[layer] = new_v
        direction[layer] = new_m / bias_first / (jnp.sqrt(new_v / bias_second) + 1e-08)
    for p in range(parts):
        grad_input[p] = every[p, 2 * width :, :].astype(jnp.bfloat16)
    held = [every[p, width : 2 * width, :] for p in range(parts)]
    summed = held[0]
    for p in range(1, parts):
        summed = summed + held[p]
    for row in range(2):
        high = from_spare(summed[16 * row : 16 * row + 8], owned, 32)
        low = from_spare(summed[16 * row + 8 : 16 * row + 16], owned, 32)
        vector[row : row + 1, :] = (high + low)[0:1]
        mine = sum(held[p] for p in range(parts) if p % 4 in (2 * row, 2 * row + 1))
        vector[2 + row : 3 + row, :] = from_spare(mine, owned + 32, 8)[0:1]


def turn_kernel(weights, turned):
    chans = weights.shape[2]
    for tap in range(weights.shape[1] // chans):
        rows = slice(tap * chans, (tap + 1) * chans)
        turned[0, rows, :] = weights[0, rows, :].T


def decode_kernel(place, a_two, weights, latent, decoded, tall, nine, weight, sem):
    copy = pltpu.make_async_copy(weights.at[1], weight, sem)
    copy.start()
    frames, flat, chans = latent.shape
    size = a_two.shape[0] // frames
    rows, every = flat // 8, size // 8
    pitch = nine.shape[0] // (frames + 2)
    depth = 9 * chans
    tall[0] = jnp.zeros(tall.shape[1:], jnp.float32)
    tall[every + 1] = jnp.zeros(tall.shape[1:], jnp.float32)
    rest = jnp.zeros((pitch // 8 - rows, 8, chans), jnp.float32)
    for t in range(frames):
        tall[1 : every + 1] = frame_of(a_two, t, size)
        part = tall[pl.ds(place[0] * rows, rows + 2)]
        for w in range(3):
            moved = col_shifted(part, w - 1)
            for h in range(3):
                view = jnp.concatenate([moved[h : h + rows], rest], 0).reshape(pitch, chans)
                number = 3 * h + w
                nine[(t + 2) * pitch : (t + 3) * pitch, number * chans : (number + 1) * chans] = view.astype(jnp.bfloat16)
    nine[0:pitch, :] = nine[2 * pitch : 3 * pitch, :]
    nine[pitch : 2 * pitch, :] = nine[2 * pitch : 3 * pitch, :]
    copy.wait()
    total = None
    for t in range(3):
        left = nine[t * pitch : (t + frames) * pitch, :]
        part = jnp.dot(left, weight[t * depth : (t + 1) * depth, :], preferred_element_type=jnp.float32)
        total = part if total is None else total + part
    for t in range(frames):
        value = latent[t].astype(jnp.float32) + total[t * pitch : t * pitch + flat, :]
        decoded[t] = value.astype(jnp.bfloat16)


def called(kernel, outs, scratch, args, scalars=0, flops=0, apart=None, limit=16):
    whole = pl.BlockSpec(memory_space=pltpu.VMEM)
    small = pl.BlockSpec(memory_space=pltpu.SMEM)
    away = pl.BlockSpec(memory_space=pl.ANY)
    moved = sum(math.prod(a.shape) * a.dtype.itemsize for a in (*args, *outs))
    return pl.pallas_call(
        kernel,
        out_shape=outs,
        in_specs=[small if n < scalars else away if n == apart else whole for n in range(len(args))],
        out_specs=[whole] * len(outs),
        scratch_shapes=scratch,
        compiler_params=pltpu.CompilerParams(vmem_limit_bytes=limit * 2**20),
        cost_estimate=pl.CostEstimate(flops=flops, bytes_accessed=moved, transcendentals=0),
    )(*args)


def held(weights):
    return [pltpu.VMEM(weights.shape[1:], weights.dtype), pltpu.SemaphoreType.DMA]


def ahead(raw, weights, gains, shifts):
    blocks, frames, flat, chans = raw.shape
    places = blocks * frames * flat
    shape = jax.ShapeDtypeStruct((places, chans), jnp.bfloat16)
    scratch = [pltpu.VMEM((places + 2 * blocks * flat, 9 * chans), jnp.bfloat16)] + held(weights)
    return called(ahead_kernel, [shape] * 3, scratch, (raw, weights, gains, shifts), 0, places * weights.size, 1, 58)


def back(raw, weights, h_one, gains, shifts):
    blocks, frames, flat, chans = raw.shape
    places = blocks * frames * flat
    outs = [jax.ShapeDtypeStruct((places, chans), jnp.bfloat16), jax.ShapeDtypeStruct((2, 8, chans), jnp.float32)]
    scratch = [
        pltpu.VMEM((places + 2 * blocks * flat, 9 * chans), jnp.bfloat16),
        pltpu.VMEM((places, chans), jnp.float32),
    ] + held(weights)
    return called(back_kernel, outs, scratch, (raw, weights, h_one, gains, shifts), 0, places * weights.size, 1, 58)


def kernel_grad(place, values, grads, extra, width, size, clips):
    places, chans = values.shape
    outs = [jax.ShapeDtypeStruct((clips, width, chans), jnp.bfloat16)]
    if extra is None:
        body = lambda p, v, g, *rest: grad_kernel(p, v, g, None, *rest)
        args = (place, values, grads)
    else:
        body, args = grad_kernel, (place, values, grads, extra)
    scratch = [
        pltpu.VMEM((places + 2 * size, chans), jnp.bfloat16),
        pltpu.VMEM((places, -(-9 * width // 128) * 128), jnp.bfloat16),
        pltpu.VMEM((27 * width, chans), jnp.float32),
    ]
    return called(body, outs, scratch, args, 1, 2 * places * 27 * width * chans)[0]


def own(place, d_h1, weights, raw_lat, raw_cot, gains, shifts, sums_two):
    blocks, frames, flat, chans = raw_lat.shape
    size = blocks * flat
    outs = [
        jax.ShapeDtypeStruct((blocks, flat, chans), jnp.float32),
        jax.ShapeDtypeStruct((32, chans), jnp.float32),
    ]
    scratch = [pltpu.VMEM((3 * size, 9 * chans), jnp.bfloat16), pltpu.VMEM((size, chans), jnp.float32)] + held(weights)
    args = (place, d_h1, weights, raw_lat, raw_cot, gains, shifts, sums_two)
    return called(own_kernel, outs, scratch, args, 1, size * weights.size, 2, 58)


def gathered(later, earlier, grads, clips):
    parts, flat, chans = grads.shape
    outs = [jax.ShapeDtypeStruct((parts, 2 * later.shape[0] + flat, chans), jnp.float32)]
    return called(functools.partial(sum_kernel, clips=clips), outs, [], (later, earlier, grads))[0]


def turn(weights):
    layers, depth, chans = weights.shape
    block = pl.BlockSpec((1, depth // 9, chans), lambda k, n: (k, n, 0))
    return pl.pallas_call(
        turn_kernel,
        grid=(layers, 9),
        out_shape=jax.ShapeDtypeStruct(weights.shape, weights.dtype),
        in_specs=[block],
        out_specs=block,
        cost_estimate=pl.CostEstimate(flops=0, bytes_accessed=4 * weights.size, transcendentals=0),
    )(weights)


def decode(place, a_two, weights, latent):
    frames, flat, chans = latent.shape
    size = a_two.shape[0] // frames
    pitch = -(-flat // 16) * 16
    outs = [jax.ShapeDtypeStruct(latent.shape, jnp.bfloat16)]
    scratch = [
        pltpu.VMEM((size // 8 + 2, 8, chans), jnp.float32),
        pltpu.VMEM(((frames + 2) * pitch, 9 * chans), jnp.bfloat16),
    ] + held(weights)
    return called(decode_kernel, outs, scratch, (place, a_two, weights, latent), 1, frames * pitch * weights.size, 2, 58)[0]


def spread(value, axis):
    return lax.all_to_all(jnp.broadcast_to(value[None], (lax.axis_size(axis),) + value.shape), axis, 0, 0)


def per_device(latents, cotangent, conv_weights, gains, shifts, moment, second):
    frames, rows, cols, chans = latents.shape[1:]
    clips, parts = lax.axis_size("dp"), lax.axis_size("space")
    me = lax.axis_index("space")
    place = me.astype(jnp.int32).reshape(1)
    width, size = chans // parts, parts * rows * cols
    f32, bf16 = jnp.float32, jnp.bfloat16
    latent = latents[0].reshape(frames, rows * cols, chans)
    raw_lat = spread(latent, "space")
    turned = turn(conv_weights)
    upstream, raw_lat, turned = lax.optimization_barrier((cotangent[0], raw_lat, turned))
    raw_cot = spread(upstream.reshape(frames, rows * cols, chans), "space")

    a_one, h_one, a_two = ahead(raw_lat, conv_weights, gains, shifts)
    later = kernel_grad(place, a_two, raw_cot, None, width, size, clips)
    later, raw_cot = lax.optimization_barrier((later, raw_cot))
    later = lax.all_to_all(later, "dp", 0, 0)

    d_h1, sums_two = back(raw_cot, turned, h_one, gains, shifts)
    grads, extra = own(place, d_h1, turned, raw_lat, raw_cot, gains, shifts, sums_two)
    earlier = kernel_grad(place, a_one, d_h1, extra, width, size, clips)
    earlier = lax.all_to_all(earlier, "dp", 0, 0)
    decoded = decode(place, a_two, conv_weights, latent)

    later = jnp.sum(later.astype(f32), 0) / clips
    every = gathered(later, earlier, grads, clips)
    every = lax.all_to_all(every, "space", 0, 0)
    shape = jax.ShapeDtypeStruct(moment.shape, f32)
    outs = [shape, shape, shape, jax.ShapeDtypeStruct((4, chans), f32)]
    outs.append(jax.ShapeDtypeStruct((frames, rows * cols, chans), bf16))
    outs = called(adam_kernel, outs, [], (every, moment, second))
    new_moment, new_second, direction, vector, grad_input = outs
    grad_input = grad_input.reshape(latents.shape)
    return (decoded.reshape(latents.shape), grad_input, new_moment, new_second, direction, vector)


def solution(mesh):
    placed = (
        P("dp", None, "space", None, None),
        P("dp", None, "space", None, None),
        P(),
        P(),
        P(),
        P(None, "dp", None),
        P(None, "dp", None),
    )
    return jax.shard_map(
        per_device,
        mesh=mesh,
        in_specs=placed,
        out_specs=(
            P("dp", None, "space", None, None),
            P("dp", None, "space", None, None),
            P(None, "dp", None),
            P(None, "dp", None),
            P(None, "dp", None),
            P(),
        ),
        check_vma=False,
    )
```

```python
import functools
import math

import jax
import jax.numpy as jnp
from jax import lax
from jax.experimental import pallas as pl
from jax.experimental.pallas import tpu as pltpu
from jax.sharding import PartitionSpec as P

GROUPS = 32
STEP = 4


bias_first = 1.0 - math.exp(100.0 * math.log(0.9))
bias_second = 1.0 - math.exp(100.0 * math.log(0.999))


def rolled(value, amount, axis):
    return pltpu.roll(value, amount % value.shape[axis], axis)


def all_cols(value):
    total = jnp.sum(value, 0)
    for step in (4, 2, 1):
        total = total + rolled(total, step, 0)
    return total


def group_all(sums):
    size = sums.shape[1] // GROUPS
    lane = lax.broadcasted_iota(jnp.int32, sums.shape, 1)
    step = 1
    while step < size:
        partner = jnp.where((lane & step) == 0, rolled(sums, -step, 1), rolled(sums, step, 1))
        sums = sums + partner
        step *= 2
    return sums


def norm_parts(values):
    count = values.shape[0] * values.shape[1] * (values.shape[2] // GROUPS)
    mean = group_all(all_cols(values)) / count
    var = group_all(all_cols(values * values)) / count - mean * mean
    return mean, lax.rsqrt(var + 1e-05)


def col_shifted(value, step):
    if step == 0:
        return value
    col = lax.broadcasted_iota(jnp.int32, value.shape, 1)
    edge = value.shape[1] - 1 if step > 0 else 0
    return jnp.where(col == edge, 0.0, rolled(value, -step, 1))


def row_shifted(value, step):
    if step == 0:
        return value
    zero = jnp.zeros_like(value[:1])
    if step > 0:
        return jnp.concatenate([value[1:], zero], 0)
    return jnp.concatenate([zero, value[:-1]], 0)


def store_nine(target, frame, value, sign):
    rows, cols, chans = value.shape
    size = rows * cols
    for w in range(3):
        moved = col_shifted(value, sign * (w - 1))
        for h in range(3):
            view = row_shifted(moved, sign * (h - 1)).reshape(size, chans)
            number = 3 * h + w
            target[pl.ds(pl.multiple_of(frame * size, 16), size), number * chans : (number + 1) * chans] = view.astype(jnp.bfloat16)


def load_frame(raw, frame):
    blocks, _, flat, chans = raw.shape
    parts = [raw[b, frame].astype(jnp.float32).reshape(flat // 8, 8, chans) for b in range(blocks)]
    return jnp.concatenate(parts, 0)


def frame_of(flat, frame, size):
    part = flat[pl.ds(pl.multiple_of(frame * size, 16), size), :]
    return part.astype(jnp.float32).reshape(size // 8, 8, part.shape[-1])


def put_frame(flat, frame, value):
    size = value.shape[0] * value.shape[1]
    flat[pl.ds(pl.multiple_of(frame * size, 16), size), :] = value.reshape(size, -1).astype(flat.dtype)


def ahead_part(raw, gains, shifts, a_one, h_one, a_two, nine, weight, copy):
    frames, chans = raw.shape[1], raw.shape[3]
    size = raw.shape[0] * raw.shape[2]
    depth = 9 * chans

    @pl.loop(0, frames, unroll=frames)
    def _(t):
        value = load_frame(raw, t)
        mean, factor = norm_parts(value)
        u = (value - mean) * factor * gains[0:1, :] + shifts[0:1, :]
        act = (u * jax.nn.sigmoid(u)).astype(jnp.bfloat16).astype(jnp.float32)
        put_frame(a_one, t, act)
        store_nine(nine, t + 2, act, 1)

    nine[0:size, :] = nine[2 * size : 3 * size, :]
    nine[size : 2 * size, :] = nine[2 * size : 3 * size, :]
    copy.wait()

    @pl.loop(0, frames // STEP, unroll=frames // STEP)
    def _(b):
        total = None
        for t in range(3):
            left = nine[pl.ds(pl.multiple_of((b * STEP + t) * size, 16), STEP * size), :]
            part = jnp.dot(left, weight[t * depth : (t + 1) * depth, :], preferred_element_type=jnp.float32)
            total = part if total is None else total + part
        h_one[pl.ds(pl.multiple_of(b * STEP * size, 16), STEP * size), :] = total.astype(jnp.bfloat16)

    @pl.loop(0, frames, unroll=frames)
    def _(t):
        value = frame_of(h_one, t, size)
        mean, factor = norm_parts(value)
        u = (value - mean) * factor * gains[1:2, :] + shifts[1:2, :]
        put_frame(a_two, t, u * jax.nn.sigmoid(u))


def back_part(raw, h_one, gains, shifts, d_h1, vectors, nine, d_act, weight, copy):
    frames, chans = raw.shape[1], raw.shape[3]
    size = raw.shape[0] * raw.shape[2]
    depth = 9 * chans

    @pl.loop(0, frames, unroll=frames)
    def _(t):
        store_nine(nine, t, load_frame(raw, t), -1)

    nine[frames * size :, :] = jnp.zeros((2 * size, depth), jnp.bfloat16)
    copy.wait()

    @pl.loop(0, frames // STEP, unroll=frames // STEP)
    def _(b):
        total = None
        for t in range(3):
            left = nine[pl.ds(pl.multiple_of((b * STEP + 2 - t) * size, 16), STEP * size), :]
            part = jnp.dot(left, weight[t * depth : (t + 1) * depth, :], preferred_element_type=jnp.float32)
            total = part if total is None else total + part
        d_act[pl.ds(pl.multiple_of(b * STEP * size, 16), STEP * size), :] = total

    pair = jnp.dot(nine[0:size, :], weight[depth : 2 * depth, :], preferred_element_type=jnp.float32)
    both = jnp.dot(nine[0 : 2 * size, :], weight[0:depth, :], preferred_element_type=jnp.float32)
    d_act[0:size, :] = d_act[0:size, :] + (pair + (both[:size] + both[size:]))

    vectors[...] = jnp.zeros_like(vectors)
    count = size * (chans // GROUPS)

    @pl.loop(0, frames, unroll=frames)
    def _(t):
        value = frame_of(h_one, t, size)
        mean, factor = norm_parts(value)
        normed = (value - mean) * factor
        u = normed * gains[1:2, :] + shifts[1:2, :]
        sig = jax.nn.sigmoid(u)
        d_out = frame_of(d_act, t, size) * (sig * (1.0 + u * (1.0 - sig)))
        d_shift = all_cols(d_out)
        d_gain = all_cols(d_out * normed)
        vectors[0] += d_gain
        vectors[1] += d_shift
        one = group_all(d_shift * gains[1:2, :]) / count
        two = group_all(d_gain * gains[1:2, :]) / count
        put_frame(d_h1, t, factor * (d_out * gains[1:2, :] - one - normed * two))


def grad_part(place, values, grads, extra, out, long, block, total):
    frames_size, chans = values.shape
    owners, tall, _ = out.shape
    size, outs = (long.shape[0] - frames_size) // 2, total.shape[0] // 27
    frames = frames_size // size
    long[0:size, :] = values[0:size, :]
    long[size : 2 * size, :] = values[0:size, :]
    long[2 * size :, :] = values[...]
    lanes = block.shape[1]
    chan = lax.broadcasted_iota(jnp.int32, (chans, lanes), 0)
    lane = lax.broadcasted_iota(jnp.int32, (chans, lanes), 1)
    pick = (chan == place[0] * outs + lane % outs).astype(jnp.bfloat16)

    @pl.loop(0, frames, unroll=frames)
    def _(t):
        if len(grads.shape) == 4:
            rows = load_frame(grads, t).reshape(size, chans).astype(jnp.bfloat16)
        else:
            rows = grads[pl.ds(pl.multiple_of(t * size, 16), size), :]
        spread_out = jnp.dot(rows, pick, preferred_element_type=jnp.float32).reshape(size // 8, 8, lanes)
        for piece in range(lanes // 128):
            value = spread_out[:, :, piece * 128 : (piece + 1) * 128]
            lane = lax.broadcasted_iota(jnp.int32, value.shape, 2)
            kept = jnp.zeros_like(value)
            for place_in in range(128 // outs):
                number = piece * (128 // outs) + place_in
                if number < 9:
                    h, w = divmod(number, 3)
                    moved = row_shifted(col_shifted(value, 1 - w), 1 - h)
                    kept = jnp.where(lane // outs == place_in, moved, kept)
            block[pl.ds(pl.multiple_of(t * size, 16), size), piece * 128 : (piece + 1) * 128] = kept.reshape(size, 128).astype(jnp.bfloat16)

    side = block[...].T
    for t in range(3):
        part = jnp.dot(side, long[t * size : (t + frames) * size, :], preferred_element_type=jnp.float32)
        total[t * 9 * outs : (t + 1) * 9 * outs, :] = part[: 9 * outs]

    owned = 27 * chans // owners
    lane = lax.broadcasted_iota(jnp.int32, (outs, chans), 1)
    for d in range(owners):
        tap, start = divmod(d * owned, chans)
        one = total[tap * outs : (tap + 1) * outs, :]
        if start + owned > chans:
            one = jnp.concatenate([one, total[(tap + 1) * outs : (tap + 2) * outs, :]], 1)
        one = rolled(one, -start, 1)[:, :chans]
        if extra is not None:
            one = jnp.where(lane < owned, one, extra[...])
        out[d] = one.astype(jnp.bfloat16)


def halves(value):
    high = value.astype(jnp.bfloat16).astype(jnp.float32)
    return high, value - high


def to_spare(value, start, width):
    chans = value.shape[1]
    row = lax.broadcasted_iota(jnp.int32, value.shape, 0)
    lane = lax.broadcasted_iota(jnp.int32, value.shape, 1)
    held = (lane >= start) & (lane < start + width)
    tiles = []
    for tile in range(chans // width // 8):
        kept = jnp.zeros_like(value)
        for r in range(8):
            moved = rolled(value, start - width * (8 * tile + r), 1)
            kept = jnp.where((row == r) & held, moved, kept)
        tiles.append(kept)
    return jnp.concatenate(tiles, 0)


def from_spare(value, start, width):
    rows, chans = value.shape
    row = lax.broadcasted_iota(jnp.int32, (8, chans), 0)
    lane = lax.broadcasted_iota(jnp.int32, (8, chans), 1)
    kept = jnp.zeros((8, chans), jnp.float32)
    for r in range(rows):
        tile = value[8 * (r // 8) : 8 * (r // 8) + 8, :]
        moved = rolled(tile, width * r - start, 1)
        kept = kept + jnp.where((row == r % 8) & (lane // width == r), moved, 0.0)
    for step in (4, 2, 1):
        kept = kept + rolled(kept, step, 0)
    return kept


def own_part(place, d_h1, raw_lat, raw_cot, gains, shifts, sums_two, grad, extra, nine, d_act, weight, copy):
    blocks, frames, flat, chans = raw_lat.shape
    size = blocks * flat
    depth = 9 * chans
    me = place[0]
    for ahead_by in range(3):
        value = frame_of(d_h1, jnp.minimum(me + ahead_by, frames - 1), size)
        if ahead_by:
            value = jnp.where(me + ahead_by < frames, value, 0.0)
        store_nine(nine, ahead_by, value, -1)
    copy.wait()

    def term(frame, tap):
        left = nine[frame * size : (frame + 1) * size, :]
        return jnp.dot(left, weight[tap * depth : (tap + 1) * depth, :], preferred_element_type=jnp.float32)

    d_act[...] = term(2, 0) + term(1, 1) + term(0, 2)

    @pl.when(me == 0)
    def _():
        d_act[...] = d_act[...] + (term(0, 1) + (term(0, 0) + term(1, 0)))

    count = size * (chans // GROUPS)
    value = load_frame(raw_lat, me)
    mean, factor = norm_parts(value)
    normed = (value - mean) * factor
    u = normed * gains[0:1, :] + shifts[0:1, :]
    sig = jax.nn.sigmoid(u)
    d_out = d_act[...].reshape(size // 8, 8, chans) * (sig * (1.0 + u * (1.0 - sig)))
    d_shift = all_cols(d_out)
    d_gain = all_cols(d_out * normed)
    one = group_all(d_shift * gains[0:1, :]) / count
    two = group_all(d_gain * gains[0:1, :]) / count
    d_in = factor * (d_out * gains[0:1, :] - one - normed * two)
    result = (load_frame(raw_cot, me) + d_in).astype(jnp.bfloat16).astype(jnp.float32)
    grad[...] = result.reshape(blocks, flat, chans)

    owned = chans - 40
    pieces = [to_spare(part, owned, 32) for part in (*halves(d_gain), *halves(d_shift))]
    gain_high, gain_low = halves(sums_two[0])
    shift_high, shift_low = halves(sums_two[1])
    turn = me % 4
    mine = jnp.where(turn < 2, jnp.where(turn == 0, gain_high, gain_low), jnp.where(turn == 2, shift_high, shift_low))
    extra[...] = jnp.concatenate(pieces, 0) + to_spare(0.5 * mine, owned + 32, 8)


def first_kernel(place, raw, weights, gains, shifts, a_one, h_one, a_two, out, nine, weight, sem, long, block, total):
    raw_lat, raw_cot = raw.at[:, 0], raw.at[:, 1]
    copy = pltpu.make_async_copy(weights.at[0], weight, sem)
    copy.start()
    ahead_part(raw_lat, gains, shifts, a_one, h_one, a_two, nine, weight, copy)
    grad_part(place, a_two, raw_cot, None, out, long, block, total)


def second_kernel(place, raw, turned, h_one, a_one, gains, shifts, grad, out, nine, weight, sem, long, block, total, other, other_sem, d_act, own_act, d_h1, sums_two, extra):
    raw_lat, raw_cot = raw.at[:, 0], raw.at[:, 1]
    copy = pltpu.make_async_copy(turned.at[1], weight, sem)
    copy.start()
    other_copy = pltpu.make_async_copy(turned.at[0], other, other_sem)
    other_copy.start()
    back_part(raw_cot, h_one, gains, shifts, d_h1, sums_two, nine, d_act, weight, copy)
    own_part(place, d_h1, raw_lat, raw_cot, gains, shifts, sums_two, grad, extra, nine, own_act, other, other_copy)
    grad_part(place, a_one, d_h1, extra, out, long, block, total)


def sum_kernel(later, earlier, grad, out, *, clips):
    total = earlier[0].astype(jnp.float32)
    for d in range(1, clips):
        total = total + earlier[d].astype(jnp.float32)
    total = total / clips
    rows = total.shape[0]
    for p in range(out.shape[0]):
        out[p, 0:rows, :] = later[...]
        out[p, rows : 2 * rows, :] = total
        out[p, 2 * rows :, :] = grad[p]


def adam_kernel(every, moment, second, new_moment, new_second, direction, vector, grad_input):
    parts, tall, chans = every.shape
    owned = moment.shape[1]
    width = chans // parts
    for layer in range(2):
        start = width * (1 - layer)
        grad = every[:, start : start + width, :].reshape(chans, chans).T[:owned, :]
        new_m = 0.9 * moment[layer] + 0.1 * grad
        new_v = 0.999 * second[layer] + 0.001 * grad * grad
        new_moment[layer] = new_m
        new_second[layer] = new_v
        direction[layer] = new_m / bias_first / (jnp.sqrt(new_v / bias_second) + 1e-08)
    for p in range(parts):
        grad_input[p] = every[p, 2 * width :, :].astype(jnp.bfloat16)
    held = [every[p, width : 2 * width, :] for p in range(parts)]
    summed = held[0]
    for p in range(1, parts):
        summed = summed + held[p]
    for row in range(2):
        high = from_spare(summed[16 * row : 16 * row + 8], owned, 32)
        low = from_spare(summed[16 * row + 8 : 16 * row + 16], owned, 32)
        vector[row : row + 1, :] = (high + low)[0:1]
        mine = sum(held[p] for p in range(parts) if p % 4 in (2 * row, 2 * row + 1))
        vector[2 + row : 3 + row, :] = from_spare(mine, owned + 32, 8)[0:1]


def turn_kernel(weights, turned):
    chans = weights.shape[2]
    for tap in range(weights.shape[1] // chans):
        rows = slice(tap * chans, (tap + 1) * chans)
        turned[0, rows, :] = weights[0, rows, :].T


def decode_kernel(place, a_two, weights, latent, decoded, tall, nine, weight, sem):
    copy = pltpu.make_async_copy(weights.at[1], weight, sem)
    copy.start()
    frames, flat, chans = latent.shape
    size = a_two.shape[0] // frames
    rows, every = flat // 8, size // 8
    pitch = nine.shape[0] // (frames + 2)
    depth = 9 * chans
    tall[0] = jnp.zeros(tall.shape[1:], jnp.float32)
    tall[every + 1] = jnp.zeros(tall.shape[1:], jnp.float32)
    rest = jnp.zeros((pitch // 8 - rows, 8, chans), jnp.float32)
    for t in range(frames):
        tall[1 : every + 1] = frame_of(a_two, t, size)
        part = tall[pl.ds(place[0] * rows, rows + 2)]
        for w in range(3):
            moved = col_shifted(part, w - 1)
            for h in range(3):
                view = jnp.concatenate([moved[h : h + rows], rest], 0).reshape(pitch, chans)
                number = 3 * h + w
                nine[(t + 2) * pitch : (t + 3) * pitch, number * chans : (number + 1) * chans] = view.astype(jnp.bfloat16)
    nine[0:pitch, :] = nine[2 * pitch : 3 * pitch, :]
    nine[pitch : 2 * pitch, :] = nine[2 * pitch : 3 * pitch, :]
    copy.wait()
    total = None
    for t in range(3):
        left = nine[t * pitch : (t + frames) * pitch, :]
        part = jnp.dot(left, weight[t * depth : (t + 1) * depth, :], preferred_element_type=jnp.float32)
        total = part if total is None else total + part
    for t in range(frames):
        value = latent[t].astype(jnp.float32) + total[t * pitch : t * pitch + flat, :]
        decoded[t] = value.astype(jnp.bfloat16)


def called(kernel, outs, scratch, args, specs=None, flops=0, limit=16):
    whole = pl.BlockSpec(memory_space=pltpu.VMEM)
    specs = specs or [whole] * len(args)
    moved = sum(math.prod(a.shape) * a.dtype.itemsize for a in (*args, *outs))
    return pl.pallas_call(
        kernel,
        out_shape=outs,
        in_specs=[whole if spec is None else spec for spec in specs],
        out_specs=[whole] * len(outs),
        scratch_shapes=scratch,
        compiler_params=pltpu.CompilerParams(vmem_limit_bytes=limit * 2**20),
        cost_estimate=pl.CostEstimate(flops=flops, bytes_accessed=moved, transcendentals=0),
    )(*args)


def held(weights):
    return [pltpu.VMEM(weights.shape[1:], weights.dtype), pltpu.SemaphoreType.DMA]


def small():
    return pl.BlockSpec(memory_space=pltpu.SMEM)


def away():
    return pl.BlockSpec(memory_space=pl.ANY)


def scratches(raw, weights, width):
    blocks, _, frames, flat, chans = raw.shape
    size = blocks * flat
    places = frames * size
    return [
        pltpu.VMEM((places + 2 * size, 9 * chans), jnp.bfloat16),
        *held(weights),
        pltpu.VMEM((places + 2 * size, chans), jnp.bfloat16),
        pltpu.VMEM((places, -(-9 * width // 128) * 128), jnp.bfloat16),
        pltpu.VMEM((27 * width, chans), jnp.float32),
    ]


def first_part(place, raw, weights, gains, shifts, width, clips):
    blocks, _, frames, flat, chans = raw.shape
    places = blocks * frames * flat
    shape = jax.ShapeDtypeStruct((places, chans), jnp.bfloat16)
    outs = [shape, shape, shape, jax.ShapeDtypeStruct((clips, width, chans), jnp.bfloat16)]
    args = (place, raw, weights, gains, shifts)
    specs = [small(), None, away(), None, None]
    return called(first_kernel, outs, scratches(raw, weights, width), args, specs, places * weights.size, 58)


def second_part(place, raw, turned, h_one, a_one, gains, shifts, width, clips):
    blocks, _, frames, flat, chans = raw.shape
    size = blocks * flat
    places = frames * size
    outs = [
        jax.ShapeDtypeStruct((blocks, flat, chans), jnp.float32),
        jax.ShapeDtypeStruct((clips, width, chans), jnp.bfloat16),
    ]
    scratch = scratches(raw, turned, width) + [
        *held(turned),
        pltpu.VMEM((places, chans), jnp.float32),
        pltpu.VMEM((size, chans), jnp.float32),
        pltpu.VMEM((places, chans), jnp.bfloat16),
        pltpu.VMEM((2, 8, chans), jnp.float32),
        pltpu.VMEM((32, chans), jnp.float32),
    ]
    args = (place, raw, turned, h_one, a_one, gains, shifts)
    specs = [small(), None, away(), None, None, None, None]
    return called(second_kernel, outs, scratch, args, specs, places * turned.size, 58)


def gathered(later, earlier, grads, clips):
    parts, flat, chans = grads.shape
    outs = [jax.ShapeDtypeStruct((parts, 2 * later.shape[0] + flat, chans), jnp.float32)]
    return called(functools.partial(sum_kernel, clips=clips), outs, [], (later, earlier, grads))[0]


def turn(weights):
    layers, depth, chans = weights.shape
    block = pl.BlockSpec((1, depth // 9, chans), lambda k, n: (k, n, 0))
    return pl.pallas_call(
        turn_kernel,
        grid=(layers, 9),
        out_shape=jax.ShapeDtypeStruct(weights.shape, weights.dtype),
        in_specs=[block],
        out_specs=block,
        cost_estimate=pl.CostEstimate(flops=0, bytes_accessed=4 * weights.size, transcendentals=0),
    )(weights)


def decode(place, a_two, weights, latent):
    frames, flat, chans = latent.shape
    size = a_two.shape[0] // frames
    pitch = -(-flat // 16) * 16
    outs = [jax.ShapeDtypeStruct(latent.shape, jnp.bfloat16)]
    scratch = [
        pltpu.VMEM((size // 8 + 2, 8, chans), jnp.float32),
        pltpu.VMEM(((frames + 2) * pitch, 9 * chans), jnp.bfloat16),
    ] + held(weights)
    args = (place, a_two, weights, latent)
    return called(decode_kernel, outs, scratch, args, [small(), None, away(), None], frames * pitch * weights.size, 58)[0]


def spread(value, axis):
    return lax.all_to_all(jnp.broadcast_to(value[None], (lax.axis_size(axis),) + value.shape), axis, 0, 0)


def per_device(latents, cotangent, conv_weights, gains, shifts, moment, second):
    frames, rows, cols, chans = latents.shape[1:]
    clips, parts = lax.axis_size("dp"), lax.axis_size("space")
    me = lax.axis_index("space")
    place = me.astype(jnp.int32).reshape(1)
    width = chans // parts
    f32, bf16 = jnp.float32, jnp.bfloat16
    latent = latents[0].reshape(frames, rows * cols, chans)
    both = jnp.stack([latent, cotangent[0].reshape(latent.shape)])
    raw, turned = lax.optimization_barrier((spread(both, "space"), turn(conv_weights)))

    a_one, h_one, a_two, later = first_part(place, raw, conv_weights, gains, shifts, width, clips)
    later = lax.all_to_all(later, "dp", 0, 0)
    grads, earlier = second_part(place, raw, turned, h_one, a_one, gains, shifts, width, clips)
    earlier = lax.all_to_all(earlier, "dp", 0, 0)
    decoded = decode(place, a_two, conv_weights, latent)

    later = jnp.sum(later.astype(f32), 0) / clips
    every = gathered(later, earlier, grads, clips)
    every = lax.all_to_all(every, "space", 0, 0)
    shape = jax.ShapeDtypeStruct(moment.shape, f32)
    outs = [shape, shape, shape, jax.ShapeDtypeStruct((4, chans), f32)]
    outs.append(jax.ShapeDtypeStruct((frames, rows * cols, chans), bf16))
    outs = called(adam_kernel, outs, [], (every, moment, second))
    new_moment, new_second, direction, vector, grad_input = outs
    grad_input = grad_input.reshape(latents.shape)
    return (decoded.reshape(latents.shape), grad_input, new_moment, new_second, direction, vector)


def solution(mesh):
    placed = (
        P("dp", None, "space", None, None),
        P("dp", None, "space", None, None),
        P(),
        P(),
        P(),
        P(None, "dp", None),
        P(None, "dp", None),
    )
    return jax.shard_map(
        per_device,
        mesh=mesh,
        in_specs=placed,
        out_specs=(
            P("dp", None, "space", None, None),
            P("dp", None, "space", None, None),
            P(None, "dp", None),
            P(None, "dp", None),
            P(None, "dp", None),
            P(),
        ),
        check_vma=False,
    )
```

```python
import functools
import math

import jax
import jax.numpy as jnp
from jax import lax
from jax.experimental import pallas as pl
from jax.experimental.pallas import tpu as pltpu
from jax.sharding import Mesh
from jax.sharding import PartitionSpec as P

GROUPS = 32
STEP = 4


bias_first = 1.0 - math.exp(100.0 * math.log(0.9))
bias_second = 1.0 - math.exp(100.0 * math.log(0.999))


def rolled(value, amount, axis):
    return pltpu.roll(value, amount % value.shape[axis], axis)


def all_cols(value):
    total = jnp.sum(value, 0)
    for step in (4, 2, 1):
        total = total + rolled(total, step, 0)
    return total


def group_all(sums):
    size = sums.shape[1] // GROUPS
    lane = lax.broadcasted_iota(jnp.int32, sums.shape, 1)
    step = 1
    while step < size:
        partner = jnp.where((lane & step) == 0, rolled(sums, -step, 1), rolled(sums, step, 1))
        sums = sums + partner
        step *= 2
    return sums


def norm_parts(values):
    count = values.shape[0] * values.shape[1] * (values.shape[2] // GROUPS)
    mean = group_all(all_cols(values)) / count
    var = group_all(all_cols(values * values)) / count - mean * mean
    return mean, lax.rsqrt(var + 1e-05)


def col_shifted(value, step):
    if step == 0:
        return value
    col = lax.broadcasted_iota(jnp.int32, value.shape, 1)
    edge = value.shape[1] - 1 if step > 0 else 0
    return jnp.where(col == edge, 0.0, rolled(value, -step, 1))


def row_shifted(value, step):
    if step == 0:
        return value
    zero = jnp.zeros_like(value[:1])
    if step > 0:
        return jnp.concatenate([value[1:], zero], 0)
    return jnp.concatenate([zero, value[:-1]], 0)


def store_nine(target, frame, value, sign):
    rows, cols, chans = value.shape
    size = rows * cols
    for w in range(3):
        moved = col_shifted(value, sign * (w - 1))
        for h in range(3):
            view = row_shifted(moved, sign * (h - 1)).reshape(size, chans)
            number = 3 * h + w
            target[pl.ds(pl.multiple_of(frame * size, 16), size), number * chans : (number + 1) * chans] = view.astype(jnp.bfloat16)


def load_frame(raw, frame):
    blocks, _, flat, chans = raw.shape
    parts = [raw[b, frame].astype(jnp.float32).reshape(flat // 8, 8, chans) for b in range(blocks)]
    return jnp.concatenate(parts, 0)


def frame_of(flat, frame, size):
    part = flat[pl.ds(pl.multiple_of(frame * size, 16), size), :]
    return part.astype(jnp.float32).reshape(size // 8, 8, part.shape[-1])


def put_frame(flat, frame, value):
    size = value.shape[0] * value.shape[1]
    flat[pl.ds(pl.multiple_of(frame * size, 16), size), :] = value.reshape(size, -1).astype(flat.dtype)


def ahead_part(raw, gains, shifts, a_one, h_one, a_two, nine, weight, copy):
    frames, chans = raw.shape[1], raw.shape[3]
    size = raw.shape[0] * raw.shape[2]
    depth = 9 * chans

    @pl.loop(0, frames, unroll=frames)
    def _(t):
        value = load_frame(raw, t)
        mean, factor = norm_parts(value)
        u = (value - mean) * factor * gains[0:1, :] + shifts[0:1, :]
        act = (u * jax.nn.sigmoid(u)).astype(jnp.bfloat16).astype(jnp.float32)
        put_frame(a_one, t, act)
        store_nine(nine, t + 2, act, 1)

    nine[0:size, :] = nine[2 * size : 3 * size, :]
    nine[size : 2 * size, :] = nine[2 * size : 3 * size, :]
    copy.wait()

    @pl.loop(0, frames // STEP, unroll=frames // STEP)
    def _(b):
        total = None
        for t in range(3):
            left = nine[pl.ds(pl.multiple_of((b * STEP + t) * size, 16), STEP * size), :]
            part = jnp.dot(left, weight[t * depth : (t + 1) * depth, :], preferred_element_type=jnp.float32)
            total = part if total is None else total + part
        h_one[pl.ds(pl.multiple_of(b * STEP * size, 16), STEP * size), :] = total.astype(jnp.bfloat16)

    @pl.loop(0, frames, unroll=frames)
    def _(t):
        value = frame_of(h_one, t, size)
        mean, factor = norm_parts(value)
        u = (value - mean) * factor * gains[1:2, :] + shifts[1:2, :]
        put_frame(a_two, t, u * jax.nn.sigmoid(u))


def back_part(raw, h_one, gains, shifts, d_h1, vectors, nine, d_act, weight, copy):
    frames, chans = raw.shape[1], raw.shape[3]
    size = raw.shape[0] * raw.shape[2]
    depth = 9 * chans

    @pl.loop(0, frames, unroll=frames)
    def _(t):
        store_nine(nine, t, load_frame(raw, t), -1)

    nine[frames * size :, :] = jnp.zeros((2 * size, depth), jnp.bfloat16)
    copy.wait()

    @pl.loop(0, frames // STEP, unroll=frames // STEP)
    def _(b):
        total = None
        for t in range(3):
            left = nine[pl.ds(pl.multiple_of((b * STEP + 2 - t) * size, 16), STEP * size), :]
            part = jnp.dot(left, weight[t * depth : (t + 1) * depth, :], preferred_element_type=jnp.float32)
            total = part if total is None else total + part
        d_act[pl.ds(pl.multiple_of(b * STEP * size, 16), STEP * size), :] = total

    pair = jnp.dot(nine[0:size, :], weight[depth : 2 * depth, :], preferred_element_type=jnp.float32)
    both = jnp.dot(nine[0 : 2 * size, :], weight[0:depth, :], preferred_element_type=jnp.float32)
    d_act[0:size, :] = d_act[0:size, :] + (pair + (both[:size] + both[size:]))

    vectors[...] = jnp.zeros_like(vectors)
    count = size * (chans // GROUPS)

    @pl.loop(0, frames, unroll=frames)
    def _(t):
        value = frame_of(h_one, t, size)
        mean, factor = norm_parts(value)
        normed = (value - mean) * factor
        u = normed * gains[1:2, :] + shifts[1:2, :]
        sig = jax.nn.sigmoid(u)
        d_out = frame_of(d_act, t, size) * (sig * (1.0 + u * (1.0 - sig)))
        d_shift = all_cols(d_out)
        d_gain = all_cols(d_out * normed)
        vectors[0] += d_gain
        vectors[1] += d_shift
        one = group_all(d_shift * gains[1:2, :]) / count
        two = group_all(d_gain * gains[1:2, :]) / count
        put_frame(d_h1, t, factor * (d_out * gains[1:2, :] - one - normed * two))


def grad_part(place, values, grads, extra, out, part_number, long, block, total):
    frames_size, chans = values.shape
    cores, pairs, _, _ = out.shape
    owners = cores * pairs
    size, outs = (long.shape[0] - frames_size) // 2, total.shape[0] // 27
    frames = frames_size // size
    long[0:size, :] = values[0:size, :]
    long[size : 2 * size, :] = values[0:size, :]
    long[2 * size :, :] = values[...]
    lanes = block.shape[1]
    chan = lax.broadcasted_iota(jnp.int32, (chans, lanes), 0)
    lane = lax.broadcasted_iota(jnp.int32, (chans, lanes), 1)
    pick = (chan == place[0] * outs + lane % outs).astype(jnp.bfloat16)

    @pl.loop(0, frames, unroll=frames)
    def _(t):
        if len(grads.shape) == 4:
            rows = load_frame(grads, t).reshape(size, chans).astype(jnp.bfloat16)
        else:
            rows = grads[pl.ds(pl.multiple_of(t * size, 16), size), :]
        spread_out = jnp.dot(rows, pick, preferred_element_type=jnp.float32).reshape(size // 8, 8, lanes)
        for piece in range(lanes // 128):
            value = spread_out[:, :, piece * 128 : (piece + 1) * 128]
            lane = lax.broadcasted_iota(jnp.int32, value.shape, 2)
            kept = jnp.zeros_like(value)
            for place_in in range(128 // outs):
                number = piece * (128 // outs) + place_in
                if number < 9:
                    h, w = divmod(number, 3)
                    moved = row_shifted(col_shifted(value, 1 - w), 1 - h)
                    kept = jnp.where(lane // outs == place_in, moved, kept)
            block[pl.ds(pl.multiple_of(t * size, 16), size), piece * 128 : (piece + 1) * 128] = kept.reshape(size, 128).astype(jnp.bfloat16)

    side = block[...].T
    for t in range(3):
        part = jnp.dot(side, long[t * size : (t + frames) * size, :], preferred_element_type=jnp.float32)
        total[t * 9 * outs : (t + 1) * 9 * outs, :] = part[: 9 * outs]

    owned = 27 * chans // owners
    lane = lax.broadcasted_iota(jnp.int32, (outs, chans), 1)
    for d in range(owners):
        tap, start = divmod(d * owned, chans)
        one = total[tap * outs : (tap + 1) * outs, :]
        if start + owned > chans:
            one = jnp.concatenate([one, total[(tap + 1) * outs : (tap + 2) * outs, :]], 1)
        one = rolled(one, -start, 1)[:, :chans]
        if extra is not None:
            one = jnp.where(lane < owned, one, extra[...])
        out[d % cores, d // cores, part_number * outs : (part_number + 1) * outs, :] = one.astype(jnp.bfloat16)


def halves(value):
    high = value.astype(jnp.bfloat16).astype(jnp.float32)
    return high, value - high


def to_spare(value, start, width):
    chans = value.shape[1]
    row = lax.broadcasted_iota(jnp.int32, value.shape, 0)
    lane = lax.broadcasted_iota(jnp.int32, value.shape, 1)
    held = (lane >= start) & (lane < start + width)
    tiles = []
    for tile in range(chans // width // 8):
        kept = jnp.zeros_like(value)
        for r in range(8):
            moved = rolled(value, start - width * (8 * tile + r), 1)
            kept = jnp.where((row == r) & held, moved, kept)
        tiles.append(kept)
    return jnp.concatenate(tiles, 0)


def from_spare(value, start, width):
    rows, chans = value.shape
    row = lax.broadcasted_iota(jnp.int32, (8, chans), 0)
    lane = lax.broadcasted_iota(jnp.int32, (8, chans), 1)
    kept = jnp.zeros((8, chans), jnp.float32)
    for r in range(rows):
        tile = value[8 * (r // 8) : 8 * (r // 8) + 8, :]
        moved = rolled(tile, width * r - start, 1)
        kept = kept + jnp.where((row == r % 8) & (lane // width == r), moved, 0.0)
    for step in (4, 2, 1):
        kept = kept + rolled(kept, step, 0)
    return kept


def own_part(place, d_h1, raw_lat, raw_cot, gains, shifts, sums_two, grad, extra, nine, d_act, weight, copy):
    blocks, frames, flat, chans = raw_lat.shape
    size = blocks * flat
    depth = 9 * chans
    me = place[0]
    for ahead_by in range(3):
        value = frame_of(d_h1, jnp.minimum(me + ahead_by, frames - 1), size)
        if ahead_by:
            value = jnp.where(me + ahead_by < frames, value, 0.0)
        store_nine(nine, ahead_by, value, -1)
    copy.wait()

    def term(frame, tap):
        left = nine[frame * size : (frame + 1) * size, :]
        return jnp.dot(left, weight[tap * depth : (tap + 1) * depth, :], preferred_element_type=jnp.float32)

    d_act[...] = term(2, 0) + term(1, 1) + term(0, 2)

    @pl.when(me == 0)
    def _():
        d_act[...] = d_act[...] + (term(0, 1) + (term(0, 0) + term(1, 0)))

    count = size * (chans // GROUPS)
    value = load_frame(raw_lat, me)
    mean, factor = norm_parts(value)
    normed = (value - mean) * factor
    u = normed * gains[0:1, :] + shifts[0:1, :]
    sig = jax.nn.sigmoid(u)
    d_out = d_act[...].reshape(size // 8, 8, chans) * (sig * (1.0 + u * (1.0 - sig)))
    d_shift = all_cols(d_out)
    d_gain = all_cols(d_out * normed)
    one = group_all(d_shift * gains[0:1, :]) / count
    two = group_all(d_gain * gains[0:1, :]) / count
    d_in = factor * (d_out * gains[0:1, :] - one - normed * two)
    result = (load_frame(raw_cot, me) + d_in).astype(jnp.bfloat16).astype(jnp.float32)
    grad[...] = result.reshape(blocks, flat, chans)

    owned = chans - 40
    pieces = [to_spare(part, owned, 32) for part in (*halves(d_gain), *halves(d_shift))]
    gain_high, gain_low = halves(sums_two[0])
    shift_high, shift_low = halves(sums_two[1])
    turn = me % 4
    mine = jnp.where(turn < 2, jnp.where(turn == 0, gain_high, gain_low), jnp.where(turn == 2, shift_high, shift_low))
    extra[...] = jnp.concatenate(pieces, 0) + to_spare(0.5 * mine, owned + 32, 8)


def whole_kernel(place, raw, weights, turned, gains, shifts, a_two, grad, out, nine, straight, back_one, back_two, sems, a_one, h_one, d_h1, d_act, own_act, sums_two, extra, long, block, total):
    raw_lat, raw_cot = raw.at[:, 0], raw.at[:, 1]
    copies = [
        pltpu.make_async_copy(weights.at[0], straight, sems.at[0]),
        pltpu.make_async_copy(turned.at[1], back_two, sems.at[1]),
        pltpu.make_async_copy(turned.at[0], back_one, sems.at[2]),
    ]
    for copy in copies:
        copy.start()
    ahead_part(raw_lat, gains, shifts, a_one, h_one, a_two, nine, straight, copies[0])
    grad_part(place, a_two, raw_cot, None, out, 0, long, block, total)
    back_part(raw_cot, h_one, gains, shifts, d_h1, sums_two, nine, d_act, back_two, copies[1])
    own_part(place, d_h1, raw_lat, raw_cot, gains, shifts, sums_two, grad, extra, nine, own_act, back_one, copies[2])
    grad_part(place, a_one, d_h1, extra, out, 1, long, block, total)


def sum_kernel(pieces, grad, out, *, clips):
    total = pieces[0].astype(jnp.float32)
    for d in range(1, pieces.shape[0]):
        total = total + pieces[d].astype(jnp.float32)
    total = total / clips
    rows = total.shape[0]
    for p in range(out.shape[0]):
        out[p, 0:rows, :] = total
        out[p, rows:, :] = grad[p]


def adam_kernel(every, moment, second, new_moment, new_second, direction, vector, grad_input):
    parts, tall, chans = every.shape
    owned = moment.shape[1]
    width = chans // parts
    for layer in range(2):
        start = width * (1 - layer)
        grad = every[:, start : start + width, :].reshape(chans, chans).T[:owned, :]
        new_m = 0.9 * moment[layer] + 0.1 * grad
        new_v = 0.999 * second[layer] + 0.001 * grad * grad
        new_moment[layer] = new_m
        new_second[layer] = new_v
        direction[layer] = new_m / bias_first / (jnp.sqrt(new_v / bias_second) + 1e-08)
    for p in range(parts):
        grad_input[p] = every[p, 2 * width :, :].astype(jnp.bfloat16)
    held = [every[p, width : 2 * width, :] for p in range(parts)]
    summed = held[0]
    for p in range(1, parts):
        summed = summed + held[p]
    for row in range(2):
        high = from_spare(summed[16 * row : 16 * row + 8], owned, 32)
        low = from_spare(summed[16 * row + 8 : 16 * row + 16], owned, 32)
        vector[row : row + 1, :] = (high + low)[0:1]
        mine = sum(held[p] for p in range(parts) if p % 4 in (2 * row, 2 * row + 1))
        vector[2 + row : 3 + row, :] = from_spare(mine, owned + 32, 8)[0:1]


def turn_kernel(weights, turned):
    chans = weights.shape[2]
    for tap in range(weights.shape[1] // chans):
        rows = slice(tap * chans, (tap + 1) * chans)
        turned[0, rows, :] = weights[0, rows, :].T


def decode_kernel(place, a_two, weights, latent, decoded, tall, nine, weight, sem):
    copy = pltpu.make_async_copy(weights.at[1], weight, sem)
    copy.start()
    frames, flat, chans = latent.shape
    size = a_two.shape[0] // frames
    rows, every = flat // 8, size // 8
    pitch = nine.shape[0] // (frames + 2)
    depth = 9 * chans
    tall[0] = jnp.zeros(tall.shape[1:], jnp.float32)
    tall[every + 1] = jnp.zeros(tall.shape[1:], jnp.float32)
    rest = jnp.zeros((pitch // 8 - rows, 8, chans), jnp.float32)
    for t in range(frames):
        tall[1 : every + 1] = frame_of(a_two, t, size)
        part = tall[pl.ds(place[0] * rows, rows + 2)]
        for w in range(3):
            moved = col_shifted(part, w - 1)
            for h in range(3):
                view = jnp.concatenate([moved[h : h + rows], rest], 0).reshape(pitch, chans)
                number = 3 * h + w
                nine[(t + 2) * pitch : (t + 3) * pitch, number * chans : (number + 1) * chans] = view.astype(jnp.bfloat16)
    nine[0:pitch, :] = nine[2 * pitch : 3 * pitch, :]
    nine[pitch : 2 * pitch, :] = nine[2 * pitch : 3 * pitch, :]
    copy.wait()
    total = None
    for t in range(3):
        left = nine[t * pitch : (t + frames) * pitch, :]
        part = jnp.dot(left, weight[t * depth : (t + 1) * depth, :], preferred_element_type=jnp.float32)
        total = part if total is None else total + part
    for t in range(frames):
        value = latent[t].astype(jnp.float32) + total[t * pitch : t * pitch + flat, :]
        decoded[t] = value.astype(jnp.bfloat16)


def called(kernel, outs, scratch, args, specs=None, flops=0, limit=16):
    whole = pl.BlockSpec(memory_space=pltpu.VMEM)
    specs = specs or [whole] * len(args)
    moved = sum(math.prod(a.shape) * a.dtype.itemsize for a in (*args, *outs))
    return pl.pallas_call(
        kernel,
        out_shape=outs,
        in_specs=[whole if spec is None else spec for spec in specs],
        out_specs=[whole] * len(outs),
        scratch_shapes=scratch,
        compiler_params=pltpu.CompilerParams(vmem_limit_bytes=limit * 2**20),
        cost_estimate=pl.CostEstimate(flops=flops, bytes_accessed=moved, transcendentals=0),
    )(*args)


def held(weights):
    return [pltpu.VMEM(weights.shape[1:], weights.dtype), pltpu.SemaphoreType.DMA]


def small():
    return pl.BlockSpec(memory_space=pltpu.SMEM)


def away():
    return pl.BlockSpec(memory_space=pl.ANY)


def whole(place, raw, weights, turned, gains, shifts, width, clips, cores):
    blocks, _, frames, flat, chans = raw.shape
    size = blocks * flat
    places = frames * size
    f32, bf16 = jnp.float32, jnp.bfloat16
    outs = [
        jax.ShapeDtypeStruct((places, chans), bf16),
        jax.ShapeDtypeStruct((blocks, flat, chans), f32),
        jax.ShapeDtypeStruct((cores, clips // cores, 2 * width, chans), bf16),
    ]
    layer = pltpu.VMEM(weights.shape[1:], bf16)
    scratch = [
        pltpu.VMEM((places + 2 * size, 9 * chans), bf16),
        layer,
        layer,
        layer,
        pltpu.SemaphoreType.DMA((3,)),
        pltpu.VMEM((places, chans), bf16),
        pltpu.VMEM((places, chans), bf16),
        pltpu.VMEM((places, chans), bf16),
        pltpu.VMEM((places, chans), f32),
        pltpu.VMEM((size, chans), f32),
        pltpu.VMEM((2, 8, chans), f32),
        pltpu.VMEM((32, chans), f32),
        pltpu.VMEM((places + 2 * size, chans), bf16),
        pltpu.VMEM((places, -(-9 * width // 128) * 128), bf16),
        pltpu.VMEM((27 * width, chans), f32),
    ]
    args = (place, raw, weights, turned, gains, shifts)
    specs = [small(), None, away(), away(), None, None]
    return called(whole_kernel, outs, scratch, args, specs, 2 * places * weights.size, 58)


def gathered(pieces, grads, clips):
    parts, flat, chans = grads.shape
    outs = [jax.ShapeDtypeStruct((parts, pieces.shape[1] + flat, chans), jnp.float32)]
    return called(functools.partial(sum_kernel, clips=clips), outs, [], (pieces, grads))[0]


def turn(weights):
    layers, depth, chans = weights.shape
    block = pl.BlockSpec((1, depth // 9, chans), lambda k, n: (k, n, 0))
    return pl.pallas_call(
        turn_kernel,
        grid=(layers, 9),
        out_shape=jax.ShapeDtypeStruct(weights.shape, weights.dtype),
        in_specs=[block],
        out_specs=block,
        cost_estimate=pl.CostEstimate(flops=0, bytes_accessed=4 * weights.size, transcendentals=0),
    )(weights)


def decode(place, a_two, weights, latent):
    frames, flat, chans = latent.shape
    size = a_two.shape[0] // frames
    pitch = -(-flat // 16) * 16
    outs = [jax.ShapeDtypeStruct(latent.shape, jnp.bfloat16)]
    scratch = [
        pltpu.VMEM((size // 8 + 2, 8, chans), jnp.float32),
        pltpu.VMEM(((frames + 2) * pitch, 9 * chans), jnp.bfloat16),
    ] + held(weights)
    args = (place, a_two, weights, latent)
    return called(decode_kernel, outs, scratch, args, [small(), None, away(), None], frames * pitch * weights.size, 58)[0]


def spread(value, axis):
    return lax.all_to_all(jnp.broadcast_to(value[None], (lax.axis_size(axis),) + value.shape), axis, 0, 0)


def per_device(latents, cotangent, conv_weights, gains, shifts, moment, second):
    frames, rows, cols, chans = latents.shape[1:]
    cores, parts = lax.axis_size("core"), lax.axis_size("space")
    clips = lax.axis_size("pair") * cores
    me = lax.axis_index("space")
    place = me.astype(jnp.int32).reshape(1)
    width = chans // parts
    f32, bf16 = jnp.float32, jnp.bfloat16
    latent = latents[0].reshape(frames, rows * cols, chans)
    both = jnp.stack([latent, cotangent[0].reshape(latent.shape)])
    raw, turned = lax.optimization_barrier((spread(both, "space"), turn(conv_weights)))

    a_two, grads, pieces = whole(place, raw, conv_weights, turned, gains, shifts, width, clips, cores)
    pieces = lax.all_to_all(pieces, "core", 0, 0)
    pieces = jnp.sum(pieces.astype(f32), 0).astype(bf16)
    pieces = lax.all_to_all(pieces, "pair", 0, 0)
    decoded = decode(place, a_two, conv_weights, latent)

    every = gathered(pieces, grads, clips)
    every = lax.all_to_all(every, "space", 0, 0)
    shape = jax.ShapeDtypeStruct(moment.shape, f32)
    outs = [shape, shape, shape, jax.ShapeDtypeStruct((4, chans), f32)]
    outs.append(jax.ShapeDtypeStruct((frames, rows * cols, chans), bf16))
    outs = called(adam_kernel, outs, [], (every, moment, second))
    new_moment, new_second, direction, vector, grad_input = outs
    grad_input = grad_input.reshape(latents.shape)
    return (decoded.reshape(latents.shape), grad_input, new_moment, new_second, direction, vector)


def solution(mesh):
    clips, parts = mesh.devices.shape
    mesh = Mesh(mesh.devices.reshape(clips // 2, 2, parts), ("pair", "core", "space"))
    dp = ("pair", "core")
    placed = (
        P(dp, None, "space", None, None),
        P(dp, None, "space", None, None),
        P(),
        P(),
        P(),
        P(None, dp, None),
        P(None, dp, None),
    )
    return jax.shard_map(
        per_device,
        mesh=mesh,
        in_specs=placed,
        out_specs=(
            P(dp, None, "space", None, None),
            P(dp, None, "space", None, None),
            P(None, dp, None),
            P(None, dp, None),
            P(None, dp, None),
            P(),
        ),
        check_vma=False,
    )
```

```python
import functools
import math

import jax
import jax.numpy as jnp
from jax import lax
from jax.experimental import pallas as pl
from jax.experimental.pallas import tpu as pltpu
from jax.sharding import Mesh
from jax.sharding import PartitionSpec as P

GROUPS = 32
STEP = 4


bias_first = 1.0 - math.exp(100.0 * math.log(0.9))
bias_second = 1.0 - math.exp(100.0 * math.log(0.999))


def rolled(value, amount, axis):
    return pltpu.roll(value, amount % value.shape[axis], axis)


def all_cols(value):
    total = jnp.sum(value, 0)
    for step in (4, 2, 1):
        total = total + rolled(total, step, 0)
    return total


def group_all(sums):
    size = sums.shape[1] // GROUPS
    lane = lax.broadcasted_iota(jnp.int32, sums.shape, 1)
    step = 1
    while step < size:
        partner = jnp.where((lane & step) == 0, rolled(sums, -step, 1), rolled(sums, step, 1))
        sums = sums + partner
        step *= 2
    return sums


def norm_parts(values):
    count = values.shape[0] * values.shape[1] * (values.shape[2] // GROUPS)
    mean = group_all(all_cols(values)) / count
    var = group_all(all_cols(values * values)) / count - mean * mean
    return mean, lax.rsqrt(var + 1e-05)


def col_shifted(value, step):
    if step == 0:
        return value
    col = lax.broadcasted_iota(jnp.int32, value.shape, 1)
    edge = value.shape[1] - 1 if step > 0 else 0
    return jnp.where(col == edge, 0.0, rolled(value, -step, 1))


def row_shifted(value, step):
    if step == 0:
        return value
    zero = jnp.zeros_like(value[:1])
    if step > 0:
        return jnp.concatenate([value[1:], zero], 0)
    return jnp.concatenate([zero, value[:-1]], 0)


def store_nine(target, frame, value, sign):
    rows, cols, chans = value.shape
    size = rows * cols
    for w in range(3):
        moved = col_shifted(value, sign * (w - 1))
        for h in range(3):
            view = row_shifted(moved, sign * (h - 1)).reshape(size, chans)
            number = 3 * h + w
            target[pl.ds(pl.multiple_of(frame * size, 16), size), number * chans : (number + 1) * chans] = view.astype(jnp.bfloat16)


def load_frame(raw, frame):
    blocks, _, flat, chans = raw.shape
    parts = [raw[b, frame].astype(jnp.float32).reshape(flat // 8, 8, chans) for b in range(blocks)]
    return jnp.concatenate(parts, 0)


def frame_of(flat, frame, size):
    part = flat[pl.ds(pl.multiple_of(frame * size, 16), size), :]
    return part.astype(jnp.float32).reshape(size // 8, 8, part.shape[-1])


def put_frame(flat, frame, value):
    size = value.shape[0] * value.shape[1]
    flat[pl.ds(pl.multiple_of(frame * size, 16), size), :] = value.reshape(size, -1).astype(flat.dtype)


def ahead_part(raw, gains, shifts, a_one, h_one, a_two, nine, weight, copy):
    frames, chans = raw.shape[1], raw.shape[3]
    size = raw.shape[0] * raw.shape[2]
    depth = 9 * chans

    @pl.loop(0, frames, unroll=frames)
    def _(t):
        value = load_frame(raw, t)
        mean, factor = norm_parts(value)
        u = (value - mean) * factor * gains[0:1, :] + shifts[0:1, :]
        act = (u * jax.nn.sigmoid(u)).astype(jnp.bfloat16).astype(jnp.float32)
        put_frame(a_one, t, act)
        store_nine(nine, t + 2, act, 1)

    nine[0:size, :] = nine[2 * size : 3 * size, :]
    nine[size : 2 * size, :] = nine[2 * size : 3 * size, :]
    copy.wait()

    @pl.loop(0, frames // STEP, unroll=frames // STEP)
    def _(b):
        total = None
        for t in range(3):
            left = nine[pl.ds(pl.multiple_of((b * STEP + t) * size, 16), STEP * size), :]
            part = jnp.dot(left, weight[t * depth : (t + 1) * depth, :], preferred_element_type=jnp.float32)
            total = part if total is None else total + part
        h_one[pl.ds(pl.multiple_of(b * STEP * size, 16), STEP * size), :] = total.astype(jnp.bfloat16)

    @pl.loop(0, frames, unroll=frames)
    def _(t):
        value = frame_of(h_one, t, size)
        mean, factor = norm_parts(value)
        u = (value - mean) * factor * gains[1:2, :] + shifts[1:2, :]
        put_frame(a_two, t, u * jax.nn.sigmoid(u))


def back_part(raw, h_one, gains, shifts, d_h1, vectors, nine, d_act, weight, copy):
    frames, chans = raw.shape[1], raw.shape[3]
    size = raw.shape[0] * raw.shape[2]
    depth = 9 * chans

    @pl.loop(0, frames, unroll=frames)
    def _(t):
        store_nine(nine, t, load_frame(raw, t), -1)

    nine[frames * size :, :] = jnp.zeros((2 * size, depth), jnp.bfloat16)
    copy.wait()

    @pl.loop(0, frames // STEP, unroll=frames // STEP)
    def _(b):
        total = None
        for t in range(3):
            left = nine[pl.ds(pl.multiple_of((b * STEP + 2 - t) * size, 16), STEP * size), :]
            part = jnp.dot(left, weight[t * depth : (t + 1) * depth, :], preferred_element_type=jnp.float32)
            total = part if total is None else total + part
        d_act[pl.ds(pl.multiple_of(b * STEP * size, 16), STEP * size), :] = total

    pair = jnp.dot(nine[0:size, :], weight[depth : 2 * depth, :], preferred_element_type=jnp.float32)
    both = jnp.dot(nine[0 : 2 * size, :], weight[0:depth, :], preferred_element_type=jnp.float32)
    d_act[0:size, :] = d_act[0:size, :] + (pair + (both[:size] + both[size:]))

    vectors[...] = jnp.zeros_like(vectors)
    count = size * (chans // GROUPS)

    @pl.loop(0, frames, unroll=frames)
    def _(t):
        value = frame_of(h_one, t, size)
        mean, factor = norm_parts(value)
        normed = (value - mean) * factor
        u = normed * gains[1:2, :] + shifts[1:2, :]
        sig = jax.nn.sigmoid(u)
        d_out = frame_of(d_act, t, size) * (sig * (1.0 + u * (1.0 - sig)))
        d_shift = all_cols(d_out)
        d_gain = all_cols(d_out * normed)
        vectors[0] += d_gain
        vectors[1] += d_shift
        one = group_all(d_shift * gains[1:2, :]) / count
        two = group_all(d_gain * gains[1:2, :]) / count
        put_frame(d_h1, t, factor * (d_out * gains[1:2, :] - one - normed * two))


def grad_part(place, values, grads, extra, out, part_number, long, block, total):
    frames_size, chans = values.shape
    cores, pairs, _, _ = out.shape
    owners = cores * pairs
    size, outs = (long.shape[0] - frames_size) // 2, total.shape[0] // 27
    frames = frames_size // size
    long[0:size, :] = values[0:size, :]
    long[size : 2 * size, :] = values[0:size, :]
    long[2 * size :, :] = values[...]
    lanes = block.shape[1]
    chan = lax.broadcasted_iota(jnp.int32, (chans, lanes), 0)
    lane = lax.broadcasted_iota(jnp.int32, (chans, lanes), 1)
    pick = (chan == place[0] * outs + lane % outs).astype(jnp.bfloat16)

    @pl.loop(0, frames, unroll=frames)
    def _(t):
        if len(grads.shape) == 4:
            rows = load_frame(grads, t).reshape(size, chans).astype(jnp.bfloat16)
        else:
            rows = grads[pl.ds(pl.multiple_of(t * size, 16), size), :]
        spread_out = jnp.dot(rows, pick, preferred_element_type=jnp.float32).reshape(size // 8, 8, lanes)
        for piece in range(lanes // 128):
            value = spread_out[:, :, piece * 128 : (piece + 1) * 128]
            lane = lax.broadcasted_iota(jnp.int32, value.shape, 2)
            kept = jnp.zeros_like(value)
            for place_in in range(128 // outs):
                number = piece * (128 // outs) + place_in
                if number < 9:
                    h, w = divmod(number, 3)
                    moved = row_shifted(col_shifted(value, 1 - w), 1 - h)
                    kept = jnp.where(lane // outs == place_in, moved, kept)
            block[pl.ds(pl.multiple_of(t * size, 16), size), piece * 128 : (piece + 1) * 128] = kept.reshape(size, 128).astype(jnp.bfloat16)

    side = block[...].T
    for t in range(3):
        part = jnp.dot(side, long[t * size : (t + frames) * size, :], preferred_element_type=jnp.float32)
        total[t * 9 * outs : (t + 1) * 9 * outs, :] = part[: 9 * outs]

    owned = 27 * chans // owners
    lane = lax.broadcasted_iota(jnp.int32, (outs, chans), 1)
    for d in range(owners):
        tap, start = divmod(d * owned, chans)
        one = total[tap * outs : (tap + 1) * outs, :]
        if start + owned > chans:
            one = jnp.concatenate([one, total[(tap + 1) * outs : (tap + 2) * outs, :]], 1)
        one = rolled(one, -start, 1)[:, :chans]
        if extra is not None:
            one = jnp.where(lane < owned, one, extra[...])
        out[d % cores, d // cores, part_number * outs : (part_number + 1) * outs, :] = one.astype(jnp.bfloat16)


def halves(value):
    high = value.astype(jnp.bfloat16).astype(jnp.float32)
    return high, value - high


def to_spare(value, start, width):
    chans = value.shape[1]
    row = lax.broadcasted_iota(jnp.int32, value.shape, 0)
    lane = lax.broadcasted_iota(jnp.int32, value.shape, 1)
    held = (lane >= start) & (lane < start + width)
    tiles = []
    for tile in range(chans // width // 8):
        kept = jnp.zeros_like(value)
        for r in range(8):
            moved = rolled(value, start - width * (8 * tile + r), 1)
            kept = jnp.where((row == r) & held, moved, kept)
        tiles.append(kept)
    return jnp.concatenate(tiles, 0)


def from_spare(value, start, width):
    rows, chans = value.shape
    row = lax.broadcasted_iota(jnp.int32, (8, chans), 0)
    lane = lax.broadcasted_iota(jnp.int32, (8, chans), 1)
    kept = jnp.zeros((8, chans), jnp.float32)
    for r in range(rows):
        tile = value[8 * (r // 8) : 8 * (r // 8) + 8, :]
        moved = rolled(tile, width * r - start, 1)
        kept = kept + jnp.where((row == r % 8) & (lane // width == r), moved, 0.0)
    for step in (4, 2, 1):
        kept = kept + rolled(kept, step, 0)
    return kept


def own_part(place, d_h1, raw_lat, raw_cot, gains, shifts, sums_two, grad, extra, nine, d_act, weight, copy):
    blocks, frames, flat, chans = raw_lat.shape
    size = blocks * flat
    depth = 9 * chans
    me = place[0]
    for ahead_by in range(3):
        value = frame_of(d_h1, jnp.minimum(me + ahead_by, frames - 1), size)
        if ahead_by:
            value = jnp.where(me + ahead_by < frames, value, 0.0)
        store_nine(nine, ahead_by, value, -1)
    copy.wait()

    def term(frame, tap):
        left = nine[frame * size : (frame + 1) * size, :]
        return jnp.dot(left, weight[tap * depth : (tap + 1) * depth, :], preferred_element_type=jnp.float32)

    d_act[...] = term(2, 0) + term(1, 1) + term(0, 2)

    @pl.when(me == 0)
    def _():
        d_act[...] = d_act[...] + (term(0, 1) + (term(0, 0) + term(1, 0)))

    count = size * (chans // GROUPS)
    value = load_frame(raw_lat, me)
    mean, factor = norm_parts(value)
    normed = (value - mean) * factor
    u = normed * gains[0:1, :] + shifts[0:1, :]
    sig = jax.nn.sigmoid(u)
    d_out = d_act[...].reshape(size // 8, 8, chans) * (sig * (1.0 + u * (1.0 - sig)))
    d_shift = all_cols(d_out)
    d_gain = all_cols(d_out * normed)
    one = group_all(d_shift * gains[0:1, :]) / count
    two = group_all(d_gain * gains[0:1, :]) / count
    d_in = factor * (d_out * gains[0:1, :] - one - normed * two)
    result = (load_frame(raw_cot, me) + d_in).astype(jnp.bfloat16).astype(jnp.float32)
    grad[...] = result.reshape(blocks, flat, chans)

    owned = chans - 40
    pieces = [to_spare(part, owned, 32) for part in (*halves(d_gain), *halves(d_shift))]
    gain_high, gain_low = halves(sums_two[0])
    shift_high, shift_low = halves(sums_two[1])
    turn = me % 4
    mine = jnp.where(turn < 2, jnp.where(turn == 0, gain_high, gain_low), jnp.where(turn == 2, shift_high, shift_low))
    extra[...] = jnp.concatenate(pieces, 0) + to_spare(0.5 * mine, owned + 32, 8)


def whole_kernel(place, raw, weights, turned, gains, shifts, a_two, grad, out, nine, straight, back_one, back_two, sems, a_one, h_one, d_h1, d_act, own_act, sums_two, extra, long, block, total):
    raw_lat, raw_cot = raw.at[:, 0], raw.at[:, 1]
    copies = [
        pltpu.make_async_copy(weights.at[0], straight, sems.at[0]),
        pltpu.make_async_copy(turned.at[1], back_two, sems.at[1]),
        pltpu.make_async_copy(turned.at[0], back_one, sems.at[2]),
    ]
    for copy in copies:
        copy.start()
    ahead_part(raw_lat, gains, shifts, a_one, h_one, a_two, nine, straight, copies[0])
    grad_part(place, a_two, raw_cot, None, out, 0, long, block, total)
    back_part(raw_cot, h_one, gains, shifts, d_h1, sums_two, nine, d_act, back_two, copies[1])
    own_part(place, d_h1, raw_lat, raw_cot, gains, shifts, sums_two, grad, extra, nine, own_act, back_one, copies[2])
    grad_part(place, a_one, d_h1, extra, out, 1, long, block, total)


def sum_kernel(pieces, grad, out, *, clips):
    total = pieces[0].astype(jnp.float32)
    for d in range(1, pieces.shape[0]):
        total = total + pieces[d].astype(jnp.float32)
    total = total / clips
    rows = total.shape[0]
    for p in range(out.shape[0]):
        out[p, 0:rows, :] = total
        out[p, rows:, :] = grad[p]


def adam_kernel(every, moment, second, new_moment, new_second, direction, vector, grad_input):
    parts, tall, chans = every.shape
    owned = moment.shape[1]
    width = chans // parts
    for layer in range(2):
        start = width * (1 - layer)
        grad = every[:, start : start + width, :].reshape(chans, chans).T[:owned, :]
        new_m = 0.9 * moment[layer] + 0.1 * grad
        new_v = 0.999 * second[layer] + 0.001 * grad * grad
        new_moment[layer] = new_m
        new_second[layer] = new_v
        direction[layer] = new_m / bias_first / (jnp.sqrt(new_v / bias_second) + 1e-08)
    for p in range(parts):
        grad_input[p] = every[p, 2 * width :, :].astype(jnp.bfloat16)
    held = [every[p, width : 2 * width, :] for p in range(parts)]
    summed = held[0]
    for p in range(1, parts):
        summed = summed + held[p]
    for row in range(2):
        high = from_spare(summed[16 * row : 16 * row + 8], owned, 32)
        low = from_spare(summed[16 * row + 8 : 16 * row + 16], owned, 32)
        vector[row : row + 1, :] = (high + low)[0:1]
        mine = sum(held[p] for p in range(parts) if p % 4 in (2 * row, 2 * row + 1))
        vector[2 + row : 3 + row, :] = from_spare(mine, owned + 32, 8)[0:1]


def turn_kernel(weights, turned):
    chans = weights.shape[2]
    for tap in range(weights.shape[1] // chans):
        rows = slice(tap * chans, (tap + 1) * chans)
        turned[0, rows, :] = weights[0, rows, :].T


def decode_kernel(place, a_two, weights, latent, decoded, tall, nine, weight, sem):
    copy = pltpu.make_async_copy(weights.at[1], weight, sem)
    copy.start()
    frames, flat, chans = latent.shape
    size = a_two.shape[0] // frames
    rows, every = flat // 8, size // 8
    pitch = nine.shape[0] // (frames + 2)
    depth = 9 * chans
    tall[0] = jnp.zeros(tall.shape[1:], jnp.float32)
    tall[every + 1] = jnp.zeros(tall.shape[1:], jnp.float32)
    rest = jnp.zeros((pitch // 8 - rows, 8, chans), jnp.float32)
    for t in range(frames):
        tall[1 : every + 1] = frame_of(a_two, t, size)
        part = tall[pl.ds(place[0] * rows, rows + 2)]
        for w in range(3):
            moved = col_shifted(part, w - 1)
            for h in range(3):
                view = jnp.concatenate([moved[h : h + rows], rest], 0).reshape(pitch, chans)
                number = 3 * h + w
                nine[(t + 2) * pitch : (t + 3) * pitch, number * chans : (number + 1) * chans] = view.astype(jnp.bfloat16)
    nine[0:pitch, :] = nine[2 * pitch : 3 * pitch, :]
    nine[pitch : 2 * pitch, :] = nine[2 * pitch : 3 * pitch, :]
    copy.wait()
    total = None
    for t in range(3):
        left = nine[t * pitch : (t + frames) * pitch, :]
        part = jnp.dot(left, weight[t * depth : (t + 1) * depth, :], preferred_element_type=jnp.float32)
        total = part if total is None else total + part
    for t in range(frames):
        value = latent[t].astype(jnp.float32) + total[t * pitch : t * pitch + flat, :]
        decoded[t] = value.astype(jnp.bfloat16)


def spread_kernel(latent, upstream, out):
    for p in range(out.shape[0]):
        out[p, 0] = latent[...]
        out[p, 1] = upstream[...]


def called(kernel, outs, scratch, args, specs=None, flops=0, limit=16):
    whole = pl.BlockSpec(memory_space=pltpu.VMEM)
    specs = specs or [whole] * len(args)
    moved = sum(math.prod(a.shape) * a.dtype.itemsize for a in (*args, *outs))
    return pl.pallas_call(
        kernel,
        out_shape=outs,
        in_specs=[whole if spec is None else spec for spec in specs],
        out_specs=[whole] * len(outs),
        scratch_shapes=scratch,
        compiler_params=pltpu.CompilerParams(vmem_limit_bytes=limit * 2**20),
        cost_estimate=pl.CostEstimate(flops=flops, bytes_accessed=moved, transcendentals=0),
    )(*args)


def held(weights):
    return [pltpu.VMEM(weights.shape[1:], weights.dtype), pltpu.SemaphoreType.DMA]


def small():
    return pl.BlockSpec(memory_space=pltpu.SMEM)


def away():
    return pl.BlockSpec(memory_space=pl.ANY)


def whole(place, raw, weights, turned, gains, shifts, width, clips, cores):
    blocks, _, frames, flat, chans = raw.shape
    size = blocks * flat
    places = frames * size
    f32, bf16 = jnp.float32, jnp.bfloat16
    outs = [
        jax.ShapeDtypeStruct((places, chans), bf16),
        jax.ShapeDtypeStruct((blocks, flat, chans), f32),
        jax.ShapeDtypeStruct((cores, clips // cores, 2 * width, chans), bf16),
    ]
    layer = pltpu.VMEM(weights.shape[1:], bf16)
    scratch = [
        pltpu.VMEM((places + 2 * size, 9 * chans), bf16),
        layer,
        layer,
        layer,
        pltpu.SemaphoreType.DMA((3,)),
        pltpu.VMEM((places, chans), bf16),
        pltpu.VMEM((places, chans), bf16),
        pltpu.VMEM((places, chans), bf16),
        pltpu.VMEM((places, chans), f32),
        pltpu.VMEM((size, chans), f32),
        pltpu.VMEM((2, 8, chans), f32),
        pltpu.VMEM((32, chans), f32),
        pltpu.VMEM((places + 2 * size, chans), bf16),
        pltpu.VMEM((places, -(-9 * width // 128) * 128), bf16),
        pltpu.VMEM((27 * width, chans), f32),
    ]
    args = (place, raw, weights, turned, gains, shifts)
    specs = [small(), None, away(), away(), None, None]
    return called(whole_kernel, outs, scratch, args, specs, 2 * places * weights.size, 44)


def gathered(pieces, grads, clips):
    parts, flat, chans = grads.shape
    outs = [jax.ShapeDtypeStruct((parts, pieces.shape[1] + flat, chans), jnp.float32)]
    return called(functools.partial(sum_kernel, clips=clips), outs, [], (pieces, grads))[0]


def turn(weights):
    layers, depth, chans = weights.shape
    block = pl.BlockSpec((1, depth // 9, chans), lambda k, n: (k, n, 0))
    return pl.pallas_call(
        turn_kernel,
        grid=(layers, 9),
        out_shape=jax.ShapeDtypeStruct(weights.shape, weights.dtype),
        in_specs=[block],
        out_specs=block,
        cost_estimate=pl.CostEstimate(flops=0, bytes_accessed=4 * weights.size, transcendentals=0),
    )(weights)


def decode(place, a_two, weights, latent):
    frames, flat, chans = latent.shape
    size = a_two.shape[0] // frames
    pitch = -(-flat // 16) * 16
    outs = [jax.ShapeDtypeStruct(latent.shape, jnp.bfloat16)]
    scratch = [
        pltpu.VMEM((size // 8 + 2, 8, chans), jnp.float32),
        pltpu.VMEM(((frames + 2) * pitch, 9 * chans), jnp.bfloat16),
    ] + held(weights)
    args = (place, a_two, weights, latent)
    return called(decode_kernel, outs, scratch, args, [small(), None, away(), None], frames * pitch * weights.size, 44)[0]


def per_device(latents, cotangent, conv_weights, gains, shifts, moment, second):
    frames, rows, cols, chans = latents.shape[1:]
    cores, parts = lax.axis_size("core"), lax.axis_size("space")
    clips = lax.axis_size("pair") * cores
    me = lax.axis_index("space")
    place = me.astype(jnp.int32).reshape(1)
    width = chans // parts
    f32, bf16 = jnp.float32, jnp.bfloat16
    latent = latents[0].reshape(frames, rows * cols, chans)
    upstream = cotangent[0].reshape(latent.shape)
    outs = [jax.ShapeDtypeStruct((parts, 2) + latent.shape, bf16)]
    raw = called(spread_kernel, outs, [], (latent, upstream), limit=58)[0]
    raw = lax.all_to_all(raw, "space", 0, 0)
    raw, turned = lax.optimization_barrier((raw, turn(conv_weights)))

    a_two, grads, pieces = whole(place, raw, conv_weights, turned, gains, shifts, width, clips, cores)
    pieces = lax.all_to_all(pieces, "core", 0, 0)
    pieces = jnp.sum(pieces.astype(f32), 0).astype(bf16)
    pieces = lax.all_to_all(pieces, "pair", 0, 0)
    decoded = decode(place, a_two, conv_weights, latent)

    every = gathered(pieces, grads, clips)
    every = lax.all_to_all(every, "space", 0, 0)
    shape = jax.ShapeDtypeStruct(moment.shape, f32)
    outs = [shape, shape, shape, jax.ShapeDtypeStruct((4, chans), f32)]
    outs.append(jax.ShapeDtypeStruct((frames, rows * cols, chans), bf16))
    outs = called(adam_kernel, outs, [], (every, moment, second))
    new_moment, new_second, direction, vector, grad_input = outs
    grad_input = grad_input.reshape(latents.shape)
    return (decoded.reshape(latents.shape), grad_input, new_moment, new_second, direction, vector)


def solution(mesh):
    clips, parts = mesh.devices.shape
    mesh = Mesh(mesh.devices.reshape(clips // 2, 2, parts), ("pair", "core", "space"))
    dp = ("pair", "core")
    placed = (
        P(dp, None, "space", None, None),
        P(dp, None, "space", None, None),
        P(),
        P(),
        P(),
        P(None, dp, None),
        P(None, dp, None),
    )
    return jax.shard_map(
        per_device,
        mesh=mesh,
        in_specs=placed,
        out_specs=(
            P(dp, None, "space", None, None),
            P(dp, None, "space", None, None),
            P(None, dp, None),
            P(None, dp, None),
            P(None, dp, None),
            P(),
        ),
        check_vma=False,
    )
```

```python
import functools
import math

import jax
import jax.numpy as jnp
from jax import lax
from jax.experimental import pallas as pl
from jax.experimental.pallas import tpu as pltpu
from jax.sharding import Mesh
from jax.sharding import PartitionSpec as P

GROUPS = 32
STEP = 4


bias_first = 1.0 - math.exp(100.0 * math.log(0.9))
bias_second = 1.0 - math.exp(100.0 * math.log(0.999))


def rolled(value, amount, axis):
    return pltpu.roll(value, amount % value.shape[axis], axis)


def all_cols(value):
    total = jnp.sum(value, 0)
    for step in (4, 2, 1):
        total = total + rolled(total, step, 0)
    return total


def group_all(sums):
    size = sums.shape[1] // GROUPS
    lane = lax.broadcasted_iota(jnp.int32, sums.shape, 1)
    step = 1
    while step < size:
        partner = jnp.where((lane & step) == 0, rolled(sums, -step, 1), rolled(sums, step, 1))
        sums = sums + partner
        step *= 2
    return sums


def norm_parts(values):
    count = values.shape[0] * values.shape[1] * (values.shape[2] // GROUPS)
    mean = group_all(all_cols(values)) / count
    var = group_all(all_cols(values * values)) / count - mean * mean
    return mean, lax.rsqrt(var + 1e-05)


def col_shifted(value, step):
    if step == 0:
        return value
    col = lax.broadcasted_iota(jnp.int32, value.shape, 1)
    edge = value.shape[1] - 1 if step > 0 else 0
    return jnp.where(col == edge, 0.0, rolled(value, -step, 1))


def row_shifted(value, step):
    if step == 0:
        return value
    zero = jnp.zeros_like(value[:1])
    if step > 0:
        return jnp.concatenate([value[1:], zero], 0)
    return jnp.concatenate([zero, value[:-1]], 0)


def store_nine(target, frame, value, sign):
    rows, cols, chans = value.shape
    size = rows * cols
    for w in range(3):
        moved = col_shifted(value, sign * (w - 1))
        for h in range(3):
            view = row_shifted(moved, sign * (h - 1)).reshape(size, chans)
            number = 3 * h + w
            target[pl.ds(pl.multiple_of(frame * size, 16), size), number * chans : (number + 1) * chans] = view.astype(jnp.bfloat16)


def load_frame(raw, frame):
    blocks, _, flat, chans = raw.shape
    parts = [raw[b, frame].astype(jnp.float32).reshape(flat // 8, 8, chans) for b in range(blocks)]
    return jnp.concatenate(parts, 0)


def frame_of(flat, frame, size):
    part = flat[pl.ds(pl.multiple_of(frame * size, 16), size), :]
    return part.astype(jnp.float32).reshape(size // 8, 8, part.shape[-1])


def put_frame(flat, frame, value):
    size = value.shape[0] * value.shape[1]
    flat[pl.ds(pl.multiple_of(frame * size, 16), size), :] = value.reshape(size, -1).astype(flat.dtype)


def ahead_part(raw, gains, shifts, a_one, h_one, a_two, nine, weight, copy):
    frames, chans = raw.shape[1], raw.shape[3]
    size = raw.shape[0] * raw.shape[2]
    depth = 9 * chans

    @pl.loop(0, frames, unroll=frames)
    def _(t):
        value = load_frame(raw, t)
        mean, factor = norm_parts(value)
        u = (value - mean) * factor * gains[0:1, :] + shifts[0:1, :]
        act = (u * jax.nn.sigmoid(u)).astype(jnp.bfloat16).astype(jnp.float32)
        put_frame(a_one, t, act)
        store_nine(nine, t + 2, act, 1)

    nine[0:size, :] = nine[2 * size : 3 * size, :]
    nine[size : 2 * size, :] = nine[2 * size : 3 * size, :]
    copy.wait()

    @pl.loop(0, frames // STEP, unroll=frames // STEP)
    def _(b):
        total = None
        for t in range(3):
            left = nine[pl.ds(pl.multiple_of((b * STEP + t) * size, 16), STEP * size), :]
            part = jnp.dot(left, weight[t * depth : (t + 1) * depth, :], preferred_element_type=jnp.float32)
            total = part if total is None else total + part
        h_one[pl.ds(pl.multiple_of(b * STEP * size, 16), STEP * size), :] = total.astype(jnp.bfloat16)

    @pl.loop(0, frames, unroll=frames)
    def _(t):
        value = frame_of(h_one, t, size)
        mean, factor = norm_parts(value)
        u = (value - mean) * factor * gains[1:2, :] + shifts[1:2, :]
        put_frame(a_two, t, u * jax.nn.sigmoid(u))


def back_part(raw, h_one, gains, shifts, d_h1, vectors, nine, d_act, weight, copy):
    frames, chans = raw.shape[1], raw.shape[3]
    size = raw.shape[0] * raw.shape[2]
    depth = 9 * chans

    @pl.loop(0, frames, unroll=frames)
    def _(t):
        store_nine(nine, t, load_frame(raw, t), -1)

    nine[frames * size :, :] = jnp.zeros((2 * size, depth), jnp.bfloat16)
    copy.wait()

    @pl.loop(0, frames // STEP, unroll=frames // STEP)
    def _(b):
        total = None
        for t in range(3):
            left = nine[pl.ds(pl.multiple_of((b * STEP + 2 - t) * size, 16), STEP * size), :]
            part = jnp.dot(left, weight[t * depth : (t + 1) * depth, :], preferred_element_type=jnp.float32)
            total = part if total is None else total + part
        d_act[pl.ds(pl.multiple_of(b * STEP * size, 16), STEP * size), :] = total

    pair = jnp.dot(nine[0:size, :], weight[depth : 2 * depth, :], preferred_element_type=jnp.float32)
    both = jnp.dot(nine[0 : 2 * size, :], weight[0:depth, :], preferred_element_type=jnp.float32)
    d_act[0:size, :] = d_act[0:size, :] + (pair + (both[:size] + both[size:]))

    vectors[...] = jnp.zeros_like(vectors)
    count = size * (chans // GROUPS)

    @pl.loop(0, frames, unroll=frames)
    def _(t):
        value = frame_of(h_one, t, size)
        mean, factor = norm_parts(value)
        normed = (value - mean) * factor
        u = normed * gains[1:2, :] + shifts[1:2, :]
        sig = jax.nn.sigmoid(u)
        d_out = frame_of(d_act, t, size) * (sig * (1.0 + u * (1.0 - sig)))
        d_shift = all_cols(d_out)
        d_gain = all_cols(d_out * normed)
        vectors[0] += d_gain
        vectors[1] += d_shift
        one = group_all(d_shift * gains[1:2, :]) / count
        two = group_all(d_gain * gains[1:2, :]) / count
        put_frame(d_h1, t, factor * (d_out * gains[1:2, :] - one - normed * two))


def grad_part(place, values, grads, extra, out, part_number, long, block, total):
    frames_size, chans = values.shape
    cores, pairs, _, _ = out.shape
    owners = cores * pairs
    size, outs = (long.shape[0] - frames_size) // 2, total.shape[0] // 27
    frames = frames_size // size
    long[0:size, :] = values[0:size, :]
    long[size : 2 * size, :] = values[0:size, :]
    long[2 * size :, :] = values[...]
    lanes = block.shape[1]
    chan = lax.broadcasted_iota(jnp.int32, (chans, lanes), 0)
    lane = lax.broadcasted_iota(jnp.int32, (chans, lanes), 1)
    pick = (chan == place[0] * outs + lane % outs).astype(jnp.bfloat16)

    @pl.loop(0, frames, unroll=frames)
    def _(t):
        if len(grads.shape) == 4:
            rows = load_frame(grads, t).reshape(size, chans).astype(jnp.bfloat16)
        else:
            rows = grads[pl.ds(pl.multiple_of(t * size, 16), size), :]
        spread_out = jnp.dot(rows, pick, preferred_element_type=jnp.float32).reshape(size // 8, 8, lanes)
        for piece in range(lanes // 128):
            value = spread_out[:, :, piece * 128 : (piece + 1) * 128]
            lane = lax.broadcasted_iota(jnp.int32, value.shape, 2)
            kept = jnp.zeros_like(value)
            for place_in in range(128 // outs):
                number = piece * (128 // outs) + place_in
                if number < 9:
                    h, w = divmod(number, 3)
                    moved = row_shifted(col_shifted(value, 1 - w), 1 - h)
                    kept = jnp.where(lane // outs == place_in, moved, kept)
            block[pl.ds(pl.multiple_of(t * size, 16), size), piece * 128 : (piece + 1) * 128] = kept.reshape(size, 128).astype(jnp.bfloat16)

    side = block[...].T
    for t in range(3):
        part = jnp.dot(side, long[t * size : (t + frames) * size, :], preferred_element_type=jnp.float32)
        total[t * 9 * outs : (t + 1) * 9 * outs, :] = part[: 9 * outs]

    owned = 27 * chans // owners
    lane = lax.broadcasted_iota(jnp.int32, (outs, chans), 1)
    for d in range(owners):
        tap, start = divmod(d * owned, chans)
        one = total[tap * outs : (tap + 1) * outs, :]
        if start + owned > chans:
            one = jnp.concatenate([one, total[(tap + 1) * outs : (tap + 2) * outs, :]], 1)
        one = rolled(one, -start, 1)[:, :chans]
        if extra is not None:
            one = jnp.where(lane < owned, one, extra[...])
        out[d % cores, d // cores, part_number * outs : (part_number + 1) * outs, :] = one.astype(jnp.bfloat16)


def halves(value):
    high = value.astype(jnp.bfloat16).astype(jnp.float32)
    return high, value - high


def to_spare(value, start, width):
    chans = value.shape[1]
    row = lax.broadcasted_iota(jnp.int32, value.shape, 0)
    lane = lax.broadcasted_iota(jnp.int32, value.shape, 1)
    held = (lane >= start) & (lane < start + width)
    tiles = []
    for tile in range(chans // width // 8):
        kept = jnp.zeros_like(value)
        for r in range(8):
            moved = rolled(value, start - width * (8 * tile + r), 1)
            kept = jnp.where((row == r) & held, moved, kept)
        tiles.append(kept)
    return jnp.concatenate(tiles, 0)


def from_spare(value, start, width):
    rows, chans = value.shape
    row = lax.broadcasted_iota(jnp.int32, (8, chans), 0)
    lane = lax.broadcasted_iota(jnp.int32, (8, chans), 1)
    kept = jnp.zeros((8, chans), jnp.float32)
    for r in range(rows):
        tile = value[8 * (r // 8) : 8 * (r // 8) + 8, :]
        moved = rolled(tile, width * r - start, 1)
        kept = kept + jnp.where((row == r % 8) & (lane // width == r), moved, 0.0)
    for step in (4, 2, 1):
        kept = kept + rolled(kept, step, 0)
    return kept


def own_part(place, d_h1, raw_lat, raw_cot, gains, shifts, sums_two, grad, extra, nine, d_act, weight, copy):
    blocks, frames, flat, chans = raw_lat.shape
    size = blocks * flat
    depth = 9 * chans
    me = place[0]
    for ahead_by in range(3):
        value = frame_of(d_h1, jnp.minimum(me + ahead_by, frames - 1), size)
        if ahead_by:
            value = jnp.where(me + ahead_by < frames, value, 0.0)
        store_nine(nine, ahead_by, value, -1)
    copy.wait()

    def term(frame, tap):
        left = nine[frame * size : (frame + 1) * size, :]
        return jnp.dot(left, weight[tap * depth : (tap + 1) * depth, :], preferred_element_type=jnp.float32)

    d_act[...] = term(2, 0) + term(1, 1) + term(0, 2)

    @pl.when(me == 0)
    def _():
        d_act[...] = d_act[...] + (term(0, 1) + (term(0, 0) + term(1, 0)))

    count = size * (chans // GROUPS)
    value = load_frame(raw_lat, me)
    mean, factor = norm_parts(value)
    normed = (value - mean) * factor
    u = normed * gains[0:1, :] + shifts[0:1, :]
    sig = jax.nn.sigmoid(u)
    d_out = d_act[...].reshape(size // 8, 8, chans) * (sig * (1.0 + u * (1.0 - sig)))
    d_shift = all_cols(d_out)
    d_gain = all_cols(d_out * normed)
    one = group_all(d_shift * gains[0:1, :]) / count
    two = group_all(d_gain * gains[0:1, :]) / count
    d_in = factor * (d_out * gains[0:1, :] - one - normed * two)
    result = (load_frame(raw_cot, me) + d_in).astype(jnp.bfloat16).astype(jnp.float32)
    grad[...] = result.reshape(blocks, flat, chans)

    owned = chans - 40
    pieces = [to_spare(part, owned, 32) for part in (*halves(d_gain), *halves(d_shift))]
    gain_high, gain_low = halves(sums_two[0])
    shift_high, shift_low = halves(sums_two[1])
    turn = me % 4
    mine = jnp.where(turn < 2, jnp.where(turn == 0, gain_high, gain_low), jnp.where(turn == 2, shift_high, shift_low))
    extra[...] = jnp.concatenate(pieces, 0) + to_spare(0.5 * mine, owned + 32, 8)


def whole_kernel(place, raw, weights, turned, gains, shifts, a_two, grad, out, nine, straight, back_one, back_two, sems, a_one, h_one, d_h1, d_act, own_act, sums_two, extra, long, block, total):
    raw_lat, raw_cot = raw.at[:, 0], raw.at[:, 1]
    copies = [
        pltpu.make_async_copy(weights.at[0], straight, sems.at[0]),
        pltpu.make_async_copy(turned.at[1], back_two, sems.at[1]),
        pltpu.make_async_copy(turned.at[0], back_one, sems.at[2]),
    ]
    for copy in copies:
        copy.start()
    ahead_part(raw_lat, gains, shifts, a_one, h_one, a_two, nine, straight, copies[0])
    grad_part(place, a_two, raw_cot, None, out, 0, long, block, total)
    back_part(raw_cot, h_one, gains, shifts, d_h1, sums_two, nine, d_act, back_two, copies[1])
    own_part(place, d_h1, raw_lat, raw_cot, gains, shifts, sums_two, grad, extra, nine, own_act, back_one, copies[2])
    grad_part(place, a_one, d_h1, extra, out, 1, long, block, total)


def sum_kernel(pieces, grad, out, *, clips):
    total = pieces[0].astype(jnp.float32)
    for d in range(1, pieces.shape[0]):
        total = total + pieces[d].astype(jnp.float32)
    total = total / clips
    rows = total.shape[0]
    for p in range(out.shape[0]):
        out[p, 0:rows, :] = total
        out[p, rows:, :] = grad[p]


def adam_kernel(every, moment, second, new_moment, new_second, direction, vector, grad_input):
    parts, tall, chans = every.shape
    owned = moment.shape[1]
    width = chans // parts
    for layer in range(2):
        start = width * (1 - layer)
        grad = every[:, start : start + width, :].reshape(chans, chans).T[:owned, :]
        new_m = 0.9 * moment[layer] + 0.1 * grad
        new_v = 0.999 * second[layer] + 0.001 * grad * grad
        new_moment[layer] = new_m
        new_second[layer] = new_v
        direction[layer] = new_m / bias_first / (jnp.sqrt(new_v / bias_second) + 1e-08)
    for p in range(parts):
        grad_input[p] = every[p, 2 * width :, :].astype(jnp.bfloat16)
    held = [every[p, width : 2 * width, :] for p in range(parts)]
    summed = held[0]
    for p in range(1, parts):
        summed = summed + held[p]
    for row in range(2):
        high = from_spare(summed[16 * row : 16 * row + 8], owned, 32)
        low = from_spare(summed[16 * row + 8 : 16 * row + 16], owned, 32)
        vector[row : row + 1, :] = (high + low)[0:1]
        mine = sum(held[p] for p in range(parts) if p % 4 in (2 * row, 2 * row + 1))
        vector[2 + row : 3 + row, :] = from_spare(mine, owned + 32, 8)[0:1]


def turn_kernel(weights, turned):
    chans = weights.shape[2]
    for tap in range(weights.shape[1] // chans):
        rows = slice(tap * chans, (tap + 1) * chans)
        turned[0, rows, :] = weights[0, rows, :].T


def decode_kernel(place, a_two, weights, latent, decoded, tall, nine, weight, sem):
    copy = pltpu.make_async_copy(weights.at[1], weight, sem)
    copy.start()
    frames, flat, chans = latent.shape
    size = a_two.shape[0] // frames
    rows, every = flat // 8, size // 8
    pitch = nine.shape[0] // (frames + 2)
    depth = 9 * chans
    tall[0] = jnp.zeros(tall.shape[1:], jnp.float32)
    tall[every + 1] = jnp.zeros(tall.shape[1:], jnp.float32)
    rest = jnp.zeros((pitch // 8 - rows, 8, chans), jnp.float32)
    for t in range(frames):
        tall[1 : every + 1] = frame_of(a_two, t, size)
        part = tall[pl.ds(place[0] * rows, rows + 2)]
        for w in range(3):
            moved = col_shifted(part, w - 1)
            for h in range(3):
                view = jnp.concatenate([moved[h : h + rows], rest], 0).reshape(pitch, chans)
                number = 3 * h + w
                nine[(t + 2) * pitch : (t + 3) * pitch, number * chans : (number + 1) * chans] = view.astype(jnp.bfloat16)
    nine[0:pitch, :] = nine[2 * pitch : 3 * pitch, :]
    nine[pitch : 2 * pitch, :] = nine[2 * pitch : 3 * pitch, :]
    copy.wait()
    total = None
    for t in range(3):
        left = nine[t * pitch : (t + frames) * pitch, :]
        part = jnp.dot(left, weight[t * depth : (t + 1) * depth, :], preferred_element_type=jnp.float32)
        total = part if total is None else total + part
    for t in range(frames):
        value = latent[t].astype(jnp.float32) + total[t * pitch : t * pitch + flat, :]
        decoded[t] = value.astype(jnp.bfloat16)


def spread_kernel(latent, upstream, out, sems):
    copies = []
    for p in range(out.shape[0]):
        copies.append(pltpu.make_async_copy(latent, out.at[p, 0], sems.at[p, 0]))
        copies.append(pltpu.make_async_copy(upstream, out.at[p, 1], sems.at[p, 1]))
    for copy in copies:
        copy.start()
    for copy in copies:
        copy.wait()


def pair_kernel(pieces, out):
    for n in range(out.shape[0]):
        out[n] = (pieces[0, n].astype(jnp.float32) + pieces[1, n].astype(jnp.float32)).astype(jnp.bfloat16)


def called(kernel, outs, scratch, args, specs=None, flops=0, limit=16, out_specs=None):
    whole = pl.BlockSpec(memory_space=pltpu.VMEM)
    specs = specs or [whole] * len(args)
    moved = sum(math.prod(a.shape) * a.dtype.itemsize for a in (*args, *outs))
    return pl.pallas_call(
        kernel,
        out_shape=outs,
        in_specs=[whole if spec is None else spec for spec in specs],
        out_specs=out_specs or [whole] * len(outs),
        scratch_shapes=scratch,
        compiler_params=pltpu.CompilerParams(vmem_limit_bytes=limit * 2**20),
        cost_estimate=pl.CostEstimate(flops=flops, bytes_accessed=moved, transcendentals=0),
    )(*args)


def held(weights):
    return [pltpu.VMEM(weights.shape[1:], weights.dtype), pltpu.SemaphoreType.DMA]


def small():
    return pl.BlockSpec(memory_space=pltpu.SMEM)


def away():
    return pl.BlockSpec(memory_space=pl.ANY)


def whole(place, raw, weights, turned, gains, shifts, width, clips, cores):
    blocks, _, frames, flat, chans = raw.shape
    size = blocks * flat
    places = frames * size
    f32, bf16 = jnp.float32, jnp.bfloat16
    outs = [
        jax.ShapeDtypeStruct((places, chans), bf16),
        jax.ShapeDtypeStruct((blocks, flat, chans), f32),
        jax.ShapeDtypeStruct((cores, clips // cores, 2 * width, chans), bf16),
    ]
    layer = pltpu.VMEM(weights.shape[1:], bf16)
    scratch = [
        pltpu.VMEM((places + 2 * size, 9 * chans), bf16),
        layer,
        layer,
        layer,
        pltpu.SemaphoreType.DMA((3,)),
        pltpu.VMEM((places, chans), bf16),
        pltpu.VMEM((places, chans), bf16),
        pltpu.VMEM((places, chans), bf16),
        pltpu.VMEM((places, chans), f32),
        pltpu.VMEM((size, chans), f32),
        pltpu.VMEM((2, 8, chans), f32),
        pltpu.VMEM((32, chans), f32),
        pltpu.VMEM((places + 2 * size, chans), bf16),
        pltpu.VMEM((places, -(-9 * width // 128) * 128), bf16),
        pltpu.VMEM((27 * width, chans), f32),
    ]
    args = (place, raw, weights, turned, gains, shifts)
    specs = [small(), None, away(), away(), None, None]
    return called(whole_kernel, outs, scratch, args, specs, 2 * places * weights.size, 44)


def gathered(pieces, grads, clips):
    parts, flat, chans = grads.shape
    outs = [jax.ShapeDtypeStruct((parts, pieces.shape[1] + flat, chans), jnp.float32)]
    return called(functools.partial(sum_kernel, clips=clips), outs, [], (pieces, grads))[0]


def turn(weights):
    layers, depth, chans = weights.shape
    block = pl.BlockSpec((1, depth // 9, chans), lambda k, n: (k, n, 0))
    return pl.pallas_call(
        turn_kernel,
        grid=(layers, 9),
        out_shape=jax.ShapeDtypeStruct(weights.shape, weights.dtype),
        in_specs=[block],
        out_specs=block,
        cost_estimate=pl.CostEstimate(flops=0, bytes_accessed=4 * weights.size, transcendentals=0),
    )(weights)


def decode(place, a_two, weights, latent):
    frames, flat, chans = latent.shape
    size = a_two.shape[0] // frames
    pitch = -(-flat // 16) * 16
    outs = [jax.ShapeDtypeStruct(latent.shape, jnp.bfloat16)]
    scratch = [
        pltpu.VMEM((size // 8 + 2, 8, chans), jnp.float32),
        pltpu.VMEM(((frames + 2) * pitch, 9 * chans), jnp.bfloat16),
    ] + held(weights)
    args = (place, a_two, weights, latent)
    return called(decode_kernel, outs, scratch, args, [small(), None, away(), None], frames * pitch * weights.size, 44)[0]


def per_device(latents, cotangent, conv_weights, gains, shifts, moment, second):
    frames, rows, cols, chans = latents.shape[1:]
    cores, parts = lax.axis_size("core"), lax.axis_size("space")
    clips = lax.axis_size("pair") * cores
    me = lax.axis_index("space")
    place = me.astype(jnp.int32).reshape(1)
    width = chans // parts
    f32, bf16 = jnp.float32, jnp.bfloat16
    latent = latents[0].reshape(frames, rows * cols, chans)
    upstream = cotangent[0].reshape(latent.shape)
    outs = [jax.ShapeDtypeStruct((parts, 2) + latent.shape, bf16)]
    raw = called(spread_kernel, outs, [pltpu.SemaphoreType.DMA((parts, 2))], (latent, upstream), limit=58, out_specs=[away()])[0]
    raw = lax.all_to_all(raw, "space", 0, 0)
    raw, turned = lax.optimization_barrier((raw, turn(conv_weights)))

    a_two, grads, pieces = whole(place, raw, conv_weights, turned, gains, shifts, width, clips, cores)
    pieces = lax.all_to_all(pieces, "core", 0, 0)
    pieces = called(pair_kernel, [jax.ShapeDtypeStruct(pieces.shape[1:], bf16)], [], (pieces,))[0]
    pieces = lax.all_to_all(pieces, "pair", 0, 0)
    decoded = decode(place, a_two, conv_weights, latent)

    every = gathered(pieces, grads, clips)
    every = lax.all_to_all(every, "space", 0, 0)
    shape = jax.ShapeDtypeStruct(moment.shape, f32)
    outs = [shape, shape, shape, jax.ShapeDtypeStruct((4, chans), f32)]
    outs.append(jax.ShapeDtypeStruct((frames, rows * cols, chans), bf16))
    outs = called(adam_kernel, outs, [], (every, moment, second))
    new_moment, new_second, direction, vector, grad_input = outs
    grad_input = grad_input.reshape(latents.shape)
    return (decoded.reshape(latents.shape), grad_input, new_moment, new_second, direction, vector)


def solution(mesh):
    clips, parts = mesh.devices.shape
    mesh = Mesh(mesh.devices.reshape(clips // 2, 2, parts), ("pair", "core", "space"))
    dp = ("pair", "core")
    placed = (
        P(dp, None, "space", None, None),
        P(dp, None, "space", None, None),
        P(),
        P(),
        P(),
        P(None, dp, None),
        P(None, dp, None),
    )
    return jax.shard_map(
        per_device,
        mesh=mesh,
        in_specs=placed,
        out_specs=(
            P(dp, None, "space", None, None),
            P(dp, None, "space", None, None),
            P(None, dp, None),
            P(None, dp, None),
            P(None, dp, None),
            P(),
        ),
        check_vma=False,
    )
```

```python
import functools
import math

import jax
import jax.numpy as jnp
from jax import lax
from jax.experimental import pallas as pl
from jax.experimental.pallas import tpu as pltpu
from jax.sharding import Mesh
from jax.sharding import PartitionSpec as P

GROUPS = 32
STEP = 4


bias_first = 1.0 - math.exp(100.0 * math.log(0.9))
bias_second = 1.0 - math.exp(100.0 * math.log(0.999))


def rolled(value, amount, axis):
    return pltpu.roll(value, amount % value.shape[axis], axis)


def all_cols(value):
    total = jnp.sum(value, 0)
    for step in (4, 2, 1):
        total = total + rolled(total, step, 0)
    return total


def group_all(sums):
    size = sums.shape[1] // GROUPS
    lane = lax.broadcasted_iota(jnp.int32, sums.shape, 1)
    step = 1
    while step < size:
        partner = jnp.where((lane & step) == 0, rolled(sums, -step, 1), rolled(sums, step, 1))
        sums = sums + partner
        step *= 2
    return sums


def norm_parts(values):
    count = values.shape[0] * values.shape[1] * (values.shape[2] // GROUPS)
    mean = group_all(all_cols(values)) / count
    var = group_all(all_cols(values * values)) / count - mean * mean
    return mean, lax.rsqrt(var + 1e-05)


def col_shifted(value, step):
    if step == 0:
        return value
    col = lax.broadcasted_iota(jnp.int32, value.shape, 1)
    edge = value.shape[1] - 1 if step > 0 else 0
    return jnp.where(col == edge, 0.0, rolled(value, -step, 1))


def row_shifted(value, step):
    if step == 0:
        return value
    zero = jnp.zeros_like(value[:1])
    if step > 0:
        return jnp.concatenate([value[1:], zero], 0)
    return jnp.concatenate([zero, value[:-1]], 0)


def store_nine(target, frame, value, sign):
    rows, cols, chans = value.shape
    size = rows * cols
    for w in range(3):
        moved = col_shifted(value, sign * (w - 1))
        for h in range(3):
            view = row_shifted(moved, sign * (h - 1)).reshape(size, chans)
            number = 3 * h + w
            target[pl.ds(pl.multiple_of(frame * size, 16), size), number * chans : (number + 1) * chans] = view.astype(jnp.bfloat16)


def load_frame(raw, frame):
    blocks, _, flat, chans = raw.shape
    parts = [raw[b, frame].astype(jnp.float32).reshape(flat // 8, 8, chans) for b in range(blocks)]
    return jnp.concatenate(parts, 0)


def frame_of(flat, frame, size):
    part = flat[pl.ds(pl.multiple_of(frame * size, 16), size), :]
    return part.astype(jnp.float32).reshape(size // 8, 8, part.shape[-1])


def put_frame(flat, frame, value):
    size = value.shape[0] * value.shape[1]
    flat[pl.ds(pl.multiple_of(frame * size, 16), size), :] = value.reshape(size, -1).astype(flat.dtype)


def ahead_part(raw, gains, shifts, a_one, h_one, a_two, nine, weight, copy):
    frames, chans = raw.shape[1], raw.shape[3]
    size = raw.shape[0] * raw.shape[2]
    depth = 9 * chans

    @pl.loop(0, frames, unroll=frames)
    def _(t):
        value = load_frame(raw, t)
        mean, factor = norm_parts(value)
        u = (value - mean) * factor * gains[0:1, :] + shifts[0:1, :]
        act = (u * jax.nn.sigmoid(u)).astype(jnp.bfloat16).astype(jnp.float32)
        put_frame(a_one, t, act)
        store_nine(nine, t + 2, act, 1)

    nine[0:size, :] = nine[2 * size : 3 * size, :]
    nine[size : 2 * size, :] = nine[2 * size : 3 * size, :]
    copy.wait()

    @pl.loop(0, frames // STEP, unroll=frames // STEP)
    def _(b):
        total = None
        for t in range(3):
            left = nine[pl.ds(pl.multiple_of((b * STEP + t) * size, 16), STEP * size), :]
            part = jnp.dot(left, weight[t * depth : (t + 1) * depth, :], preferred_element_type=jnp.float32)
            total = part if total is None else total + part
        h_one[pl.ds(pl.multiple_of(b * STEP * size, 16), STEP * size), :] = total.astype(jnp.bfloat16)

    @pl.loop(0, frames, unroll=frames)
    def _(t):
        value = frame_of(h_one, t, size)
        mean, factor = norm_parts(value)
        u = (value - mean) * factor * gains[1:2, :] + shifts[1:2, :]
        put_frame(a_two, t, u * jax.nn.sigmoid(u))


def back_part(raw, h_one, gains, shifts, d_h1, vectors, nine, d_act, weight, copy):
    frames, chans = raw.shape[1], raw.shape[3]
    size = raw.shape[0] * raw.shape[2]
    depth = 9 * chans

    @pl.loop(0, frames, unroll=frames)
    def _(t):
        store_nine(nine, t, load_frame(raw, t), -1)

    nine[frames * size :, :] = jnp.zeros((2 * size, depth), jnp.bfloat16)
    copy.wait()

    @pl.loop(0, frames // STEP, unroll=frames // STEP)
    def _(b):
        total = None
        for t in range(3):
            left = nine[pl.ds(pl.multiple_of((b * STEP + 2 - t) * size, 16), STEP * size), :]
            part = jnp.dot(left, weight[t * depth : (t + 1) * depth, :], preferred_element_type=jnp.float32)
            total = part if total is None else total + part
        d_act[pl.ds(pl.multiple_of(b * STEP * size, 16), STEP * size), :] = total

    pair = jnp.dot(nine[0:size, :], weight[depth : 2 * depth, :], preferred_element_type=jnp.float32)
    both = jnp.dot(nine[0 : 2 * size, :], weight[0:depth, :], preferred_element_type=jnp.float32)
    d_act[0:size, :] = d_act[0:size, :] + (pair + (both[:size] + both[size:]))

    vectors[...] = jnp.zeros_like(vectors)
    count = size * (chans // GROUPS)

    @pl.loop(0, frames, unroll=frames)
    def _(t):
        value = frame_of(h_one, t, size)
        mean, factor = norm_parts(value)
        normed = (value - mean) * factor
        u = normed * gains[1:2, :] + shifts[1:2, :]
        sig = jax.nn.sigmoid(u)
        d_out = frame_of(d_act, t, size) * (sig * (1.0 + u * (1.0 - sig)))
        d_shift = all_cols(d_out)
        d_gain = all_cols(d_out * normed)
        vectors[0] += d_gain
        vectors[1] += d_shift
        one = group_all(d_shift * gains[1:2, :]) / count
        two = group_all(d_gain * gains[1:2, :]) / count
        put_frame(d_h1, t, factor * (d_out * gains[1:2, :] - one - normed * two))


def grad_part(place, values, grads, extra, out, part_number, long, block, total):
    frames_size, chans = values.shape
    cores, pairs, _, _ = out.shape
    owners = cores * pairs
    size, outs = (long.shape[0] - frames_size) // 2, total.shape[0] // 27
    frames = frames_size // size
    long[0:size, :] = values[0:size, :]
    long[size : 2 * size, :] = values[0:size, :]
    long[2 * size :, :] = values[...]
    lanes = block.shape[1]
    chan = lax.broadcasted_iota(jnp.int32, (chans, lanes), 0)
    lane = lax.broadcasted_iota(jnp.int32, (chans, lanes), 1)
    pick = (chan == place[0] * outs + lane % outs).astype(jnp.bfloat16)

    @pl.loop(0, frames, unroll=frames)
    def _(t):
        if len(grads.shape) == 4:
            rows = load_frame(grads, t).reshape(size, chans).astype(jnp.bfloat16)
        else:
            rows = grads[pl.ds(pl.multiple_of(t * size, 16), size), :]
        spread_out = jnp.dot(rows, pick, preferred_element_type=jnp.float32).reshape(size // 8, 8, lanes)
        for piece in range(lanes // 128):
            value = spread_out[:, :, piece * 128 : (piece + 1) * 128]
            lane = lax.broadcasted_iota(jnp.int32, value.shape, 2)
            kept = jnp.zeros_like(value)
            for place_in in range(128 // outs):
                number = piece * (128 // outs) + place_in
                if number < 9:
                    h, w = divmod(number, 3)
                    moved = row_shifted(col_shifted(value, 1 - w), 1 - h)
                    kept = jnp.where(lane // outs == place_in, moved, kept)
            block[pl.ds(pl.multiple_of(t * size, 16), size), piece * 128 : (piece + 1) * 128] = kept.reshape(size, 128).astype(jnp.bfloat16)

    side = block[...].T
    for t in range(3):
        part = jnp.dot(side, long[t * size : (t + frames) * size, :], preferred_element_type=jnp.float32)
        total[t * 9 * outs : (t + 1) * 9 * outs, :] = part[: 9 * outs]

    owned = 27 * chans // owners
    lane = lax.broadcasted_iota(jnp.int32, (outs, chans), 1)
    for d in range(owners):
        tap, start = divmod(d * owned, chans)
        one = total[tap * outs : (tap + 1) * outs, :]
        if start + owned > chans:
            one = jnp.concatenate([one, total[(tap + 1) * outs : (tap + 2) * outs, :]], 1)
        one = rolled(one, -start, 1)[:, :chans]
        if extra is not None:
            one = jnp.where(lane < owned, one, extra[...])
        out[d % cores, d // cores, part_number * outs : (part_number + 1) * outs, :] = one.astype(jnp.bfloat16)


def halves(value):
    high = value.astype(jnp.bfloat16).astype(jnp.float32)
    return high, value - high


def to_spare(value, start, width):
    chans = value.shape[1]
    row = lax.broadcasted_iota(jnp.int32, value.shape, 0)
    lane = lax.broadcasted_iota(jnp.int32, value.shape, 1)
    held = (lane >= start) & (lane < start + width)
    tiles = []
    for tile in range(chans // width // 8):
        kept = jnp.zeros_like(value)
        for r in range(8):
            moved = rolled(value, start - width * (8 * tile + r), 1)
            kept = jnp.where((row == r) & held, moved, kept)
        tiles.append(kept)
    return jnp.concatenate(tiles, 0)


def from_spare(value, start, width):
    rows, chans = value.shape
    row = lax.broadcasted_iota(jnp.int32, (8, chans), 0)
    lane = lax.broadcasted_iota(jnp.int32, (8, chans), 1)
    kept = jnp.zeros((8, chans), jnp.float32)
    for r in range(rows):
        tile = value[8 * (r // 8) : 8 * (r // 8) + 8, :]
        moved = rolled(tile, width * r - start, 1)
        kept = kept + jnp.where((row == r % 8) & (lane // width == r), moved, 0.0)
    for step in (4, 2, 1):
        kept = kept + rolled(kept, step, 0)
    return kept


def own_part(place, d_h1, raw_lat, raw_cot, gains, shifts, sums_two, grad, extra, nine, d_act, weight, copy):
    blocks, frames, flat, chans = raw_lat.shape
    size = blocks * flat
    depth = 9 * chans
    me = place[0]
    for ahead_by in range(3):
        value = frame_of(d_h1, jnp.minimum(me + ahead_by, frames - 1), size)
        if ahead_by:
            value = jnp.where(me + ahead_by < frames, value, 0.0)
        store_nine(nine, ahead_by, value, -1)
    copy.wait()

    def term(frame, tap):
        left = nine[frame * size : (frame + 1) * size, :]
        return jnp.dot(left, weight[tap * depth : (tap + 1) * depth, :], preferred_element_type=jnp.float32)

    d_act[...] = term(2, 0) + term(1, 1) + term(0, 2)

    @pl.when(me == 0)
    def _():
        pair = jnp.dot(nine[0 : 2 * size, :], weight[0:depth, :], preferred_element_type=jnp.float32)
        d_act[...] = d_act[...] + (term(0, 1) + (pair[:size] + pair[size:]))

    count = size * (chans // GROUPS)
    value = load_frame(raw_lat, me)
    mean, factor = norm_parts(value)
    normed = (value - mean) * factor
    u = normed * gains[0:1, :] + shifts[0:1, :]
    sig = jax.nn.sigmoid(u)
    d_out = d_act[...].reshape(size // 8, 8, chans) * (sig * (1.0 + u * (1.0 - sig)))
    d_shift = all_cols(d_out)
    d_gain = all_cols(d_out * normed)
    one = group_all(d_shift * gains[0:1, :]) / count
    two = group_all(d_gain * gains[0:1, :]) / count
    d_in = factor * (d_out * gains[0:1, :] - one - normed * two)
    result = (load_frame(raw_cot, me) + d_in).astype(jnp.bfloat16).astype(jnp.float32)
    grad[...] = result.reshape(blocks, flat, chans)

    owned = chans - 40
    pieces = [to_spare(part, owned, 32) for part in (*halves(d_gain), *halves(d_shift))]
    gain_high, gain_low = halves(sums_two[0])
    shift_high, shift_low = halves(sums_two[1])
    turn = me % 4
    mine = jnp.where(turn < 2, jnp.where(turn == 0, gain_high, gain_low), jnp.where(turn == 2, shift_high, shift_low))
    extra[...] = jnp.concatenate(pieces, 0) + to_spare(0.5 * mine, owned + 32, 8)


def whole_kernel(place, raw, weights, turned, gains, shifts, a_two, grad, out, nine, straight, back_one, back_two, sems, a_one, h_one, d_h1, d_act, own_act, sums_two, extra, long, block, total):
    raw_lat, raw_cot = raw.at[:, 0], raw.at[:, 1]
    copies = [
        pltpu.make_async_copy(weights.at[0], straight, sems.at[0]),
        pltpu.make_async_copy(turned.at[1], back_two, sems.at[1]),
        pltpu.make_async_copy(turned.at[0], back_one, sems.at[2]),
    ]
    for copy in copies:
        copy.start()
    ahead_part(raw_lat, gains, shifts, a_one, h_one, a_two, nine, straight, copies[0])
    grad_part(place, a_two, raw_cot, None, out, 0, long, block, total)
    back_part(raw_cot, h_one, gains, shifts, d_h1, sums_two, nine, d_act, back_two, copies[1])
    own_part(place, d_h1, raw_lat, raw_cot, gains, shifts, sums_two, grad, extra, nine, own_act, back_one, copies[2])
    grad_part(place, a_one, d_h1, extra, out, 1, long, block, total)


def sum_kernel(pieces, grad, out, *, clips):
    total = pieces[0].astype(jnp.float32)
    for d in range(1, pieces.shape[0]):
        total = total + pieces[d].astype(jnp.float32)
    total = total / clips
    rows = total.shape[0]
    for p in range(out.shape[0]):
        out[p, 0:rows, :] = total
        out[p, rows:, :] = grad[p]


def adam_kernel(every, moment, second, new_moment, new_second, direction, vector, grad_input):
    parts, tall, chans = every.shape
    owned = moment.shape[1]
    width = chans // parts
    for layer in range(2):
        start = width * (1 - layer)
        grad = every[:, start : start + width, :].reshape(chans, chans).T[:owned, :]
        new_m = 0.9 * moment[layer] + 0.1 * grad
        new_v = 0.999 * second[layer] + 0.001 * grad * grad
        new_moment[layer] = new_m
        new_second[layer] = new_v
        direction[layer] = new_m / bias_first / (jnp.sqrt(new_v / bias_second) + 1e-08)
    for p in range(parts):
        grad_input[p] = every[p, 2 * width :, :].astype(jnp.bfloat16)
    held = [every[p, width : 2 * width, :] for p in range(parts)]
    summed = held[0]
    for p in range(1, parts):
        summed = summed + held[p]
    for row in range(2):
        high = from_spare(summed[16 * row : 16 * row + 8], owned, 32)
        low = from_spare(summed[16 * row + 8 : 16 * row + 16], owned, 32)
        vector[row : row + 1, :] = (high + low)[0:1]
        mine = sum(held[p] for p in range(parts) if p % 4 in (2 * row, 2 * row + 1))
        vector[2 + row : 3 + row, :] = from_spare(mine, owned + 32, 8)[0:1]


def turn_kernel(weights, turned):
    chans = weights.shape[2]
    for tap in range(weights.shape[1] // chans):
        rows = slice(tap * chans, (tap + 1) * chans)
        turned[0, rows, :] = weights[0, rows, :].T


def decode_kernel(place, a_two, weights, latent, decoded, tall, nine, weight, sem):
    copy = pltpu.make_async_copy(weights.at[1], weight, sem)
    copy.start()
    frames, flat, chans = latent.shape
    size = a_two.shape[0] // frames
    rows, every = flat // 8, size // 8
    pitch = nine.shape[0] // (frames + 2)
    depth = 9 * chans
    tall[0] = jnp.zeros(tall.shape[1:], jnp.float32)
    tall[every + 1] = jnp.zeros(tall.shape[1:], jnp.float32)
    rest = jnp.zeros((pitch // 8 - rows, 8, chans), jnp.float32)
    for t in range(frames):
        tall[1 : every + 1] = frame_of(a_two, t, size)
        part = tall[pl.ds(place[0] * rows, rows + 2)]
        for w in range(3):
            moved = col_shifted(part, w - 1)
            for h in range(3):
                view = jnp.concatenate([moved[h : h + rows], rest], 0).reshape(pitch, chans)
                number = 3 * h + w
                nine[(t + 2) * pitch : (t + 3) * pitch, number * chans : (number + 1) * chans] = view.astype(jnp.bfloat16)
    nine[0:pitch, :] = nine[2 * pitch : 3 * pitch, :]
    nine[pitch : 2 * pitch, :] = nine[2 * pitch : 3 * pitch, :]
    copy.wait()
    total = None
    for t in range(3):
        left = nine[t * pitch : (t + frames) * pitch, :]
        part = jnp.dot(left, weight[t * depth : (t + 1) * depth, :], preferred_element_type=jnp.float32)
        total = part if total is None else total + part
    for t in range(frames):
        value = latent[t].astype(jnp.float32) + total[t * pitch : t * pitch + flat, :]
        decoded[t] = value.astype(jnp.bfloat16)


def spread_kernel(latent, upstream, out, sems):
    copies = []
    for p in range(out.shape[0]):
        copies.append(pltpu.make_async_copy(latent, out.at[p, 0], sems.at[p, 0]))
        copies.append(pltpu.make_async_copy(upstream, out.at[p, 1], sems.at[p, 1]))
    for copy in copies:
        copy.start()
    for copy in copies:
        copy.wait()


def pair_kernel(pieces, out):
    for n in range(out.shape[0]):
        out[n] = (pieces[0, n].astype(jnp.float32) + pieces[1, n].astype(jnp.float32)).astype(jnp.bfloat16)


def called(kernel, outs, scratch, args, specs=None, flops=0, limit=16, out_specs=None):
    whole = pl.BlockSpec(memory_space=pltpu.VMEM)
    specs = specs or [whole] * len(args)
    moved = sum(math.prod(a.shape) * a.dtype.itemsize for a in (*args, *outs))
    return pl.pallas_call(
        kernel,
        out_shape=outs,
        in_specs=[whole if spec is None else spec for spec in specs],
        out_specs=out_specs or [whole] * len(outs),
        scratch_shapes=scratch,
        compiler_params=pltpu.CompilerParams(vmem_limit_bytes=limit * 2**20),
        cost_estimate=pl.CostEstimate(flops=flops, bytes_accessed=moved, transcendentals=0),
    )(*args)


def held(weights):
    return [pltpu.VMEM(weights.shape[1:], weights.dtype), pltpu.SemaphoreType.DMA]


def small():
    return pl.BlockSpec(memory_space=pltpu.SMEM)


def away():
    return pl.BlockSpec(memory_space=pl.ANY)


def whole(place, raw, weights, turned, gains, shifts, width, clips, cores):
    blocks, _, frames, flat, chans = raw.shape
    size = blocks * flat
    places = frames * size
    f32, bf16 = jnp.float32, jnp.bfloat16
    outs = [
        jax.ShapeDtypeStruct((places, chans), bf16),
        jax.ShapeDtypeStruct((blocks, flat, chans), f32),
        jax.ShapeDtypeStruct((cores, clips // cores, 2 * width, chans), bf16),
    ]
    layer = pltpu.VMEM(weights.shape[1:], bf16)
    scratch = [
        pltpu.VMEM((places + 2 * size, 9 * chans), bf16),
        layer,
        layer,
        layer,
        pltpu.SemaphoreType.DMA((3,)),
        pltpu.VMEM((places, chans), bf16),
        pltpu.VMEM((places, chans), bf16),
        pltpu.VMEM((places, chans), bf16),
        pltpu.VMEM((places, chans), f32),
        pltpu.VMEM((size, chans), f32),
        pltpu.VMEM((2, 8, chans), f32),
        pltpu.VMEM((32, chans), f32),
        pltpu.VMEM((places + 2 * size, chans), bf16),
        pltpu.VMEM((places, -(-9 * width // 128) * 128), bf16),
        pltpu.VMEM((27 * width, chans), f32),
    ]
    args = (place, raw, weights, turned, gains, shifts)
    specs = [small(), None, away(), away(), None, None]
    return called(whole_kernel, outs, scratch, args, specs, 2 * places * weights.size, 44)


def gathered(pieces, grads, clips):
    parts, flat, chans = grads.shape
    outs = [jax.ShapeDtypeStruct((parts, pieces.shape[1] + flat, chans), jnp.float32)]
    return called(functools.partial(sum_kernel, clips=clips), outs, [], (pieces, grads))[0]


def turn(weights):
    layers, depth, chans = weights.shape
    block = pl.BlockSpec((1, depth // 9, chans), lambda k, n: (k, n, 0))
    return pl.pallas_call(
        turn_kernel,
        grid=(layers, 9),
        out_shape=jax.ShapeDtypeStruct(weights.shape, weights.dtype),
        in_specs=[block],
        out_specs=block,
        cost_estimate=pl.CostEstimate(flops=0, bytes_accessed=4 * weights.size, transcendentals=0),
    )(weights)


def decode(place, a_two, weights, latent):
    frames, flat, chans = latent.shape
    size = a_two.shape[0] // frames
    pitch = -(-flat // 16) * 16
    outs = [jax.ShapeDtypeStruct(latent.shape, jnp.bfloat16)]
    scratch = [
        pltpu.VMEM((size // 8 + 2, 8, chans), jnp.float32),
        pltpu.VMEM(((frames + 2) * pitch, 9 * chans), jnp.bfloat16),
    ] + held(weights)
    args = (place, a_two, weights, latent)
    return called(decode_kernel, outs, scratch, args, [small(), None, away(), None], frames * pitch * weights.size, 44)[0]


def per_device(latents, cotangent, conv_weights, gains, shifts, moment, second):
    frames, rows, cols, chans = latents.shape[1:]
    cores, parts = lax.axis_size("core"), lax.axis_size("space")
    clips = lax.axis_size("pair") * cores
    me = lax.axis_index("space")
    place = me.astype(jnp.int32).reshape(1)
    width = chans // parts
    f32, bf16 = jnp.float32, jnp.bfloat16
    latent = latents[0].reshape(frames, rows * cols, chans)
    upstream = cotangent[0].reshape(latent.shape)
    outs = [jax.ShapeDtypeStruct((parts, 2) + latent.shape, bf16)]
    raw = called(spread_kernel, outs, [pltpu.SemaphoreType.DMA((parts, 2))], (latent, upstream), [away(), away()], limit=58, out_specs=[away()])[0]
    raw = lax.all_to_all(raw, "space", 0, 0)
    raw, turned = lax.optimization_barrier((raw, turn(conv_weights)))

    a_two, grads, pieces = whole(place, raw, conv_weights, turned, gains, shifts, width, clips, cores)
    pieces = lax.all_to_all(pieces, "core", 0, 0)
    pieces = called(pair_kernel, [jax.ShapeDtypeStruct(pieces.shape[1:], bf16)], [], (pieces,))[0]
    pieces = lax.all_to_all(pieces, "pair", 0, 0)
    decoded = decode(place, a_two, conv_weights, latent)

    every = gathered(pieces, grads, clips)
    every = lax.all_to_all(every, "space", 0, 0)
    shape = jax.ShapeDtypeStruct(moment.shape, f32)
    outs = [shape, shape, shape, jax.ShapeDtypeStruct((4, chans), f32)]
    outs.append(jax.ShapeDtypeStruct((frames, rows * cols, chans), bf16))
    outs = called(adam_kernel, outs, [], (every, moment, second))
    new_moment, new_second, direction, vector, grad_input = outs
    grad_input = grad_input.reshape(latents.shape)
    return (decoded.reshape(latents.shape), grad_input, new_moment, new_second, direction, vector)


def solution(mesh):
    clips, parts = mesh.devices.shape
    mesh = Mesh(mesh.devices.reshape(clips // 2, 2, parts), ("pair", "core", "space"))
    dp = ("pair", "core")
    placed = (
        P(dp, None, "space", None, None),
        P(dp, None, "space", None, None),
        P(),
        P(),
        P(),
        P(None, dp, None),
        P(None, dp, None),
    )
    return jax.shard_map(
        per_device,
        mesh=mesh,
        in_specs=placed,
        out_specs=(
            P(dp, None, "space", None, None),
            P(dp, None, "space", None, None),
            P(None, dp, None),
            P(None, dp, None),
            P(None, dp, None),
            P(),
        ),
        check_vma=False,
    )
```
